128 devices in a mesh: hst: 4 (over x), row: 32 (over z, y, core).
Axes of the slice: x: 4, y: 4, z: 4, core: 2. Of those that a mesh axis runs over, the one named last changes fastest.
Arguments:
- tables: bfloat16 [16, 32768, 160], P('hst', 'row'), may hold values from -1.75 to 1.75
- indices: int32 [16384, 16, 8], P(None, 'hst'), may hold values from 0 to 32767
- lengths: int32 [16384, 16], P(None, 'hst'), may hold values from 1 to 8
- feature_order: int32 [16], replicated, may hold values from 0 to 15, each once
- proj_weight: bfloat16 [24, 16], replicated, may hold values from -1.5 to 1.5
- fm_gain: float32 [384], replicated, may hold values from 0.25 to 1.75
- up_weight: bfloat16 [384, 1024], replicated, may hold values from -0.3125 to 0.3125
- down_weight: bfloat16 [1024, 1280], replicated, may hold values from -0.1875 to 0.1875
- compress_weight: bfloat16 [8, 16], replicated, may hold values from -1.5 to 1.5
- out_gain: float32 [16, 160], replicated, may hold values from 0.25 to 1.75
Outputs:
- wukong_out: bfloat16 [16384, 16, 160], P(('hst', 'row'))
The draws below stay inside these ranges and needn't reach their ends.
Inputs may be any that keep to these rules, and one draw needn't show every extreme that they name: `feature_order`: each of 0 to 15 once.
All inputs are finite; a program needn't handle non-finite values.
Results may differ from the reference program's by a relative error of at most 0.017.
Values may be sent and summed in bfloat16 or wider, within the bound.
No kernel may reach another device: no remote copies, remote signals or barrier semaphores. Data moves between devices by JAX's collectives and lax.ppermute only.
A program may use at most 192 MiB of HBM per device.

```python
import math
import jax
import jax.numpy as jnp
import numpy as np
from jax import lax

EMB = 160
ROWS_DEV = 1024
SLOTS = 8
RANK = 24
MLP_W = 1024
FEAT = 16
HALF_FEAT = 8
ROWS = 32768
BATCH = 16384
N_ROW = 32


def set_ends(entries, stream_key, smallest, high):
    place = [jax.random.randint(jax.random.fold_in(stream_key, axis), (), 0, length) for axis, length in enumerate(entries.shape)]
    longest = entries.shape.index(max(entries.shape))
    next_to = place[:longest] + [(place[longest] + 1) % entries.shape[longest]] + place[longest + 1:]
    return entries.at[tuple(place)].set(smallest).at[tuple(next_to)].set(high)


def steps_of(stream_key, extent, pieces, least, high):
    level = 1.0
    for position, parts in pieces:
        draws = jax.random.uniform(jax.random.fold_in(jax.random.fold_in(stream_key, 6), position), (parts,), jnp.float32, least / len(pieces), high / len(pieces))
        level = level * jnp.repeat(jnp.exp(draws), extent[position] // parts).reshape((-1,) + (1,) * (len(extent) - 1 - position))
    return level


def rank_bounds(number_of, skew):
    portions = [(1 << 20) // math.isqrt(standing ** skew) + 1 for standing in range(1, number_of + 1)]
    scale = 1 + sum(portions) // (1 << 30)
    return np.cumsum(np.array([max(1, weight // scale) for weight in portions]))


def skewed_ids(rng, extent, number_of, skew):
    grid = rank_bounds(number_of, skew)
    pick = jax.random.randint(jax.random.fold_in(rng, 1), extent, 0, int(grid[number_of - 1]))
    standing = jnp.searchsorted(jnp.asarray(grid, jnp.int32), pick, side="right")
    return jax.random.permutation(jax.random.fold_in(rng, 2), number_of)[standing].astype(jnp.int32)


def noise(own_key, dims, deviation, most, split=(), held_as=jnp.bfloat16):
    level = steps_of(own_key, dims, split, -0.22, 0.18) if split else 1.0
    entries = jax.random.normal(own_key, dims, jnp.float32) * deviation * level
    return jnp.minimum(jnp.maximum(entries, -most), most).astype(held_as)


def setup_inputs(seed: int = 0) -> dict:
    arg_keys = jax.random.split(jax.random.key(seed), 11)
    tables = noise(arg_keys[0], (FEAT, ROWS, EMB), 0.3, 1.75, ((0, 4), (1, 32)))
    indices = set_ends(skewed_ids(arg_keys[1], (BATCH, FEAT, SLOTS), ROWS, 1), jax.random.fold_in(arg_keys[1], 3), 0, ROWS - 1).astype(jnp.int32)
    lengths = set_ends(jax.random.randint(arg_keys[2], (BATCH, FEAT), 1, SLOTS + 1), jax.random.fold_in(arg_keys[2], 1), 1, SLOTS).astype(jnp.int32)
    feature_order = jax.random.permutation(arg_keys[3], FEAT).astype(jnp.int32)
    proj_weight = noise(arg_keys[4], (RANK, FEAT), FEAT ** -0.5, 1.5)
    fm_gain = jnp.clip(1.0 + 0.15 * jax.random.normal(arg_keys[5], (FEAT * RANK,), jnp.float32), 0.25, 1.75)
    up_weight = noise(arg_keys[6], (FEAT * RANK, MLP_W), (FEAT * RANK) ** -0.5, 0.3125)
    down_weight = noise(arg_keys[7], (MLP_W, HALF_FEAT * EMB), MLP_W ** -0.5, 0.1875)
    compress_weight = noise(arg_keys[8], (HALF_FEAT, FEAT), FEAT ** -0.5, 1.5)
    out_gain = jnp.clip(1.0 + 0.15 * jax.random.normal(arg_keys[9], (FEAT, EMB), jnp.float32), 0.25, 1.75)
    return {"tables": tables, "indices": indices, "lengths": lengths, "feature_order": feature_order, "proj_weight": proj_weight, "fm_gain": fm_gain, "up_weight": up_weight, "down_weight": down_weight, "compress_weight": compress_weight, "out_gain": out_gain}


def layer_norm(values, gain):
    center = values - lax.optimization_barrier(jnp.mean(values, axis=-1, keepdims=True))
    spread = lax.optimization_barrier(jnp.mean(center * center, axis=-1, keepdims=True))
    return center / jnp.sqrt(spread + 1e-05) * gain

def reference(tables, indices, lengths, feature_order, proj_weight, fm_gain, up_weight, down_weight, compress_weight, out_gain):
    slot_ids = jnp.arange(SLOTS).astype(jnp.int32)
    shard_ids = jnp.arange(N_ROW).astype(jnp.int32)

    def pool_one(triple):
        table, rows_used, counts_used = triple
        looked = table[rows_used].astype(jnp.float32)
        usable = (slot_ids[None, :] < counts_used[:, None]).astype(jnp.float32)
        owner = ((rows_used // ROWS_DEV).astype(jnp.int32)[:, :, None] == shard_ids[None, None, :]).astype(jnp.float32)
        owner = owner * usable[:, :, None]
        partial_value = jnp.einsum('bls,ble->bse', owner, looked).astype(jnp.bfloat16)
        return lax.optimization_barrier(jnp.sum(partial_value.astype(jnp.float32), axis=1)).astype(jnp.bfloat16)
    pooled = lax.map(pool_one, (tables, jnp.swapaxes(indices, 0, 1), jnp.swapaxes(lengths, 0, 1)))
    pooled = jnp.swapaxes(pooled, 0, 1)
    embedded = jnp.zeros_like(pooled).at[:, feature_order, :].set(pooled)
    batch_rows = embedded.shape[0]
    wide = embedded.astype(jnp.float32)
    projected = jnp.einsum('kf,bfe->bke', proj_weight.astype(jnp.float32), wide).astype(jnp.bfloat16)
    interaction = jnp.einsum('bfe,bke->bfk', wide, projected.astype(jnp.float32))
    normed = layer_norm(interaction.reshape(batch_rows, FEAT * RANK), fm_gain).astype(jnp.bfloat16)
    hidden = jnp.maximum(jnp.dot(normed, up_weight, preferred_element_type=jnp.float32), 0.0).astype(jnp.bfloat16)
    fm_block = jnp.dot(hidden, down_weight, preferred_element_type=jnp.float32).reshape(batch_rows, HALF_FEAT, EMB)
    compressed = jnp.einsum('mf,bfe->bme', compress_weight.astype(jnp.float32), wide)
    summed = jnp.concatenate([fm_block, compressed], axis=1) + wide
    result = layer_norm(summed.reshape(batch_rows, FEAT * EMB), out_gain.reshape(FEAT * EMB))
    return result.reshape(batch_rows, FEAT, EMB).astype(jnp.bfloat16)
```

```python
import functools

import jax
import jax.numpy as jnp
from jax import lax
from jax.experimental import pallas as pl
from jax.experimental.pallas import tpu as pltpu
from jax.sharding import PartitionSpec as P

LANES = 128
ROWS_DEV = 1024
SUB = 256
GATHER = 8
BLOCKS = GATHER * ROWS_DEV // SUB
BAG_BLOCKS = 16
STEPS = BAG_BLOCKS // 2


def prep_kernel(pos_ref, idx_ref, len_ref, keys_ref, lid_ref, mask_ref):
    host, z, y, core = pos_ref[0], pos_ref[1], pos_ref[2], pos_ref[3]
    table = pl.program_id(0)
    over_z = table % 2 == 0
    slot = lax.broadcasted_iota(jnp.int32, (8, LANES), 0)
    pick = lax.broadcasted_iota(jnp.int32, (len_ref.shape[0], LANES), 0)
    for n in range(BAG_BLOCKS):
        dest, hrel = n // 4, n % 4
        owner_host = (host + hrel) & 3
        row_dev = jnp.where(
            over_z,
            z * 8 + ((y + dest) & 3) * 2 + core,
            ((z + dest) & 3) * 8 + y * 2 + core,
        )
        start = pl.multiple_of((owner_host * 32 + row_dev) * LANES, LANES)
        v = idx_ref[0, :, pl.ds(start, LANES)]
        used = jnp.sum(
            jnp.where(pick == table, len_ref[:, pl.ds(start, LANES)], 0), axis=0, keepdims=True
        )
        at_z, at_y, at_core = v >> 13, (v >> 11) & 3, (v >> 10) & 1
        here = jnp.where(over_z, at_y - y, at_z - z) == 0
        shard = jnp.where(over_z, (at_z - z) & 3, (at_y - y) & 3) * 2 + (at_core ^ core)
        local = shard * ROWS_DEV + (v & (ROWS_DEV - 1))
        local = jnp.where(here & (slot < used), local, -1)
        for s in range(8):
            lid_ref[0, s, n : n + 1, :] = local[s : s + 1, :]
    for g in range(BAG_BLOCKS // 8):
        rows = pl.ds(g * 8, 8)
        lids = [lid_ref[0, s, rows, :] for s in range(8)]
        high = [x >> 8 for x in lids]
        low = [(x & (SUB - 1)).astype(jnp.float32) for x in lids]

        def one_block(blk, mask):
            at = [h == blk for h in high]
            up = [jnp.where(a, l, 511.0) for a, l in zip(at, low)]
            down = [jnp.where(a, l, -1.0) for a, l in zip(at, low)]
            first = functools.reduce(jnp.minimum, up)
            last = functools.reduce(jnp.maximum, down)
            n_first = sum(jnp.where(u == first, 1.0, 0.0) for u in up)
            n_last = sum(jnp.where(d == last, 1.0, 0.0) for d in down)
            total = sum(jnp.where(a, 1.0, 0.0) for a in at)
            more = (n_first + n_last) < total
            keys_ref[0, blk, 0, rows, :] = first
            keys_ref[0, blk, 1, rows, :] = n_first
            keys_ref[0, blk, 2, rows, :] = jnp.where(last == first, -1.0, last)
            keys_ref[0, blk, 3, rows, :] = n_last
            return mask | jnp.where(more, jnp.int32(1) << blk, 0)

        mask_ref[0, rows, :] = lax.fori_loop(
            0, BLOCKS, one_block, jnp.zeros((8, LANES), jnp.int32)
        )


def prep(pos, idx, lens):
    tables = idx.shape[0]
    return pl.pallas_call(
        prep_kernel,
        grid=(tables,),
        in_specs=[
            pl.BlockSpec(memory_space=pltpu.SMEM),
            pl.BlockSpec((1,) + idx.shape[1:], lambda j: (j, 0, 0)),
            pl.BlockSpec(lens.shape, lambda j: (0, 0)),
        ],
        out_specs=[
            pl.BlockSpec((1, BLOCKS, 4, BAG_BLOCKS, LANES), lambda j: (j, 0, 0, 0, 0)),
            pl.BlockSpec((1, 8, BAG_BLOCKS, LANES), lambda j: (j, 0, 0, 0)),
            pl.BlockSpec((1, BAG_BLOCKS, LANES), lambda j: (j, 0, 0)),
        ],
        out_shape=[
            jax.ShapeDtypeStruct((tables, BLOCKS, 4, BAG_BLOCKS, LANES), jnp.float32),
            jax.ShapeDtypeStruct((tables, 8, BAG_BLOCKS, LANES), jnp.int32),
            jax.ShapeDtypeStruct((tables, BAG_BLOCKS, LANES), jnp.int32),
        ],
        compiler_params=pltpu.CompilerParams(vmem_limit_bytes=32 << 20),
        cost_estimate=pl.CostEstimate(
            flops=40_000_000, bytes_accessed=9_000_000, transcendentals=0
        ),
        name="prep",
    )(pos, idx, lens)


def pool_kernel(mask_ref, keys_ref, lid_ref, *rest):
    tabs = rest[:GATHER]
    outs = rest[GATHER : GATHER + 4]
    acc, counts, extra = rest[GATHER + 4 :]
    step = pl.program_id(0)
    row_ids = [
        (lax.broadcasted_iota(jnp.int32, (16, LANES), 0) + c * 16)
        .astype(jnp.float32)
        .astype(jnp.bfloat16)
        for c in range(SUB // 16)
    ]

    def wide(x):
        return jnp.broadcast_to(x, (16, LANES)).astype(jnp.bfloat16)

    for blk in range(BLOCKS):
        for half in range(2):
            row = pl.ds(2 * step + half, 1)
            k1, m1, k2, m2 = (wide(keys_ref[0, blk, v, row, :]) for v in range(4))
            for c in range(SUB // 16):
                counts[
                    blk * SUB + c * 16 : blk * SUB + (c + 1) * 16,
                    half * LANES : (half + 1) * LANES,
                ] = jnp.where(
                    k1 == row_ids[c], m1, jnp.where(k2 == row_ids[c], m2, jnp.bfloat16(0))
                )
    total = None
    for g in range(GATHER):
        part = jnp.dot(
            tabs[g][...],
            counts[g * ROWS_DEV : (g + 1) * ROWS_DEV, :],
            preferred_element_type=jnp.float32,
        )
        total = part if total is None else total + part
    acc[...] = total

    mask = mask_ref[2 * step] | mask_ref[2 * step + 1]

    @pl.when(mask != 0)
    def _():
        def fix(blk, carry):
            @pl.when(((mask >> blk) & 1) == 1)
            def _():
                for half in range(2):
                    row = pl.ds(2 * step + half, 1)
                    k1 = keys_ref[0, blk, 0, row, :]
                    k2 = keys_ref[0, blk, 2, row, :]
                    left = []
                    for s in range(8):
                        x = lid_ref[0, s, row, :]
                        low = jnp.where(
                            (x >> 8) == blk, (x & (SUB - 1)).astype(jnp.float32), -1.0
                        )
                        left.append(wide(jnp.where((low == k1) | (low == k2), -1.0, low)))
                    for c in range(SUB // 16):
                        n = jnp.zeros((16, LANES), jnp.bfloat16)
                        for k in left:
                            n = n + jnp.where(k == row_ids[c], jnp.bfloat16(1), jnp.bfloat16(0))
                        extra[c * 16 : (c + 1) * 16, half * LANES : (half + 1) * LANES] = n
                columns = pl.ds(pl.multiple_of((blk & 3) * SUB, SUB), SUB)
                for g in range(GATHER):

                    @pl.when((blk >> 2) == g)
                    def _(g=g):
                        acc[...] += jnp.dot(
                            tabs[g][:, columns], extra[...], preferred_element_type=jnp.float32
                        )

            return carry

        lax.fori_loop(0, BLOCKS, fix, 0)

    result = acc[...].astype(jnp.bfloat16)
    place = (step % 2) * 2
    for d in range(4):

        @pl.when(step // 2 == d)
        def _(d=d):
            outs[d][pl.ds(place, 1), :, :] = result[None, :, :LANES]
            outs[d][pl.ds(place + 1, 1), :, :] = result[None, :, LANES:]


def pool(table, mask, keys, lids, shards):
    emb, rows = shards[0].shape
    return pl.pallas_call(
        pool_kernel,
        grid=(STEPS,),
        in_specs=[
            pl.BlockSpec(memory_space=pltpu.SMEM),
            pl.BlockSpec((1,) + keys.shape[1:], lambda i: (table, 0, 0, 0, 0)),
            pl.BlockSpec((1,) + lids.shape[1:], lambda i: (table, 0, 0, 0)),
        ]
        + [pl.BlockSpec((emb, rows), lambda i: (0, 0))] * GATHER,
        out_specs=[pl.BlockSpec((4, emb, LANES), lambda i: (0, 0, 0))] * 4,
        out_shape=[jax.ShapeDtypeStruct((4, emb, LANES), jnp.bfloat16)] * 4,
        scratch_shapes=[
            pltpu.VMEM((emb, 2 * LANES), jnp.float32),
            pltpu.VMEM((GATHER * rows, 2 * LANES), jnp.bfloat16),
            pltpu.VMEM((SUB, 2 * LANES), jnp.bfloat16),
        ],
        compiler_params=pltpu.CompilerParams(vmem_limit_bytes=32 << 20),
        cost_estimate=pl.CostEstimate(
            flops=2 * GATHER * rows * 2048 * 256, bytes_accessed=5_000_000, transcendentals=0
        ),
        name="pool",
    )(mask, keys, lids, *shards)


def tail_kernel(
    host_ref,
    order_ref,
    proj_ref,
    compress_ref,
    *rest,
):
    parts = rest[:4]
    fm_gain_ref, up_ref, down_ref, gain_ref, out_ref, emb, gram, summed = rest[4:]
    host = host_ref[0]
    for d in range(4):
        source = (host - d) & 3
        for j in range(4):
            at = order_ref[source * 4 + j]
            emb[pl.ds(at, 1), :, :] = parts[d][j : j + 1, :, :].astype(jnp.float32)
    feats, width, lanes = emb.shape
    rank = proj_ref.shape[0]

    for f in range(feats):
        x = emb[f]
        for g in range(f + 1):
            dot = jnp.sum(x * emb[g], axis=0, keepdims=True)
            gram[f, g : g + 1, :] = dot
            if g != f:
                gram[g, f : f + 1, :] = dot
    rows = []
    for k in range(rank):
        row = None
        for g in range(feats):
            term = proj_ref[k, g] * gram[g]
            row = term if row is None else row + term
        rows.append(row)
    inv = 1.0 / (rank * feats)
    mean = jnp.sum(sum(rows), axis=0, keepdims=True) * inv
    rows = [r - mean for r in rows]
    spread = jnp.sum(sum(r * r for r in rows), axis=0, keepdims=True) * inv
    scale = 1.0 / jnp.sqrt(spread + 1e-05)
    normed = jnp.concatenate(
        [rows[k] * scale * fm_gain_ref[:, k : k + 1] for k in range(rank)], axis=0
    ).astype(jnp.bfloat16)
    hidden = jnp.maximum(
        jnp.dot(up_ref[...], normed, preferred_element_type=jnp.float32), 0.0
    ).astype(jnp.bfloat16)
    half = feats // 2
    for m in range(half):
        block = jnp.dot(
            down_ref[m * width : (m + 1) * width, :], hidden, preferred_element_type=jnp.float32
        )
        summed[m] = block + emb[m]
        acc = emb[half + m]
        for f in range(feats):
            acc = acc + compress_ref[m, f] * emb[f]
        summed[half + m] = acc
    inv = 1.0 / (feats * width)
    total = summed[0]
    for f in range(1, feats):
        total = total + summed[f]
    mean = jnp.sum(total, axis=0, keepdims=True) * inv
    square = None
    for f in range(feats):
        c = summed[f] - mean
        square = c * c if square is None else square + c * c
    spread = jnp.sum(square, axis=0, keepdims=True) * inv
    scale = 1.0 / jnp.sqrt(spread + 1e-05)
    for f in range(feats):
        out_ref[f] = ((summed[f] - mean) * scale * gain_ref[:, f : f + 1]).astype(jnp.bfloat16)


def tail(host, order, proj, compress, parts, fm_gain, up, down, gain):
    feats, width = order.shape[0], parts[0].shape[1]
    smem = pl.BlockSpec(memory_space=pltpu.SMEM)
    vmem = pl.BlockSpec(memory_space=pltpu.VMEM)
    return pl.pallas_call(
        tail_kernel,
        in_specs=[smem] * 4 + [vmem] * 8,
        out_specs=vmem,
        out_shape=jax.ShapeDtypeStruct((feats, width, LANES), jnp.bfloat16),
        scratch_shapes=[
            pltpu.VMEM((feats, width, LANES), jnp.float32),
            pltpu.VMEM((feats, feats, LANES), jnp.float32),
            pltpu.VMEM((feats, width, LANES), jnp.float32),
        ],
        compiler_params=pltpu.CompilerParams(vmem_limit_bytes=32 << 20),
        cost_estimate=pl.CostEstimate(
            flops=1_000_000_000, bytes_accessed=8_000_000, transcendentals=0
        ),
        name="tail",
    )(host, order, proj, compress, *parts, fm_gain, up, down, gain)


def row_moves(axis, step):
    pairs = []
    for z in range(4):
        for y in range(4):
            for core in range(2):
                to = {
                    "z": (((z + step) % 4) * 8 + y * 2 + core),
                    "y": (z * 8 + ((y + step) % 4) * 2 + core),
                    "core": (z * 8 + y * 2 + (core + step) % 2),
                }[axis]
                pairs.append((z * 8 + y * 2 + core, to))
    return pairs


def gather_shards(shard, axis):
    near = [shard]
    for rel in range(1, 4):
        near.append(lax.ppermute(shard, "row", row_moves(axis, 4 - rel)))
    far = [lax.ppermute(x, "row", row_moves("core", 1)) for x in near]
    return [x for pair in zip(near, far) for x in pair]


def exchange(blocks, axis):
    total = blocks[0].astype(jnp.float32)
    for d in range(1, 4):
        total = total + lax.ppermute(blocks[d], "row", row_moves(axis, d)).astype(jnp.float32)
    return total.astype(jnp.bfloat16)


def on_device(
    tables,
    indices,
    lengths,
    feature_order,
    proj_weight,
    fm_gain,
    up_weight,
    down_weight,
    compress_weight,
    out_gain,
):
    host = lax.axis_index("hst")
    row = lax.axis_index("row")
    pos = jnp.stack([host, row // 8, (row // 2) % 4, row % 2]).astype(jnp.int32)
    n_tables = tables.shape[0]
    feats, emb = out_gain.shape
    rank = proj_weight.shape[0]
    width = up_weight.shape[1]

    flipped = jnp.swapaxes(tables, 1, 2)
    shards = [
        gather_shards(flipped[j], "z" if j % 2 == 0 else "y") for j in range(n_tables)
    ]
    keys, lids, masks = prep(pos, jnp.transpose(indices, (1, 2, 0)), lengths.T)
    masks = lax.reduce(masks, jnp.int32(0), lax.bitwise_or, (2,))
    sums = []
    for j in range(n_tables):
        blocks = pool(j, masks[j], keys, lids, shards[j])
        sums.append(exchange(blocks, "y" if j % 2 == 0 else "z"))

    parts = []
    for d in range(4):
        block = jnp.stack([s[d] for s in sums])
        if d:
            block = lax.ppermute(block, "hst", [(h, (h + d) % 4) for h in range(4)])
        parts.append(block)
    up = jnp.transpose(up_weight.reshape(feats, rank, width), (2, 1, 0)).reshape(
        width, rank * feats
    )
    result = tail(
        pos[:1],
        feature_order,
        proj_weight.astype(jnp.float32),
        compress_weight.astype(jnp.float32),
        parts,
        fm_gain.reshape(feats, rank),
        up,
        down_weight.T,
        out_gain.T,
    )
    return jnp.transpose(result, (2, 0, 1))


def solution(mesh):
    in_specs = (
        P("hst", "row", None),
        P(None, "hst", None),
        P(None, "hst"),
        P(),
        P(),
        P(),
        P(),
        P(),
        P(),
        P(),
    )
    out_specs = P(("hst", "row"), None, None)
    return jax.shard_map(
        on_device, mesh=mesh, in_specs=in_specs, out_specs=out_specs, check_vma=False
    )
```

```python
import functools

import jax
import jax.numpy as jnp
from jax import lax
from jax.experimental import pallas as pl
from jax.experimental.pallas import tpu as pltpu
from jax.sharding import PartitionSpec as P

LANES = 128
ROWS_DEV = 1024
SUB = 256
GATHER = 8
BLOCKS = GATHER * ROWS_DEV // SUB
BAG_BLOCKS = 16
STEPS = BAG_BLOCKS // 2


def prep_kernel(pos_ref, idx_ref, len_ref, keys_ref, lid_ref, mask_ref):
    host, z, y, core = pos_ref[0], pos_ref[1], pos_ref[2], pos_ref[3]
    table = pl.program_id(0)
    over_z = table % 2 == 0
    slot = lax.broadcasted_iota(jnp.int32, (8, LANES), 0)
    pick = lax.broadcasted_iota(jnp.int32, (len_ref.shape[0], LANES), 0)
    for n in range(BAG_BLOCKS):
        dest, hrel = n // 4, n % 4
        owner_host = (host + hrel) & 3
        row_dev = jnp.where(
            over_z,
            z * 8 + ((y + dest) & 3) * 2 + core,
            ((z + dest) & 3) * 8 + y * 2 + core,
        )
        start = pl.multiple_of((owner_host * 32 + row_dev) * LANES, LANES)
        v = idx_ref[0, :, pl.ds(start, LANES)]
        used = jnp.sum(
            jnp.where(pick == table, len_ref[:, pl.ds(start, LANES)], 0), axis=0, keepdims=True
        )
        at_z, at_y, at_core = v >> 13, (v >> 11) & 3, (v >> 10) & 1
        here = jnp.where(over_z, at_y - y, at_z - z) == 0
        shard = jnp.where(over_z, (at_z - z) & 3, (at_y - y) & 3) * 2 + (at_core ^ core)
        local = shard * ROWS_DEV + (v & (ROWS_DEV - 1))
        local = jnp.where(here & (slot < used), local, -1)
        for s in range(8):
            lid_ref[0, s, n : n + 1, :] = local[s : s + 1, :]
    for g in range(BAG_BLOCKS // 8):
        rows = pl.ds(g * 8, 8)
        lids = [lid_ref[0, s, rows, :] for s in range(8)]
        high = [x >> 8 for x in lids]
        low = [(x & (SUB - 1)).astype(jnp.float32) for x in lids]

        def one_block(blk, mask):
            at = [h == blk for h in high]
            up = [jnp.where(a, l, 511.0) for a, l in zip(at, low)]
            down = [jnp.where(a, l, -1.0) for a, l in zip(at, low)]
            first = functools.reduce(jnp.minimum, up)
            last = functools.reduce(jnp.maximum, down)
            n_first = sum(jnp.where(u == first, 1.0, 0.0) for u in up)
            n_last = sum(jnp.where(d == last, 1.0, 0.0) for d in down)
            total = sum(jnp.where(a, 1.0, 0.0) for a in at)
            more = (n_first + n_last) < total
            keys_ref[0, blk, 0, rows, :] = first
            keys_ref[0, blk, 1, rows, :] = n_first
            keys_ref[0, blk, 2, rows, :] = jnp.where(last == first, -1.0, last)
            keys_ref[0, blk, 3, rows, :] = n_last
            return mask | jnp.where(more, jnp.int32(1) << blk, 0)

        mask_ref[0, rows, :] = lax.fori_loop(
            0, BLOCKS, one_block, jnp.zeros((8, LANES), jnp.int32)
        )


def prep(pos, idx, lens):
    tables = idx.shape[0]
    return pl.pallas_call(
        prep_kernel,
        grid=(tables,),
        in_specs=[
            pl.BlockSpec(memory_space=pltpu.SMEM),
            pl.BlockSpec((1,) + idx.shape[1:], lambda j: (j, 0, 0)),
            pl.BlockSpec(lens.shape, lambda j: (0, 0)),
        ],
        out_specs=[
            pl.BlockSpec((1, BLOCKS, 4, BAG_BLOCKS, LANES), lambda j: (j, 0, 0, 0, 0)),
            pl.BlockSpec((1, 8, BAG_BLOCKS, LANES), lambda j: (j, 0, 0, 0)),
            pl.BlockSpec((1, BAG_BLOCKS, LANES), lambda j: (j, 0, 0)),
        ],
        out_shape=[
            jax.ShapeDtypeStruct((tables, BLOCKS, 4, BAG_BLOCKS, LANES), jnp.float32),
            jax.ShapeDtypeStruct((tables, 8, BAG_BLOCKS, LANES), jnp.int32),
            jax.ShapeDtypeStruct((tables, BAG_BLOCKS, LANES), jnp.int32),
        ],
        compiler_params=pltpu.CompilerParams(vmem_limit_bytes=32 << 20),
        cost_estimate=pl.CostEstimate(
            flops=40_000_000, bytes_accessed=9_000_000, transcendentals=0
        ),
        name="prep",
    )(pos, idx, lens)


def pool_kernel(mask_ref, keys_ref, lid_ref, *rest):
    tabs = rest[:GATHER]
    outs = rest[GATHER : GATHER + 4]
    acc, counts, extra = rest[GATHER + 4 :]
    step = pl.program_id(0)
    row_ids = [
        (lax.broadcasted_iota(jnp.int32, (16, 2 * LANES), 0) + c * 16)
        .astype(jnp.float32)
        .astype(jnp.bfloat16)
        for c in range(SUB // 16)
    ]

    def wide(x):
        return jnp.broadcast_to(x, (16, LANES)).astype(jnp.bfloat16)

    for blk in range(BLOCKS):
        k1, m1, k2, m2 = (
            jnp.concatenate(
                [wide(keys_ref[0, blk, v, pl.ds(2 * step + half, 1), :]) for half in range(2)],
                axis=1,
            )
            for v in range(4)
        )
        for c in range(SUB // 16):
            counts[blk * SUB + c * 16 : blk * SUB + (c + 1) * 16, :] = jnp.where(
                k1 == row_ids[c], m1, jnp.where(k2 == row_ids[c], m2, jnp.bfloat16(0))
            )
    total = None
    for g in range(GATHER):
        part = jnp.dot(
            tabs[g][...],
            counts[g * ROWS_DEV : (g + 1) * ROWS_DEV, :],
            preferred_element_type=jnp.float32,
        )
        total = part if total is None else total + part
    acc[...] = total

    mask = mask_ref[2 * step] | mask_ref[2 * step + 1]

    @pl.when(mask != 0)
    def _():
        def fix(blk, carry):
            @pl.when(((mask >> blk) & 1) == 1)
            def _():
                for half in range(2):
                    row = pl.ds(2 * step + half, 1)
                    k1 = keys_ref[0, blk, 0, row, :]
                    k2 = keys_ref[0, blk, 2, row, :]
                    left = []
                    for s in range(8):
                        x = lid_ref[0, s, row, :]
                        low = jnp.where(
                            (x >> 8) == blk, (x & (SUB - 1)).astype(jnp.float32), -1.0
                        )
                        left.append(wide(jnp.where((low == k1) | (low == k2), -1.0, low)))
                    for c in range(SUB // 16):
                        n = jnp.zeros((16, LANES), jnp.bfloat16)
                        for k in left:
                            n = n + jnp.where(k == row_ids[c][:, :LANES], jnp.bfloat16(1), jnp.bfloat16(0))
                        extra[c * 16 : (c + 1) * 16, half * LANES : (half + 1) * LANES] = n
                columns = pl.ds(pl.multiple_of((blk & 3) * SUB, SUB), SUB)
                for g in range(GATHER):

                    @pl.when((blk >> 2) == g)
                    def _(g=g):
                        acc[...] += jnp.dot(
                            tabs[g][:, columns], extra[...], preferred_element_type=jnp.float32
                        )

            return carry

        lax.fori_loop(0, BLOCKS, fix, 0)

    result = acc[...].astype(jnp.bfloat16)
    place = (step % 2) * 2
    for d in range(4):

        @pl.when(step // 2 == d)
        def _(d=d):
            outs[d][pl.ds(place, 1), :, :] = result[None, :, :LANES]
            outs[d][pl.ds(place + 1, 1), :, :] = result[None, :, LANES:]


def pool(table, mask, keys, lids, shards):
    emb, rows = shards[0].shape
    return pl.pallas_call(
        pool_kernel,
        grid=(STEPS,),
        in_specs=[
            pl.BlockSpec(memory_space=pltpu.SMEM),
            pl.BlockSpec((1,) + keys.shape[1:], lambda i: (table, 0, 0, 0, 0)),
            pl.BlockSpec((1,) + lids.shape[1:], lambda i: (table, 0, 0, 0)),
        ]
        + [pl.BlockSpec((emb, rows), lambda i: (0, 0))] * GATHER,
        out_specs=[pl.BlockSpec((4, emb, LANES), lambda i: (0, 0, 0))] * 4,
        out_shape=[jax.ShapeDtypeStruct((4, emb, LANES), jnp.bfloat16)] * 4,
        scratch_shapes=[
            pltpu.VMEM((emb, 2 * LANES), jnp.float32),
            pltpu.VMEM((GATHER * rows, 2 * LANES), jnp.bfloat16),
            pltpu.VMEM((SUB, 2 * LANES), jnp.bfloat16),
        ],
        compiler_params=pltpu.CompilerParams(vmem_limit_bytes=32 << 20),
        cost_estimate=pl.CostEstimate(
            flops=2 * GATHER * rows * 2048 * 256, bytes_accessed=5_000_000, transcendentals=0
        ),
        name="pool",
    )(mask, keys, lids, *shards)


def tail_kernel(
    host_ref,
    order_ref,
    proj_ref,
    compress_ref,
    *rest,
):
    parts = rest[:8]
    fm_gain_ref, up_ref, down_ref, gain_ref, out_ref, emb, gram, summed = rest[8:]
    host = host_ref[0]
    for d in range(4):
        source = (host - d) & 3
        for j in range(4):
            at = order_ref[source * 4 + j]
            part, k = (parts[d], j) if j < 3 else (parts[4 + d], 0)
            emb[pl.ds(at, 1), :, :] = part[k : k + 1, :, :].astype(jnp.float32)
    feats, width, lanes = emb.shape
    rank = proj_ref.shape[0]

    for f in range(feats):
        x = emb[f]
        for g in range(f + 1):
            dot = jnp.sum(x * emb[g], axis=0, keepdims=True)
            gram[f, g : g + 1, :] = dot
            if g != f:
                gram[g, f : f + 1, :] = dot
    rows = []
    for k in range(rank):
        row = None
        for g in range(feats):
            term = proj_ref[k, g] * gram[g]
            row = term if row is None else row + term
        rows.append(row)
    inv = 1.0 / (rank * feats)
    mean = jnp.sum(sum(rows), axis=0, keepdims=True) * inv
    rows = [r - mean for r in rows]
    spread = jnp.sum(sum(r * r for r in rows), axis=0, keepdims=True) * inv
    scale = 1.0 / jnp.sqrt(spread + 1e-05)
    normed = jnp.concatenate(
        [rows[k] * scale * fm_gain_ref[:, k : k + 1] for k in range(rank)], axis=0
    ).astype(jnp.bfloat16)
    hidden = jnp.maximum(
        jnp.dot(up_ref[...], normed, preferred_element_type=jnp.float32), 0.0
    ).astype(jnp.bfloat16)
    half = feats // 2
    for m in range(half):
        block = jnp.dot(
            down_ref[m * width : (m + 1) * width, :], hidden, preferred_element_type=jnp.float32
        )
        summed[m] = block + emb[m]
        acc = emb[half + m]
        for f in range(feats):
            acc = acc + compress_ref[m, f] * emb[f]
        summed[half + m] = acc
    inv = 1.0 / (feats * width)
    total = summed[0]
    for f in range(1, feats):
        total = total + summed[f]
    mean = jnp.sum(total, axis=0, keepdims=True) * inv
    square = None
    for f in range(feats):
        c = summed[f] - mean
        square = c * c if square is None else square + c * c
    spread = jnp.sum(square, axis=0, keepdims=True) * inv
    scale = 1.0 / jnp.sqrt(spread + 1e-05)
    for f in range(feats):
        out_ref[f] = ((summed[f] - mean) * scale * gain_ref[:, f : f + 1]).astype(jnp.bfloat16)


def tail(host, order, proj, compress, parts, fm_gain, up, down, gain):
    feats, width = order.shape[0], parts[0].shape[1]
    smem = pl.BlockSpec(memory_space=pltpu.SMEM)
    vmem = pl.BlockSpec(memory_space=pltpu.VMEM)
    return pl.pallas_call(
        tail_kernel,
        in_specs=[smem] * 4 + [vmem] * 12,
        out_specs=vmem,
        out_shape=jax.ShapeDtypeStruct((feats, width, LANES), jnp.bfloat16),
        scratch_shapes=[
            pltpu.VMEM((feats, width, LANES), jnp.float32),
            pltpu.VMEM((feats, feats, LANES), jnp.float32),
            pltpu.VMEM((feats, width, LANES), jnp.float32),
        ],
        compiler_params=pltpu.CompilerParams(vmem_limit_bytes=32 << 20),
        cost_estimate=pl.CostEstimate(
            flops=1_000_000_000, bytes_accessed=8_000_000, transcendentals=0
        ),
        name="tail",
    )(host, order, proj, compress, *parts, fm_gain, up, down, gain)


def row_moves(axis, step):
    pairs = []
    for z in range(4):
        for y in range(4):
            for core in range(2):
                to = {
                    "z": (((z + step) % 4) * 8 + y * 2 + core),
                    "y": (z * 8 + ((y + step) % 4) * 2 + core),
                    "core": (z * 8 + y * 2 + (core + step) % 2),
                }[axis]
                pairs.append((z * 8 + y * 2 + core, to))
    return pairs


def near_shards(shard, axis):
    return [
        lax.ppermute(shard, "row", row_moves(axis, 4 - rel)) for rel in range(1, 4)
    ]


def other_core(x):
    return lax.ppermute(x, "row", row_moves("core", 1))


def exchange(blocks, axis):
    total = blocks[0].astype(jnp.float32)
    for d in range(1, 4):
        total = total + lax.ppermute(blocks[d], "row", row_moves(axis, d)).astype(jnp.float32)
    return total.astype(jnp.bfloat16)


def on_device(
    tables,
    indices,
    lengths,
    feature_order,
    proj_weight,
    fm_gain,
    up_weight,
    down_weight,
    compress_weight,
    out_gain,
):
    host = lax.axis_index("hst")
    row = lax.axis_index("row")
    pos = jnp.stack([host, row // 8, (row // 2) % 4, row % 2]).astype(jnp.int32)
    n_tables = tables.shape[0]
    feats, emb = out_gain.shape
    rank = proj_weight.shape[0]
    width = up_weight.shape[1]

    flipped = jnp.swapaxes(tables, 1, 2)
    axes = ["z" if j % 2 == 0 else "y" for j in range(n_tables)]
    own = [flipped[j] for j in range(n_tables)]
    own_far = [other_core(x) for x in own]
    near = [near_shards(own[j], axes[j]) for j in range(2)]
    keys, lids, masks = prep(pos, jnp.transpose(indices, (1, 2, 0)), lengths.T)
    masks = lax.reduce(masks, jnp.int32(0), lax.bitwise_or, (2,))
    up = jnp.transpose(up_weight.reshape(feats, rank, width), (2, 1, 0)).reshape(
        width, rank * feats
    )
    down = down_weight.T
    near, masks, up, down, own = lax.optimization_barrier((near, masks, up, down, own))
    far = [[other_core(x) for x in near[j]] for j in range(2)]
    near += [near_shards(own[j], axes[j]) for j in range(2, n_tables)]
    sums = []
    masks = [masks[j] for j in range(n_tables)]
    for j in range(n_tables):
        shards = [own[j], own_far[j]] + [x for pair in zip(near[j], far[j]) for x in pair]
        blocks = pool(j, masks[j], keys, lids, shards)
        if j + 2 < n_tables:
            near[j + 2], masks[j + 1 :], blocks = lax.optimization_barrier(
                (near[j + 2], masks[j + 1 :], blocks)
            )
            far.append([other_core(x) for x in near[j + 2]])
        elif j + 1 < n_tables:
            masks[j + 1], blocks = lax.optimization_barrier((masks[j + 1], blocks))
        sums.append(exchange(blocks, "y" if j % 2 == 0 else "z"))

    parts = []
    for group in (sums[:3], sums[3:]):
        for d in range(4):
            block = jnp.stack([x[d] for x in group])
            if d:
                block = lax.ppermute(block, "hst", [(h, (h + d) % 4) for h in range(4)])
            parts.append(block)
    result = tail(
        pos[:1],
        feature_order,
        proj_weight.astype(jnp.float32),
        compress_weight.astype(jnp.float32),
        parts,
        fm_gain.reshape(feats, rank),
        up,
        down,
        out_gain.T,
    )
    return jnp.transpose(result, (2, 0, 1))


def solution(mesh):
    in_specs = (
        P("hst", "row", None),
        P(None, "hst", None),
        P(None, "hst"),
        P(),
        P(),
        P(),
        P(),
        P(),
        P(),
        P(),
    )
    out_specs = P(("hst", "row"), None, None)
    return jax.shard_map(
        on_device, mesh=mesh, in_specs=in_specs, out_specs=out_specs, check_vma=False
    )
```

```python
import functools

import jax
import jax.numpy as jnp
from jax import lax
from jax.experimental import pallas as pl
from jax.experimental.pallas import tpu as pltpu
from jax.sharding import PartitionSpec as P

LANES = 128
ROWS_DEV = 1024
SUB = 256
GATHER = 8
BLOCKS = GATHER * ROWS_DEV // SUB
BAG_BLOCKS = 16
PAIR = 2 * LANES


def prep_kernel(pos_ref, idx_ref, len_ref, keys_ref, lid_ref, mask_ref):
    host, z, y, core = pos_ref[0], pos_ref[1], pos_ref[2], pos_ref[3]
    table = pl.program_id(0)
    over_z = table < 2
    slot = lax.broadcasted_iota(jnp.int32, (8, LANES), 0)
    pick = lax.broadcasted_iota(jnp.int32, (len_ref.shape[0], LANES), 0)
    for n in range(BAG_BLOCKS):
        dest, hrel = n // 4, n % 4
        owner_host = (host + hrel) & 3
        row_dev = jnp.where(
            over_z,
            z * 8 + ((y + dest) & 3) * 2 + core,
            ((z + dest) & 3) * 8 + y * 2 + core,
        )
        start = pl.multiple_of((owner_host * 32 + row_dev) * LANES, LANES)
        v = idx_ref[0, :, pl.ds(start, LANES)]
        used = jnp.sum(
            jnp.where(pick == table, len_ref[:, pl.ds(start, LANES)], 0), axis=0, keepdims=True
        )
        at_z, at_y, at_core = v >> 13, (v >> 11) & 3, (v >> 10) & 1
        here = jnp.where(over_z, at_y - y, at_z - z) == 0
        away = jnp.where(over_z, (at_z - z) & 3, (at_y - y) & 3)
        other = at_core ^ core
        shard = jnp.where(away == 0, other, away + 1 + 3 * other)
        local = shard * ROWS_DEV + (v & (ROWS_DEV - 1))
        local = jnp.where(here & (slot < used), local, -1)
        for s in range(8):
            lid_ref[0, s, n : n + 1, :] = local[s : s + 1, :]
    for g in range(BAG_BLOCKS // 8):
        rows = pl.ds(g * 8, 8)
        lids = [lid_ref[0, s, rows, :] for s in range(8)]
        high = [x >> 8 for x in lids]
        low = [(x & (SUB - 1)).astype(jnp.float32) for x in lids]

        def one_block(blk, mask):
            at = [h == blk for h in high]
            up = [jnp.where(a, l, 511.0) for a, l in zip(at, low)]
            down = [jnp.where(a, l, -1.0) for a, l in zip(at, low)]
            first = functools.reduce(jnp.minimum, up)
            last = functools.reduce(jnp.maximum, down)
            n_first = sum(jnp.where(u == first, 1.0, 0.0) for u in up)
            n_last = sum(jnp.where(d == last, 1.0, 0.0) for d in down)
            total = sum(jnp.where(a, 1.0, 0.0) for a in at)
            more = (n_first + n_last) < total
            keys_ref[0, blk, 0, rows, :] = first
            keys_ref[0, blk, 1, rows, :] = n_first
            keys_ref[0, blk, 2, rows, :] = jnp.where(last == first, -1.0, last)
            keys_ref[0, blk, 3, rows, :] = n_last
            return mask | jnp.where(more, jnp.int32(1) << blk, 0)

        mask_ref[0, rows, :] = lax.fori_loop(
            0, BLOCKS, one_block, jnp.zeros((8, LANES), jnp.int32)
        )


def prep(pos, idx, lens):
    tables = idx.shape[0]
    return pl.pallas_call(
        prep_kernel,
        grid=(tables,),
        in_specs=[
            pl.BlockSpec(memory_space=pltpu.SMEM),
            pl.BlockSpec((1,) + idx.shape[1:], lambda j: (j, 0, 0)),
            pl.BlockSpec(lens.shape, lambda j: (0, 0)),
        ],
        out_specs=[
            pl.BlockSpec((1, BLOCKS, 4, BAG_BLOCKS, LANES), lambda j: (j, 0, 0, 0, 0)),
            pl.BlockSpec((1, 8, BAG_BLOCKS, LANES), lambda j: (j, 0, 0, 0)),
            pl.BlockSpec((1, BAG_BLOCKS, LANES), lambda j: (j, 0, 0)),
        ],
        out_shape=[
            jax.ShapeDtypeStruct((tables, BLOCKS, 4, BAG_BLOCKS, LANES), jnp.float32),
            jax.ShapeDtypeStruct((tables, 8, BAG_BLOCKS, LANES), jnp.int32),
            jax.ShapeDtypeStruct((tables, BAG_BLOCKS, LANES), jnp.int32),
        ],
        compiler_params=pltpu.CompilerParams(vmem_limit_bytes=32 << 20),
        cost_estimate=pl.CostEstimate(
            flops=40_000_000, bytes_accessed=9_000_000, transcendentals=0
        ),
        name="prep",
    )(pos, idx, lens)


def pool_kernel(first_shard, n_shards, has_base, is_last, table0, *refs):
    mask_ref, keys_ref, lid_ref = refs[:3]
    tabs = refs[3 : 3 + n_shards]
    refs = refs[3 + n_shards :]
    if has_base:
        base_ref, refs = refs[0], refs[1:]
    if is_last:
        outs, (sums, counts, extra) = refs[:4], refs[4:]
    else:
        sums, counts, extra = refs
    table, step = pl.program_id(0), pl.program_id(1)
    first_block = first_shard * (ROWS_DEV // SUB)
    n_blocks = n_shards * (ROWS_DEV // SUB)
    row_ids = [
        (lax.broadcasted_iota(jnp.int32, (16, PAIR), 0) + c * 16)
        .astype(jnp.float32)
        .astype(jnp.bfloat16)
        for c in range(SUB // 16)
    ]

    def wide(x):
        return jnp.broadcast_to(x, (16, LANES)).astype(jnp.bfloat16)

    for part in range(2):
        bag = 4 * step + 2 * part
        for blk in range(n_blocks):
            k1, m1, k2, m2 = (
                jnp.concatenate(
                    [
                        wide(keys_ref[0, first_block + blk, v, pl.ds(bag + half, 1), :])
                        for half in range(2)
                    ],
                    axis=1,
                )
                for v in range(4)
            )
            for c in range(SUB // 16):
                counts[part, blk * SUB + c * 16 : blk * SUB + (c + 1) * 16, :] = jnp.where(
                    k1 == row_ids[c], m1, jnp.where(k2 == row_ids[c], m2, jnp.bfloat16(0))
                )
        total = base_ref[0, 0, part] if has_base else None
        for g in range(n_shards):
            product = jnp.dot(
                tabs[g][0],
                counts[part, g * ROWS_DEV : (g + 1) * ROWS_DEV, :],
                preferred_element_type=jnp.float32,
            )
            total = product if total is None else total + product
        sums[0, 0, part] = total

    stage_bits = ((1 << n_blocks) - 1) << first_block
    stage_bits = stage_bits - (1 << 32) if stage_bits >= 1 << 31 else stage_bits
    for part in range(2):
        bag = 4 * step + 2 * part
        mask = mask_ref[table0 + table, bag] | mask_ref[table0 + table, bag + 1]

        @pl.when((mask & jnp.int32(stage_bits)) != 0)
        def _(part=part, bag=bag, mask=mask):
            def fix(at, carry):
                blk = first_block + at

                @pl.when(((mask >> blk) & 1) == 1)
                def _():
                    for half in range(2):
                        row = pl.ds(bag + half, 1)
                        k1 = keys_ref[0, blk, 0, row, :]
                        k2 = keys_ref[0, blk, 2, row, :]
                        left = []
                        for s in range(8):
                            x = lid_ref[0, s, row, :]
                            low = jnp.where(
                                (x >> 8) == blk, (x & (SUB - 1)).astype(jnp.float32), -1.0
                            )
                            left.append(wide(jnp.where((low == k1) | (low == k2), -1.0, low)))
                        for c in range(SUB // 16):
                            n = jnp.zeros((16, LANES), jnp.bfloat16)
                            for k in left:
                                n = n + jnp.where(
                                    k == row_ids[c][:, :LANES], jnp.bfloat16(1), jnp.bfloat16(0)
                                )
                            extra[c * 16 : (c + 1) * 16, half * LANES : (half + 1) * LANES] = n
                    columns = pl.ds(pl.multiple_of((at & 3) * SUB, SUB), SUB)
                    for g in range(n_shards):

                        @pl.when((at >> 2) == g)
                        def _(g=g):
                            sums[0, 0, part] += jnp.dot(
                                tabs[g][0, :, columns],
                                extra[...],
                                preferred_element_type=jnp.float32,
                            )

                return carry

            lax.fori_loop(0, n_blocks, fix, 0)

    if is_last:
        for d in range(4):

            @pl.when(step == d)
            def _(d=d):
                for part in range(2):
                    result = sums[0, 0, part].astype(jnp.bfloat16)
                    outs[d][0, 2 * part] = result[:, :LANES]
                    outs[d][0, 2 * part + 1] = result[:, LANES:]


def pool(first_shard, tables, masks, keys, lids, shards, base, is_last, name):
    n_tables = len(tables)
    table0 = tables[0]
    n_shards = len(shards)
    _, emb, rows = shards[0].shape
    sums_block = (1, 1, 2, emb, PAIR)
    sums_spec = pl.BlockSpec(sums_block, lambda j, i: (j, i, 0, 0, 0))
    in_specs = [
        pl.BlockSpec(memory_space=pltpu.SMEM),
        pl.BlockSpec((1,) + keys.shape[1:], lambda j, i: (table0 + j, 0, 0, 0, 0)),
        pl.BlockSpec((1,) + lids.shape[1:], lambda j, i: (table0 + j, 0, 0, 0)),
    ] + [pl.BlockSpec((1, emb, rows), lambda j, i: (j, 0, 0))] * n_shards
    args = [masks, keys, lids, *shards]
    if base is not None:
        from_table = base[1]
        in_specs.append(pl.BlockSpec(sums_block, lambda j, i: (from_table + j, i, 0, 0, 0)))
        args.append(base[0])
    scratch = [
        pltpu.VMEM((2, n_shards * rows, PAIR), jnp.bfloat16),
        pltpu.VMEM((SUB, PAIR), jnp.bfloat16),
    ]
    if is_last:
        out_specs = [pl.BlockSpec((1, 4, emb, LANES), lambda j, i: (j, 0, 0, 0))] * 4
        out_shape = [jax.ShapeDtypeStruct((n_tables, 4, emb, LANES), jnp.bfloat16)] * 4
        scratch = [pltpu.VMEM(sums_block, jnp.float32)] + scratch
    else:
        out_specs = sums_spec
        out_shape = jax.ShapeDtypeStruct((n_tables, 4, 2, emb, PAIR), jnp.float32)
    return pl.pallas_call(
        functools.partial(
            pool_kernel, first_shard, n_shards, base is not None, is_last, table0
        ),
        grid=(n_tables, 4),
        in_specs=in_specs,
        out_specs=out_specs,
        out_shape=out_shape,
        scratch_shapes=scratch,
        compiler_params=pltpu.CompilerParams(vmem_limit_bytes=32 << 20),
        cost_estimate=pl.CostEstimate(
            flops=2 * n_tables * n_shards * rows * 2048 * 256,
            bytes_accessed=5_000_000,
            transcendentals=0,
        ),
        name=name,
    )(*args)


def tail_kernel(
    host_ref,
    order_ref,
    proj_ref,
    compress_ref,
    *rest,
):
    parts = rest[:8]
    fm_gain_ref, up_ref, down_ref, gain_ref, out_ref, emb, gram, summed = rest[8:]
    host = host_ref[0]
    for d in range(4):
        source = (host - d) & 3
        for j in range(4):
            at = order_ref[source * 4 + j]
            part = parts[(j // 2) * 4 + d]
            emb[pl.ds(at, 1), :, :] = part[j % 2 : j % 2 + 1, :, :].astype(jnp.float32)
    feats, width, lanes = emb.shape
    rank = proj_ref.shape[0]

    for f in range(feats):
        x = emb[f]
        for g in range(f + 1):
            dot = jnp.sum(x * emb[g], axis=0, keepdims=True)
            gram[f, g : g + 1, :] = dot
            if g != f:
                gram[g, f : f + 1, :] = dot
    rows = []
    for k in range(rank):
        row = None
        for g in range(feats):
            term = proj_ref[k, g] * gram[g]
            row = term if row is None else row + term
        rows.append(row)
    inv = 1.0 / (rank * feats)
    mean = jnp.sum(sum(rows), axis=0, keepdims=True) * inv
    rows = [r - mean for r in rows]
    spread = jnp.sum(sum(r * r for r in rows), axis=0, keepdims=True) * inv
    scale = 1.0 / jnp.sqrt(spread + 1e-05)
    normed = jnp.concatenate(
        [rows[k] * scale * fm_gain_ref[:, k : k + 1] for k in range(rank)], axis=0
    ).astype(jnp.bfloat16)
    hidden = jnp.maximum(
        jnp.dot(up_ref[...], normed, preferred_element_type=jnp.float32), 0.0
    ).astype(jnp.bfloat16)
    half = feats // 2
    for m in range(half):
        block = jnp.dot(
            down_ref[m * width : (m + 1) * width, :], hidden, preferred_element_type=jnp.float32
        )
        summed[m] = block + emb[m]
        acc = emb[half + m]
        for f in range(feats):
            acc = acc + compress_ref[m, f] * emb[f]
        summed[half + m] = acc
    inv = 1.0 / (feats * width)
    total = summed[0]
    for f in range(1, feats):
        total = total + summed[f]
    mean = jnp.sum(total, axis=0, keepdims=True) * inv
    square = None
    for f in range(feats):
        c = summed[f] - mean
        square = c * c if square is None else square + c * c
    spread = jnp.sum(square, axis=0, keepdims=True) * inv
    scale = 1.0 / jnp.sqrt(spread + 1e-05)
    for f in range(feats):
        out_ref[f] = ((summed[f] - mean) * scale * gain_ref[:, f : f + 1]).astype(jnp.bfloat16)


def tail(host, order, proj, compress, parts, fm_gain, up, down, gain):
    feats, width = order.shape[0], parts[0].shape[1]
    smem = pl.BlockSpec(memory_space=pltpu.SMEM)
    vmem = pl.BlockSpec(memory_space=pltpu.VMEM)
    return pl.pallas_call(
        tail_kernel,
        in_specs=[smem] * 4 + [vmem] * 12,
        out_specs=vmem,
        out_shape=jax.ShapeDtypeStruct((feats, width, LANES), jnp.bfloat16),
        scratch_shapes=[
            pltpu.VMEM((feats, width, LANES), jnp.float32),
            pltpu.VMEM((feats, feats, LANES), jnp.float32),
            pltpu.VMEM((feats, width, LANES), jnp.float32),
        ],
        compiler_params=pltpu.CompilerParams(vmem_limit_bytes=32 << 20),
        cost_estimate=pl.CostEstimate(
            flops=1_000_000_000, bytes_accessed=8_000_000, transcendentals=0
        ),
        name="tail",
    )(host, order, proj, compress, *parts, fm_gain, up, down, gain)


def row_moves(axis, step):
    pairs = []
    for z in range(4):
        for y in range(4):
            for core in range(2):
                to = {
                    "z": (((z + step) % 4) * 8 + y * 2 + core),
                    "y": (z * 8 + ((y + step) % 4) * 2 + core),
                    "core": (z * 8 + y * 2 + (core + step) % 2),
                }[axis]
                pairs.append((z * 8 + y * 2 + core, to))
    return pairs


def near_shards(shard, axis):
    return [lax.ppermute(shard, "row", row_moves(axis, 4 - rel)) for rel in range(1, 4)]


def other_core(x):
    return lax.ppermute(x, "row", row_moves("core", 1))


def exchange(blocks, axis):
    total = blocks[0].astype(jnp.float32)
    for d in range(1, 4):
        total = total + lax.ppermute(blocks[d], "row", row_moves(axis, d)).astype(jnp.float32)
    total = total.astype(jnp.bfloat16)
    return [total[:, 0]] + [
        lax.ppermute(total[:, d], "hst", [(h, (h + d) % 4) for h in range(4)])
        for d in range(1, 4)
    ]


def on_device(
    tables,
    indices,
    lengths,
    feature_order,
    proj_weight,
    fm_gain,
    up_weight,
    down_weight,
    compress_weight,
    out_gain,
):
    host = lax.axis_index("hst")
    row = lax.axis_index("row")
    pos = jnp.stack([host, row // 8, (row // 2) % 4, row % 2]).astype(jnp.int32)
    n_tables = tables.shape[0]
    feats, emb = out_gain.shape
    rank = proj_weight.shape[0]
    width = up_weight.shape[1]

    flipped = jnp.swapaxes(tables, 1, 2)
    keys, lids, masks = prep(pos, jnp.transpose(indices, (1, 2, 0)), lengths.T)
    masks = lax.reduce(masks, jnp.int32(0), lax.bitwise_or, (2,))
    up = jnp.transpose(up_weight.reshape(feats, rank, width), (2, 1, 0)).reshape(
        width, rank * feats
    )
    small = (
        feature_order,
        proj_weight.astype(jnp.float32),
        compress_weight.astype(jnp.float32),
        fm_gain.reshape(feats, rank),
        out_gain.T,
    )
    masks, up, down, small = lax.optimization_barrier((masks, up, down_weight.T, small))
    order, proj, compress, fm_gain, gain = small

    own_far = other_core(flipped)
    pairs = [(0, 1), (2, 3)]
    axes = ["z", "y"]
    near = [near_shards(flipped[2 * p : 2 * p + 2], axes[p]) for p in range(2)]
    sums = pool(
        0, (0, 1, 2, 3), masks, keys, lids, [flipped, own_far], None, False, "pool_own"
    )
    near, sums = lax.optimization_barrier((near, sums))
    far = [[other_core(x) for x in near[p]] for p in range(2)]
    parts = []
    sums = [
        pool(2, pairs[p], masks, keys, lids, near[p], (sums, 2 * p), False, "pool_near")
        for p in range(2)
    ]
    far, sums = lax.optimization_barrier((far, sums))
    for p in range(2):
        blocks = pool(5, pairs[p], masks, keys, lids, far[p], (sums[p], 0), True, "pool_far")
        if p == 0:
            blocks, sums[1] = lax.optimization_barrier((blocks, sums[1]))
        parts += exchange(blocks, axes[1 - p])
    result = tail(pos[:1], order, proj, compress, parts, fm_gain, up, down, gain)
    return jnp.transpose(result, (2, 0, 1))


def solution(mesh):
    in_specs = (
        P("hst", "row", None),
        P(None, "hst", None),
        P(None, "hst"),
        P(),
        P(),
        P(),
        P(),
        P(),
        P(),
        P(),
    )
    out_specs = P(("hst", "row"), None, None)
    return jax.shard_map(
        on_device, mesh=mesh, in_specs=in_specs, out_specs=out_specs, check_vma=False
    )
```

```python
import functools

import jax
import jax.numpy as jnp
from jax import lax
from jax.experimental import pallas as pl
from jax.experimental.pallas import tpu as pltpu
from jax.sharding import PartitionSpec as P

LANES = 128
ROWS_DEV = 1024
SUB = 256
GATHER = 8
BLOCKS = GATHER * ROWS_DEV // SUB
BAG_BLOCKS = 16
PAIR = 2 * LANES


def prep_kernel(pos_ref, idx_ref, len_ref, keys_ref, lid_ref, mask_ref):
    host, z, y, core = pos_ref[0], pos_ref[1], pos_ref[2], pos_ref[3]
    table = pl.program_id(0)
    over_z = table < 2
    slot = lax.broadcasted_iota(jnp.int32, (8, LANES), 0)
    pick = lax.broadcasted_iota(jnp.int32, (len_ref.shape[0], LANES), 0)
    for n in range(BAG_BLOCKS):
        dest, hrel = n // 4, n % 4
        owner_host = (host + hrel) & 3
        row_dev = jnp.where(
            over_z,
            z * 8 + ((y + dest) & 3) * 2 + core,
            ((z + dest) & 3) * 8 + y * 2 + core,
        )
        start = pl.multiple_of((owner_host * 32 + row_dev) * LANES, LANES)
        v = idx_ref[0, :, pl.ds(start, LANES)]
        used = jnp.sum(
            jnp.where(pick == table, len_ref[:, pl.ds(start, LANES)], 0), axis=0, keepdims=True
        )
        at_z, at_y, at_core = v >> 13, (v >> 11) & 3, (v >> 10) & 1
        here = jnp.where(over_z, at_y - y, at_z - z) == 0
        away = (at_y - y) & 3
        other = at_core ^ core
        ring = jnp.where(away == 0, other, away + 1 + 3 * other)
        shard = jnp.where(over_z, at_z * 2 + at_core, ring)
        local = shard * ROWS_DEV + (v & (ROWS_DEV - 1))
        local = jnp.where(here & (slot < used), local, -1)
        for s in range(8):
            lid_ref[0, s, n : n + 1, :] = local[s : s + 1, :]
    for g in range(BAG_BLOCKS // 8):
        rows = pl.ds(g * 8, 8)
        lids = [lid_ref[0, s, rows, :] for s in range(8)]
        high = [x >> 8 for x in lids]
        low = [(x & (SUB - 1)).astype(jnp.float32) for x in lids]

        def one_block(blk, mask):
            at = [h == blk for h in high]
            up = [jnp.where(a, l, 511.0) for a, l in zip(at, low)]
            down = [jnp.where(a, l, -1.0) for a, l in zip(at, low)]
            first = functools.reduce(jnp.minimum, up)
            last = functools.reduce(jnp.maximum, down)
            n_first = sum(jnp.where(u == first, 1.0, 0.0) for u in up)
            n_last = sum(jnp.where(d == last, 1.0, 0.0) for d in down)
            total = sum(jnp.where(a, 1.0, 0.0) for a in at)
            more = (n_first + n_last) < total
            keys_ref[0, blk, 0, rows, :] = first
            keys_ref[0, blk, 1, rows, :] = n_first
            keys_ref[0, blk, 2, rows, :] = jnp.where(last == first, -1.0, last)
            keys_ref[0, blk, 3, rows, :] = n_last
            return mask | jnp.where(more, jnp.int32(1) << blk, 0)

        mask_ref[0, rows, :] = lax.fori_loop(
            0, BLOCKS, one_block, jnp.zeros((8, LANES), jnp.int32)
        )


def prep(pos, idx, lens):
    tables = idx.shape[0]
    return pl.pallas_call(
        prep_kernel,
        grid=(tables,),
        in_specs=[
            pl.BlockSpec(memory_space=pltpu.SMEM),
            pl.BlockSpec((1,) + idx.shape[1:], lambda j: (j, 0, 0)),
            pl.BlockSpec(lens.shape, lambda j: (0, 0)),
        ],
        out_specs=[
            pl.BlockSpec((1, BLOCKS, 4, BAG_BLOCKS, LANES), lambda j: (j, 0, 0, 0, 0)),
            pl.BlockSpec((1, 8, BAG_BLOCKS, LANES), lambda j: (j, 0, 0, 0)),
            pl.BlockSpec((1, BAG_BLOCKS, LANES), lambda j: (j, 0, 0)),
        ],
        out_shape=[
            jax.ShapeDtypeStruct((tables, BLOCKS, 4, BAG_BLOCKS, LANES), jnp.float32),
            jax.ShapeDtypeStruct((tables, 8, BAG_BLOCKS, LANES), jnp.int32),
            jax.ShapeDtypeStruct((tables, BAG_BLOCKS, LANES), jnp.int32),
        ],
        compiler_params=pltpu.CompilerParams(vmem_limit_bytes=60 << 20),
        cost_estimate=pl.CostEstimate(
            flops=40_000_000, bytes_accessed=9_000_000, transcendentals=0
        ),
        name="prep",
    )(pos, idx, lens)


def pool_kernel(first_shard, n_shards, has_base, is_last, table0, *refs):
    mask_ref, keys_ref, lid_ref = refs[:3]
    tabs = refs[3 : 3 + n_shards]
    refs = refs[3 + n_shards :]
    if has_base:
        base_ref, refs = refs[0], refs[1:]
    if is_last:
        outs, (sums, counts, extra) = refs[:4], refs[4:]
    else:
        sums, counts, extra = refs
    table, step = pl.program_id(0), pl.program_id(1)
    first_block = first_shard * (ROWS_DEV // SUB)
    n_blocks = n_shards * (ROWS_DEV // SUB)
    row_ids = [
        (lax.broadcasted_iota(jnp.int32, (16, PAIR), 0) + c * 16)
        .astype(jnp.float32)
        .astype(jnp.bfloat16)
        for c in range(SUB // 16)
    ]

    def wide(x):
        return jnp.broadcast_to(x, (16, LANES)).astype(jnp.bfloat16)

    for part in range(2):
        bag = 4 * step + 2 * part
        for blk in range(n_blocks):
            k1, m1, k2, m2 = (
                jnp.concatenate(
                    [
                        wide(keys_ref[0, first_block + blk, v, pl.ds(bag + half, 1), :])
                        for half in range(2)
                    ],
                    axis=1,
                )
                for v in range(4)
            )
            for c in range(SUB // 16):
                counts[part, blk * SUB + c * 16 : blk * SUB + (c + 1) * 16, :] = jnp.where(
                    k1 == row_ids[c], m1, jnp.where(k2 == row_ids[c], m2, jnp.bfloat16(0))
                )
        total = base_ref[0, 0, part] if has_base else None
        for g in range(n_shards):
            product = jnp.dot(
                tabs[g][0],
                counts[part, g * ROWS_DEV : (g + 1) * ROWS_DEV, :],
                preferred_element_type=jnp.float32,
            )
            total = product if total is None else total + product
        sums[0, 0, part] = total

    stage_bits = ((1 << n_blocks) - 1) << first_block
    stage_bits = stage_bits - (1 << 32) if stage_bits >= 1 << 31 else stage_bits
    for part in range(2):
        bag = 4 * step + 2 * part
        mask = mask_ref[table0 + table, bag] | mask_ref[table0 + table, bag + 1]

        @pl.when((mask & jnp.int32(stage_bits)) != 0)
        def _(part=part, bag=bag, mask=mask):
            def fix(at, carry):
                blk = first_block + at

                @pl.when(((mask >> blk) & 1) == 1)
                def _():
                    for half in range(2):
                        row = pl.ds(bag + half, 1)
                        k1 = keys_ref[0, blk, 0, row, :]
                        k2 = keys_ref[0, blk, 2, row, :]
                        left = []
                        for s in range(8):
                            x = lid_ref[0, s, row, :]
                            low = jnp.where(
                                (x >> 8) == blk, (x & (SUB - 1)).astype(jnp.float32), -1.0
                            )
                            left.append(wide(jnp.where((low == k1) | (low == k2), -1.0, low)))
                        for c in range(SUB // 16):
                            n = jnp.zeros((16, LANES), jnp.bfloat16)
                            for k in left:
                                n = n + jnp.where(
                                    k == row_ids[c][:, :LANES], jnp.bfloat16(1), jnp.bfloat16(0)
                                )
                            extra[c * 16 : (c + 1) * 16, half * LANES : (half + 1) * LANES] = n
                    columns = pl.ds(pl.multiple_of((at & 3) * SUB, SUB), SUB)
                    for g in range(n_shards):

                        @pl.when((at >> 2) == g)
                        def _(g=g):
                            sums[0, 0, part] += jnp.dot(
                                tabs[g][0, :, columns],
                                extra[...],
                                preferred_element_type=jnp.float32,
                            )

                return carry

            lax.fori_loop(0, n_blocks, fix, 0)

    if is_last:
        for d in range(4):

            @pl.when(step == d)
            def _(d=d):
                for part in range(2):
                    result = sums[0, 0, part].astype(jnp.bfloat16)
                    outs[d][2 * part, 0] = result[:, :LANES]
                    outs[d][2 * part + 1, 0] = result[:, LANES:]


def piece(array, first_table=0, stacked=None):
    block = (1,) + array.shape[-2:]
    if stacked is None:
        return array, pl.BlockSpec(block, lambda j, i: (first_table + j, 0, 0))
    return array, pl.BlockSpec((None,) + block, lambda j, i: (stacked, j, 0, 0))


def pool(first_shard, tables, masks, keys, lids, shards, base, is_last, name):
    n_tables = len(tables)
    table0 = tables[0]
    n_shards = len(shards)
    emb, rows = shards[0][0].shape[-2:]
    sums_block = (1, 1, 2, emb, PAIR)
    sums_spec = pl.BlockSpec(sums_block, lambda j, i: (j, i, 0, 0, 0))
    in_specs = [
        pl.BlockSpec(memory_space=pltpu.SMEM),
        pl.BlockSpec((1,) + keys.shape[1:], lambda j, i: (table0 + j, 0, 0, 0, 0)),
        pl.BlockSpec((1,) + lids.shape[1:], lambda j, i: (table0 + j, 0, 0, 0)),
    ] + [spec for _, spec in shards]
    args = [masks, keys, lids] + [array for array, _ in shards]
    if base is not None:
        in_specs.append(sums_spec)
        args.append(base)
    scratch = [
        pltpu.VMEM((2, n_shards * rows, PAIR), jnp.bfloat16),
        pltpu.VMEM((SUB, PAIR), jnp.bfloat16),
    ]
    if is_last:
        out_specs = [pl.BlockSpec((4, 1, emb, LANES), lambda j, i: (0, j, 0, 0))] * 4
        out_shape = [jax.ShapeDtypeStruct((4, n_tables, emb, LANES), jnp.bfloat16)] * 4
        scratch = [pltpu.VMEM(sums_block, jnp.float32)] + scratch
    else:
        out_specs = sums_spec
        out_shape = jax.ShapeDtypeStruct((n_tables, 4, 2, emb, PAIR), jnp.float32)
    return pl.pallas_call(
        functools.partial(
            pool_kernel, first_shard, n_shards, base is not None, is_last, table0
        ),
        grid=(n_tables, 4),
        in_specs=in_specs,
        out_specs=out_specs,
        out_shape=out_shape,
        scratch_shapes=scratch,
        compiler_params=pltpu.CompilerParams(vmem_limit_bytes=60 << 20),
        cost_estimate=pl.CostEstimate(
            flops=2 * n_tables * n_shards * rows * 2048 * 256,
            bytes_accessed=5_000_000,
            transcendentals=0,
        ),
        name=name,
    )(*args)


def tail_kernel(
    host_ref,
    order_ref,
    compress_ref,
    *rest,
):
    parts = rest[:8]
    proj_ref, fm_gain_ref, up_ref, down_ref, gain_ref, out_ref, emb, gram, summed = rest[8:]
    host = host_ref[0]
    for d in range(4):
        source = (host - d) & 3
        for j in range(4):
            at = order_ref[source * 4 + j]
            part = parts[(j // 2) * 4 + d]
            emb[at] = part[j % 2].astype(jnp.float32)
    feats, width, lanes = emb.shape
    rank = proj_ref.shape[0]

    for f in range(feats):
        x = emb[f]
        for g in range(f + 1):
            dot = jnp.sum(x * emb[g], axis=0, keepdims=True)
            gram[f, g : g + 1, :] = dot
            if g != f:
                gram[g, f : f + 1, :] = dot
    proj = [jnp.broadcast_to(proj_ref[:, g : g + 1], (rank, lanes)) for g in range(feats)]
    rows = []
    for f in range(feats):
        row = None
        for g in range(feats):
            term = proj[g] * gram[f, g : g + 1, :]
            row = term if row is None else row + term
        rows.append(row)
    inv = 1.0 / (rank * feats)
    mean = jnp.sum(sum(rows), axis=0, keepdims=True) * inv
    rows = [r - mean for r in rows]
    spread = jnp.sum(sum(r * r for r in rows), axis=0, keepdims=True) * inv
    scale = 1.0 / jnp.sqrt(spread + 1e-05)
    normed = jnp.concatenate(
        [rows[f] * scale * fm_gain_ref[:, f : f + 1] for f in range(feats)], axis=0
    ).astype(jnp.bfloat16)
    hidden = jnp.maximum(
        jnp.dot(up_ref[...], normed, preferred_element_type=jnp.float32), 0.0
    ).astype(jnp.bfloat16)
    half = feats // 2
    for m in range(half):
        block = jnp.dot(
            down_ref[m * width : (m + 1) * width, :], hidden, preferred_element_type=jnp.float32
        )
        summed[m] = block + emb[m]
        acc = emb[half + m]
        for f in range(feats):
            acc = acc + compress_ref[m, f] * emb[f]
        summed[half + m] = acc
    inv = 1.0 / (feats * width)
    total = summed[0]
    for f in range(1, feats):
        total = total + summed[f]
    mean = jnp.sum(total, axis=0, keepdims=True) * inv
    square = None
    for f in range(feats):
        c = summed[f] - mean
        square = c * c if square is None else square + c * c
    spread = jnp.sum(square, axis=0, keepdims=True) * inv
    scale = 1.0 / jnp.sqrt(spread + 1e-05)
    for f in range(feats):
        out_ref[f] = ((summed[f] - mean) * scale * gain_ref[:, f : f + 1]).astype(jnp.bfloat16)


def tail(host, order, proj, compress, parts, fm_gain, up, down, gain):
    feats, width = order.shape[0], parts[0].shape[2]
    smem = pl.BlockSpec(memory_space=pltpu.SMEM)
    vmem = pl.BlockSpec(memory_space=pltpu.VMEM)
    mine = pl.BlockSpec((None,) + parts[0].shape[1:], lambda i: (0, 0, 0, 0))
    there = pl.BlockSpec(parts[1].shape, lambda i: (0, 0, 0))
    return pl.pallas_call(
        tail_kernel,
        grid=(1,),
        in_specs=[smem] * 3 + ([mine] + [there] * 3) * 2 + [vmem] * 5,
        out_specs=vmem,
        out_shape=jax.ShapeDtypeStruct((feats, width, LANES), jnp.bfloat16),
        scratch_shapes=[
            pltpu.VMEM((feats, width, LANES), jnp.float32),
            pltpu.VMEM((feats, feats, LANES), jnp.float32),
            pltpu.VMEM((feats, width, LANES), jnp.float32),
        ],
        compiler_params=pltpu.CompilerParams(vmem_limit_bytes=32 << 20),
        cost_estimate=pl.CostEstimate(
            flops=1_000_000_000, bytes_accessed=8_000_000, transcendentals=0
        ),
        name="tail",
    )(host, order, compress, *parts, proj, fm_gain, up, down, gain)


def row_moves(axis, step):
    pairs = []
    for z in range(4):
        for y in range(4):
            for core in range(2):
                to = {
                    "z": (((z + step) % 4) * 8 + y * 2 + core),
                    "y": (z * 8 + ((y + step) % 4) * 2 + core),
                    "core": (z * 8 + y * 2 + (core + step) % 2),
                }[axis]
                pairs.append((z * 8 + y * 2 + core, to))
    return pairs


def near_shards(shard, axis):
    return [lax.ppermute(shard, "row", row_moves(axis, 4 - rel)) for rel in range(1, 4)]


def other_core(x):
    return lax.ppermute(x, "row", row_moves("core", 1))


def to_owners(blocks, axis):
    return [blocks[0]] + [
        lax.ppermute(blocks[d], "row", row_moves(axis, d)) for d in range(1, 4)
    ]


def to_hosts(blocks):
    total = sum(b.astype(jnp.float32) for b in blocks).astype(jnp.bfloat16)
    return [total] + [
        lax.ppermute(total[d], "hst", [(h, (h + d) % 4) for h in range(4)]) for d in range(1, 4)
    ]


def on_device(
    tables,
    indices,
    lengths,
    feature_order,
    proj_weight,
    fm_gain,
    up_weight,
    down_weight,
    compress_weight,
    out_gain,
):
    host = lax.axis_index("hst")
    row = lax.axis_index("row")
    pos = jnp.stack([host, row // 8, (row // 2) % 4, row % 2]).astype(jnp.int32)
    feats = out_gain.shape[0]
    rank = proj_weight.shape[0]

    flipped = jnp.swapaxes(tables, 1, 2)
    keys, lids, masks = prep(pos, jnp.transpose(indices, (1, 2, 0)), lengths.T)
    masks = lax.reduce(masks, jnp.int32(0), lax.bitwise_or, (2,))
    small = (
        feature_order,
        proj_weight.astype(jnp.float32),
        compress_weight.astype(jnp.float32),
        fm_gain.reshape(feats, rank).T,
        out_gain.T,
    )
    masks, up, down, small = lax.optimization_barrier(
        (masks, up_weight.T, down_weight.T, small)
    )
    order, proj, compress, fm_gain, gain = small

    ring = flipped[2:]
    own_far = other_core(ring)
    near = near_shards(ring, "y")
    whole = lax.all_gather(
        flipped[:2],
        "row",
        axis_index_groups=[
            [z * 8 + y * 2 + core for z in range(4) for core in range(2)] for y in range(4)
        ],
    )
    sums = pool(
        0,
        (2, 3),
        masks,
        keys,
        lids,
        [piece(flipped, 2), piece(own_far)],
        None,
        False,
        "pool_own",
    )
    near, sums = lax.optimization_barrier((near, sums))
    far = [other_core(x) for x in near]
    sums = pool(2, (2, 3), masks, keys, lids, [piece(x) for x in near], sums, False, "pool_near")
    far, sums = lax.optimization_barrier((far, sums))
    blocks = pool(5, (2, 3), masks, keys, lids, [piece(x) for x in far], sums, True, "pool_far")
    masks, _ = lax.optimization_barrier((masks, blocks))
    arrived = to_owners(blocks, "z")
    blocks = pool(
        0,
        (0, 1),
        masks,
        keys,
        lids,
        [piece(whole, stacked=g) for g in range(GATHER)],
        None,
        True,
        "pool_whole",
    )
    blocks, arrived = lax.optimization_barrier((blocks, arrived))
    parts = to_hosts(to_owners(blocks, "y")) + to_hosts(arrived)
    result = tail(pos[:1], order, proj, compress, parts, fm_gain, up, down, gain)
    return jnp.transpose(result, (2, 0, 1))


def solution(mesh):
    in_specs = (
        P("hst", "row", None),
        P(None, "hst", None),
        P(None, "hst"),
        P(),
        P(),
        P(),
        P(),
        P(),
        P(),
        P(),
    )
    out_specs = P(("hst", "row"), None, None)
    return jax.shard_map(
        on_device, mesh=mesh, in_specs=in_specs, out_specs=out_specs, check_vma=False
    )
```

```python
import functools

import jax
import jax.numpy as jnp
from jax import lax
from jax.experimental import pallas as pl
from jax.experimental.pallas import tpu as pltpu
from jax.sharding import PartitionSpec as P

LANES = 128
ROWS_DEV = 1024
SUB = 256
GATHER = 8
BLOCKS = GATHER * ROWS_DEV // SUB
BAG_BLOCKS = 16
PAIR = 2 * LANES


def prep_kernel(pos_ref, idx_ref, len_ref, keys_ref, lid_ref, mask_ref):
    host, z, y, core = pos_ref[0], pos_ref[1], pos_ref[2], pos_ref[3]
    table = pl.program_id(0)
    over_z = table < 2
    slot = lax.broadcasted_iota(jnp.int32, (8, LANES), 0)
    pick = lax.broadcasted_iota(jnp.int32, (len_ref.shape[0], LANES), 0)
    for n in range(BAG_BLOCKS):
        dest, hrel = n // 4, n % 4
        owner_host = (host + hrel) & 3
        row_dev = jnp.where(
            over_z,
            z * 8 + ((y + dest) & 3) * 2 + core,
            ((z + dest) & 3) * 8 + y * 2 + core,
        )
        start = pl.multiple_of((owner_host * 32 + row_dev) * LANES, LANES)
        v = idx_ref[0, :, pl.ds(start, LANES)]
        used = jnp.sum(
            jnp.where(pick == table, len_ref[:, pl.ds(start, LANES)], 0), axis=0, keepdims=True
        )
        at_z, at_y, at_core = v >> 13, (v >> 11) & 3, (v >> 10) & 1
        here = jnp.where(over_z, at_y - y, at_z - z) == 0
        away = jnp.where(over_z, at_z - z, at_y - y) & 3
        shard = jnp.where(away == 2, 4, 2 + (away >> 1))
        other = at_core ^ core
        shard = jnp.where(away == 0, other, shard + 3 * other)
        local = shard * ROWS_DEV + (v & (ROWS_DEV - 1))
        local = jnp.where(here & (slot < used), local, -1)
        for s in range(8):
            lid_ref[0, s, n : n + 1, :] = local[s : s + 1, :]
    for g in range(BAG_BLOCKS // 8):
        rows = pl.ds(g * 8, 8)
        lids = [lid_ref[0, s, rows, :] for s in range(8)]
        high = [x >> 8 for x in lids]
        low = [(x & (SUB - 1)).astype(jnp.float32) for x in lids]

        def one_block(blk, mask):
            at = [h == blk for h in high]
            up = [jnp.where(a, l, 511.0) for a, l in zip(at, low)]
            down = [jnp.where(a, l, -1.0) for a, l in zip(at, low)]
            first = functools.reduce(jnp.minimum, up)
            last = functools.reduce(jnp.maximum, down)
            n_first = sum(jnp.where(u == first, 1.0, 0.0) for u in up)
            n_last = sum(jnp.where(d == last, 1.0, 0.0) for d in down)
            total = sum(jnp.where(a, 1.0, 0.0) for a in at)
            more = (n_first + n_last) < total
            keys_ref[0, blk, 0, rows, :] = first
            keys_ref[0, blk, 1, rows, :] = n_first
            keys_ref[0, blk, 2, rows, :] = jnp.where(last == first, -1.0, last)
            keys_ref[0, blk, 3, rows, :] = n_last
            return mask | jnp.where(more, jnp.int32(1) << blk, 0)

        mask_ref[0, rows, :] = lax.fori_loop(
            0, BLOCKS, one_block, jnp.zeros((8, LANES), jnp.int32)
        )


def prep(pos, idx, lens):
    tables = idx.shape[0]
    return pl.pallas_call(
        prep_kernel,
        grid=(tables,),
        in_specs=[
            pl.BlockSpec(memory_space=pltpu.SMEM),
            pl.BlockSpec((1,) + idx.shape[1:], lambda j: (j, 0, 0)),
            pl.BlockSpec(lens.shape, lambda j: (0, 0)),
        ],
        out_specs=[
            pl.BlockSpec((1, BLOCKS, 4, BAG_BLOCKS, LANES), lambda j: (j, 0, 0, 0, 0)),
            pl.BlockSpec((1, 8, BAG_BLOCKS, LANES), lambda j: (j, 0, 0, 0)),
            pl.BlockSpec((1, BAG_BLOCKS, LANES), lambda j: (j, 0, 0)),
        ],
        out_shape=[
            jax.ShapeDtypeStruct((tables, BLOCKS, 4, BAG_BLOCKS, LANES), jnp.float32),
            jax.ShapeDtypeStruct((tables, 8, BAG_BLOCKS, LANES), jnp.int32),
            jax.ShapeDtypeStruct((tables, BAG_BLOCKS, LANES), jnp.int32),
        ],
        compiler_params=pltpu.CompilerParams(vmem_limit_bytes=60 << 20),
        cost_estimate=pl.CostEstimate(
            flops=40_000_000, bytes_accessed=9_000_000, transcendentals=0
        ),
        name="prep",
    )(pos, idx, lens)


def pool_kernel(layout, has_base, is_last, table0, *refs):
    n_pieces = len(layout)
    mask_ref, lid_ref = refs[:2]
    keys = refs[2 : 2 + n_pieces]
    tabs = refs[2 + n_pieces : 2 + 2 * n_pieces]
    refs = refs[2 + 2 * n_pieces :]
    if has_base:
        base_ref, refs = refs[0], refs[1:]
    if is_last:
        outs, (sums, counts, extra) = refs[:4], refs[4:]
    else:
        sums, counts, extra = refs
    table, step = pl.program_id(0), pl.program_id(1)
    first_block = layout[0][0]
    n_blocks = sum(n for _, n in layout)
    row_ids = [
        (lax.broadcasted_iota(jnp.int32, (16, PAIR), 0) + c * 16)
        .astype(jnp.float32)
        .astype(jnp.bfloat16)
        for c in range(SUB // 16)
    ]

    def wide(x):
        return jnp.broadcast_to(x, (16, LANES)).astype(jnp.bfloat16)

    for part in range(2):
        bag = 4 * step + 2 * part
        for (first, n), key in zip(layout, keys):
            for b in range(n):
                k1, m1, k2, m2 = (
                    jnp.concatenate(
                        [wide(key[0, 0, b, v, pl.ds(bag + half, 1), :]) for half in range(2)],
                        axis=1,
                    )
                    for v in range(4)
                )
                row = (first - first_block + b) * SUB
                for c in range(SUB // 16):
                    counts[part, row + c * 16 : row + (c + 1) * 16, :] = jnp.where(
                        k1 == row_ids[c], m1, jnp.where(k2 == row_ids[c], m2, jnp.bfloat16(0))
                    )
        total = base_ref[0, 0, part] if has_base else None
        for (first, n), tab in zip(layout, tabs):
            row = (first - first_block) * SUB
            product = jnp.dot(
                tab[0], counts[part, row : row + n * SUB, :], preferred_element_type=jnp.float32
            )
            total = product if total is None else total + product
        sums[0, 0, part] = total

    stage_bits = ((1 << n_blocks) - 1) << first_block
    stage_bits = stage_bits - (1 << 32) if stage_bits >= 1 << 31 else stage_bits
    for part in range(2):
        bag = 4 * step + 2 * part
        mask = mask_ref[table0 + table, bag] | mask_ref[table0 + table, bag + 1]

        @pl.when((mask & jnp.int32(stage_bits)) != 0)
        def _(part=part, bag=bag, mask=mask):
            def fix(at, carry):
                blk = first_block + at

                @pl.when(((mask >> blk) & 1) == 1)
                def _():
                    for half in range(2):
                        row = pl.ds(bag + half, 1)
                        lids = [lid_ref[0, s, row, :] for s in range(8)]
                        low = [
                            jnp.where((x >> 8) == blk, (x & (SUB - 1)).astype(jnp.float32), -1.0)
                            for x in lids
                        ]
                        last = functools.reduce(jnp.maximum, low)
                        first = functools.reduce(
                            jnp.minimum, [jnp.where(x < 0.0, 511.0, x) for x in low]
                        )
                        left = [
                            wide(jnp.where((x == first) | (x == last), -1.0, x)) for x in low
                        ]
                        for c in range(SUB // 16):
                            n = jnp.zeros((16, LANES), jnp.bfloat16)
                            for k in left:
                                n = n + jnp.where(
                                    k == row_ids[c][:, :LANES], jnp.bfloat16(1), jnp.bfloat16(0)
                                )
                            extra[c * 16 : (c + 1) * 16, half * LANES : (half + 1) * LANES] = n
                    for (first, n), tab in zip(layout, tabs):

                        @pl.when((blk >= first) & (blk < first + n))
                        def _(first=first, tab=tab):
                            columns = pl.ds(pl.multiple_of((blk - first) * SUB, SUB), SUB)
                            sums[0, 0, part] += jnp.dot(
                                tab[0, :, columns],
                                extra[...],
                                preferred_element_type=jnp.float32,
                            )

                return carry

            lax.fori_loop(0, n_blocks, fix, 0)

    if is_last:
        for d in range(4):

            @pl.when(step == d)
            def _(d=d):
                for part in range(2):
                    result = sums[0, 0, part].astype(jnp.bfloat16)
                    outs[d][2 * part, 0] = result[:, :LANES]
                    outs[d][2 * part + 1, 0] = result[:, LANES:]


def pool(tables, masks, keys, lids, pieces, base, is_last, name):
    n_tables = len(tables)
    table0 = tables[0]
    emb = pieces[0][0].shape[1]
    sums_block = (1, 1, 2, emb, PAIR)
    sums_spec = pl.BlockSpec(sums_block, lambda j, i: (j, i, 0, 0, 0))
    layout, key_specs, tab_specs = [], [], []
    for array, start_table, shard, start in pieces:
        n = array.shape[2] // SUB
        layout.append(((shard * ROWS_DEV + start) // SUB, n))
        key_specs.append(
            pl.BlockSpec(
                (1, 1, n) + keys.shape[3:],
                lambda j, i, shard=shard, at=start // SUB // n: (table0 + j, shard, at, 0, 0, 0),
            )
        )
        tab_specs.append(
            pl.BlockSpec(
                (1,) + array.shape[1:], lambda j, i, skip=table0 - start_table: (skip + j, 0, 0)
            )
        )
    rows = sum(n for _, n in layout) * SUB
    in_specs = [
        pl.BlockSpec(memory_space=pltpu.SMEM),
        pl.BlockSpec((1,) + lids.shape[1:], lambda j, i: (table0 + j, 0, 0, 0)),
        *key_specs,
        *tab_specs,
    ]
    args = [masks, lids] + [keys] * len(pieces) + [p[0] for p in pieces]
    if base is not None:
        array, start_table = base
        in_specs.append(
            pl.BlockSpec(sums_block, lambda j, i: (table0 - start_table + j, i, 0, 0, 0))
        )
        args.append(array)
    scratch = [
        pltpu.VMEM((2, rows, PAIR), jnp.bfloat16),
        pltpu.VMEM((SUB, PAIR), jnp.bfloat16),
    ]
    if is_last:
        out_specs = [pl.BlockSpec((4, 1, emb, LANES), lambda j, i: (0, j, 0, 0))] * 4
        out_shape = [jax.ShapeDtypeStruct((4, n_tables, emb, LANES), jnp.bfloat16)] * 4
        scratch = [pltpu.VMEM(sums_block, jnp.float32)] + scratch
    else:
        out_specs = sums_spec
        out_shape = jax.ShapeDtypeStruct((n_tables, 4, 2, emb, PAIR), jnp.float32)
    return pl.pallas_call(
        functools.partial(pool_kernel, tuple(layout), base is not None, is_last, table0),
        grid=(n_tables, 4),
        in_specs=in_specs,
        out_specs=out_specs,
        out_shape=out_shape,
        scratch_shapes=scratch,
        compiler_params=pltpu.CompilerParams(vmem_limit_bytes=60 << 20),
        cost_estimate=pl.CostEstimate(
            flops=2 * n_tables * rows * 2048 * 256,
            bytes_accessed=5_000_000,
            transcendentals=0,
        ),
        name=name,
    )(*args)


def tail_kernel(
    host_ref,
    order_ref,
    compress_ref,
    *rest,
):
    parts = rest[:8]
    proj_ref, fm_gain_ref, up_ref, down_ref, gain_ref, out_ref, emb, gram, summed = rest[8:]
    host = host_ref[0]
    for d in range(4):
        source = (host - d) & 3
        for j in range(4):
            at = order_ref[source * 4 + j]
            part = parts[(j // 2) * 4 + d]
            emb[at] = part[j % 2].astype(jnp.float32)
    feats, width, lanes = emb.shape
    rank = proj_ref.shape[0]

    for f in range(feats):
        x = emb[f]
        for g in range(f + 1):
            dot = jnp.sum(x * emb[g], axis=0, keepdims=True)
            gram[f, g : g + 1, :] = dot
            if g != f:
                gram[g, f : f + 1, :] = dot
    proj = [jnp.broadcast_to(proj_ref[:, g : g + 1], (rank, lanes)) for g in range(feats)]
    rows = []
    for f in range(feats):
        row = None
        for g in range(feats):
            term = proj[g] * gram[f, g : g + 1, :]
            row = term if row is None else row + term
        rows.append(row)
    inv = 1.0 / (rank * feats)
    mean = jnp.sum(sum(rows), axis=0, keepdims=True) * inv
    rows = [r - mean for r in rows]
    spread = jnp.sum(sum(r * r for r in rows), axis=0, keepdims=True) * inv
    scale = 1.0 / jnp.sqrt(spread + 1e-05)
    normed = jnp.concatenate(
        [rows[f] * scale * fm_gain_ref[:, f : f + 1] for f in range(feats)], axis=0
    ).astype(jnp.bfloat16)
    hidden = jnp.maximum(
        jnp.dot(up_ref[...], normed, preferred_element_type=jnp.float32), 0.0
    ).astype(jnp.bfloat16)
    half = feats // 2
    for m in range(half):
        block = jnp.dot(
            down_ref[m * width : (m + 1) * width, :], hidden, preferred_element_type=jnp.float32
        )
        summed[m] = block + emb[m]
        acc = emb[half + m]
        for f in range(feats):
            acc = acc + compress_ref[m, f] * emb[f]
        summed[half + m] = acc
    inv = 1.0 / (feats * width)
    total = summed[0]
    for f in range(1, feats):
        total = total + summed[f]
    mean = jnp.sum(total, axis=0, keepdims=True) * inv
    square = None
    for f in range(feats):
        c = summed[f] - mean
        square = c * c if square is None else square + c * c
    spread = jnp.sum(square, axis=0, keepdims=True) * inv
    scale = 1.0 / jnp.sqrt(spread + 1e-05)
    for f in range(feats):
        out_ref[f] = ((summed[f] - mean) * scale * gain_ref[:, f : f + 1]).astype(jnp.bfloat16)


def tail(host, order, proj, compress, parts, fm_gain, up, down, gain):
    feats, width = order.shape[0], parts[0].shape[2]
    smem = pl.BlockSpec(memory_space=pltpu.SMEM)
    vmem = pl.BlockSpec(memory_space=pltpu.VMEM)
    mine = pl.BlockSpec((None,) + parts[0].shape[1:], lambda i: (0, 0, 0, 0))
    there = pl.BlockSpec(parts[1].shape, lambda i: (0, 0, 0))
    return pl.pallas_call(
        tail_kernel,
        grid=(1,),
        in_specs=[smem] * 3 + ([mine] + [there] * 3) * 2 + [vmem] * 5,
        out_specs=vmem,
        out_shape=jax.ShapeDtypeStruct((feats, width, LANES), jnp.bfloat16),
        scratch_shapes=[
            pltpu.VMEM((feats, width, LANES), jnp.float32),
            pltpu.VMEM((feats, feats, LANES), jnp.float32),
            pltpu.VMEM((feats, width, LANES), jnp.float32),
        ],
        compiler_params=pltpu.CompilerParams(vmem_limit_bytes=32 << 20),
        cost_estimate=pl.CostEstimate(
            flops=1_000_000_000, bytes_accessed=8_000_000, transcendentals=0
        ),
        name="tail",
    )(host, order, compress, *parts, proj, fm_gain, up, down, gain)


def row_moves(axis, step):
    pairs = []
    for z in range(4):
        for y in range(4):
            for core in range(2):
                to = {
                    "z": (((z + step) % 4) * 8 + y * 2 + core),
                    "y": (z * 8 + ((y + step) % 4) * 2 + core),
                    "core": (z * 8 + y * 2 + (core + step) % 2),
                }[axis]
                pairs.append((z * 8 + y * 2 + core, to))
    return pairs


def other_core(x):
    return lax.ppermute(x, "row", row_moves("core", 1))


def to_owners(blocks, axis):
    return [blocks[0]] + [
        lax.ppermute(blocks[d], "row", row_moves(axis, d)) for d in range(1, 4)
    ]


def to_hosts(blocks):
    total = sum(b.astype(jnp.float32) for b in blocks).astype(jnp.bfloat16)
    return [total] + [
        lax.ppermute(total[d], "hst", [(h, (h + d) % 4) for h in range(4)]) for d in range(1, 4)
    ]


def on_device(
    tables,
    indices,
    lengths,
    feature_order,
    proj_weight,
    fm_gain,
    up_weight,
    down_weight,
    compress_weight,
    out_gain,
):
    host = lax.axis_index("hst")
    row = lax.axis_index("row")
    pos = jnp.stack([host, row // 8, (row // 2) % 4, row % 2]).astype(jnp.int32)
    feats = out_gain.shape[0]
    rank = proj_weight.shape[0]

    flipped = jnp.swapaxes(tables, 1, 2)
    keys, lids, masks = prep(pos, jnp.transpose(indices, (1, 2, 0)), lengths.T)
    masks = lax.reduce(masks, jnp.int32(0), lax.bitwise_or, (2,))
    small = (
        feature_order,
        proj_weight.astype(jnp.float32),
        compress_weight.astype(jnp.float32),
        fm_gain.reshape(feats, rank).T,
        out_gain.T,
    )
    masks, up, down, small = lax.optimization_barrier(
        (masks, up_weight.T, down_weight.T, small)
    )
    order, proj, compress, fm_gain, gain = small

    keys = keys.reshape((keys.shape[0], GATHER, ROWS_DEV // SUB) + keys.shape[2:])
    pairs = [(0, 1), (2, 3)]
    axes = ["z", "y"]

    def move(x, axis, step):
        return lax.ppermute(x, "row", row_moves(axis, step))

    sides = []
    for p in range(2):
        mine = flipped[2 * p : 2 * p + 2]
        sides.append([move(mine, axes[p], 3), move(mine, axes[p], 1)])
    own_far = other_core(flipped)
    sides, masks = lax.optimization_barrier((sides, masks))
    half = ROWS_DEV // 2
    beyond = [
        [move(up1[:, :, :half], axis, 3), move(down1[:, :, half:], axis, 1)]
        for (up1, down1), axis in zip(sides, axes)
    ]

    def stage(p, arrays, shard):
        one, three, two_a, two_b = arrays
        start = pairs[p][0]
        return [
            (one, start, shard, 0),
            (three, start, shard + 1, 0),
            (two_a, start, shard + 2, 0),
            (two_b, start, shard + 2, half),
        ]

    sums = pool(
        (0, 1, 2, 3),
        masks,
        keys,
        lids,
        [(flipped, 0, 0, 0), (own_far, 0, 1, 0)],
        None,
        False,
        "pool_own",
    )
    sums, beyond, masks = lax.optimization_barrier((sums, beyond, masks))
    near = [sides[p] + beyond[p] for p in range(2)]
    far = [[other_core(x) for x in near[p]] for p in range(2)]
    after = []
    for p in range(2):
        after.append(
            pool(
                pairs[p], masks, keys, lids, stage(p, near[p], 2), (sums, 0), False, "pool_near"
            )
        )
        masks, _ = lax.optimization_barrier((masks, after[p]))
    blocks = pool(
        pairs[0], masks, keys, lids, stage(0, far[0], 5), (after[0], 0), True, "pool_far"
    )
    masks, _ = lax.optimization_barrier((masks, blocks))
    arrived = to_owners(blocks, axes[1])
    blocks = pool(
        pairs[1], masks, keys, lids, stage(1, far[1], 5), (after[1], 2), True, "pool_far"
    )
    blocks, arrived = lax.optimization_barrier((blocks, arrived))
    parts_b = to_hosts(to_owners(blocks, axes[0]))
    parts = to_hosts(arrived) + parts_b
    result = tail(pos[:1], order, proj, compress, parts, fm_gain, up, down, gain)
    return jnp.transpose(result, (2, 0, 1))


def solution(mesh):
    in_specs = (
        P("hst", "row", None),
        P(None, "hst", None),
        P(None, "hst"),
        P(),
        P(),
        P(),
        P(),
        P(),
        P(),
        P(),
    )
    out_specs = P(("hst", "row"), None, None)
    return jax.shard_map(
        on_device, mesh=mesh, in_specs=in_specs, out_specs=out_specs, check_vma=False
    )
```

```python
import functools

import jax
import jax.numpy as jnp
from jax import lax
from jax.experimental import pallas as pl
from jax.experimental.pallas import tpu as pltpu
from jax.sharding import PartitionSpec as P

LANES = 128
ROWS_DEV = 1024
SUB = 256
GATHER = 8
BLOCKS = GATHER * ROWS_DEV // SUB
BAG_BLOCKS = 16
PAIR = 2 * LANES


def prep_kernel(pos_ref, idx_ref, len_ref, keys_ref, lid_ref, mask_ref):
    host, z, y, core = pos_ref[0], pos_ref[1], pos_ref[2], pos_ref[3]
    table = pl.program_id(0)
    over_z = table < 2
    slot = lax.broadcasted_iota(jnp.int32, (8, LANES), 0)
    pick = lax.broadcasted_iota(jnp.int32, (len_ref.shape[0], LANES), 0)
    for n in range(BAG_BLOCKS):
        dest, hrel = n // 4, n % 4
        owner_host = (host + hrel) & 3
        row_dev = jnp.where(
            over_z,
            z * 8 + ((y + dest) & 3) * 2 + core,
            ((z + dest) & 3) * 8 + y * 2 + core,
        )
        start = pl.multiple_of((owner_host * 32 + row_dev) * LANES, LANES)
        v = idx_ref[0, :, pl.ds(start, LANES)]
        used = jnp.sum(
            jnp.where(pick == table, len_ref[:, pl.ds(start, LANES)], 0), axis=0, keepdims=True
        )
        at_z, at_y, at_core = v >> 13, (v >> 11) & 3, (v >> 10) & 1
        here = jnp.where(over_z, at_y - y, at_z - z) == 0
        away = jnp.where(over_z, at_z - z, at_y - y) & 3
        shard = jnp.where(away == 2, 4, 2 + (away >> 1))
        other = at_core ^ core
        shard = jnp.where(away == 0, other, shard + 3 * other)
        local = shard * ROWS_DEV + (v & (ROWS_DEV - 1))
        local = jnp.where(here & (slot < used), local, -1)
        for s in range(8):
            lid_ref[0, s, n : n + 1, :] = local[s : s + 1, :]
    for g in range(BAG_BLOCKS // 8):
        rows = pl.ds(g * 8, 8)
        lids = [lid_ref[0, s, rows, :] for s in range(8)]
        high = [x >> 8 for x in lids]
        low = [(x & (SUB - 1)).astype(jnp.float32) for x in lids]

        def one_block(blk, mask):
            at = [h == blk for h in high]
            up = [jnp.where(a, l, 511.0) for a, l in zip(at, low)]
            down = [jnp.where(a, l, -1.0) for a, l in zip(at, low)]
            first = functools.reduce(jnp.minimum, up)
            last = functools.reduce(jnp.maximum, down)
            n_first = sum(jnp.where(u == first, 1.0, 0.0) for u in up)
            n_last = sum(jnp.where(d == last, 1.0, 0.0) for d in down)
            total = sum(jnp.where(a, 1.0, 0.0) for a in at)
            more = (n_first + n_last) < total
            keys_ref[0, blk, 0, rows, :] = first
            keys_ref[0, blk, 1, rows, :] = n_first
            keys_ref[0, blk, 2, rows, :] = jnp.where(last == first, -1.0, last)
            keys_ref[0, blk, 3, rows, :] = n_last
            return mask | jnp.where(more, jnp.int32(1) << blk, 0)

        mask = lax.fori_loop(0, BLOCKS, one_block, jnp.zeros((8, LANES), jnp.int32))
        for shift in (64, 32, 16, 8, 4, 2, 1):
            mask = mask | pltpu.roll(mask, shift, 1)
        mask_ref[0, rows, :] = mask


def prep(pos, idx, lens):
    tables = idx.shape[0]
    return pl.pallas_call(
        prep_kernel,
        grid=(tables,),
        in_specs=[
            pl.BlockSpec(memory_space=pltpu.SMEM),
            pl.BlockSpec((1,) + idx.shape[1:], lambda j: (j, 0, 0)),
            pl.BlockSpec(lens.shape, lambda j: (0, 0)),
        ],
        out_specs=[
            pl.BlockSpec((1, BLOCKS, 4, BAG_BLOCKS, LANES), lambda j: (j, 0, 0, 0, 0)),
            pl.BlockSpec((1, 8, BAG_BLOCKS, LANES), lambda j: (j, 0, 0, 0)),
            pl.BlockSpec((1, BAG_BLOCKS, LANES), lambda j: (j, 0, 0)),
        ],
        out_shape=[
            jax.ShapeDtypeStruct((tables, BLOCKS, 4, BAG_BLOCKS, LANES), jnp.float32),
            jax.ShapeDtypeStruct((tables, 8, BAG_BLOCKS, LANES), jnp.int32),
            jax.ShapeDtypeStruct((tables, BAG_BLOCKS, LANES), jnp.int32),
        ],
        compiler_params=pltpu.CompilerParams(vmem_limit_bytes=24 << 20),
        cost_estimate=pl.CostEstimate(
            flops=40_000_000, bytes_accessed=9_000_000, transcendentals=0
        ),
        name="prep",
    )(pos, idx, lens)


def pool_kernel(layout, has_base, is_last, table0, *refs):
    n_pieces = len(layout)
    mask_ref, lid_ref = refs[:2]
    keys = refs[2 : 2 + n_pieces]
    tabs = refs[2 + n_pieces : 2 + 2 * n_pieces]
    refs = refs[2 + 2 * n_pieces :]
    if has_base:
        base_ref, refs = refs[0], refs[1:]
    if is_last:
        outs, (sums, counts, extra) = refs[:4], refs[4:]
    else:
        sums, counts, extra = refs
    table, step = pl.program_id(0), pl.program_id(1)
    first_block = layout[0][0]
    n_blocks = sum(n for _, n in layout)
    row_ids = [
        (lax.broadcasted_iota(jnp.int32, (16, PAIR), 0) + c * 16)
        .astype(jnp.float32)
        .astype(jnp.bfloat16)
        for c in range(SUB // 16)
    ]

    def wide(x):
        return jnp.broadcast_to(x, (16, LANES)).astype(jnp.bfloat16)

    for part in range(2):
        bag = 4 * step + 2 * part
        for (first, n), key in zip(layout, keys):
            for b in range(n):
                k1, m1, k2, m2 = (
                    jnp.concatenate(
                        [wide(key[0, 0, b, v, pl.ds(bag + half, 1), :]) for half in range(2)],
                        axis=1,
                    )
                    for v in range(4)
                )
                row = (first - first_block + b) * SUB
                for c in range(SUB // 16):
                    counts[part, row + c * 16 : row + (c + 1) * 16, :] = jnp.where(
                        k1 == row_ids[c], m1, jnp.where(k2 == row_ids[c], m2, jnp.bfloat16(0))
                    )
        total = base_ref[0, 0, part] if has_base else None
        for (first, n), tab in zip(layout, tabs):
            row = (first - first_block) * SUB
            product = jnp.dot(
                tab[0], counts[part, row : row + n * SUB, :], preferred_element_type=jnp.float32
            )
            total = product if total is None else total + product
        sums[0, 0, part] = total

    stage_bits = ((1 << n_blocks) - 1) << first_block
    stage_bits = stage_bits - (1 << 32) if stage_bits >= 1 << 31 else stage_bits
    for part in range(2):
        bag = 4 * step + 2 * part
        mask = mask_ref[table0 + table, bag, 0] | mask_ref[table0 + table, bag + 1, 0]

        @pl.when((mask & jnp.int32(stage_bits)) != 0)
        def _(part=part, bag=bag, mask=mask):
            def fix(at, carry):
                blk = first_block + at

                @pl.when(((mask >> blk) & 1) == 1)
                def _():
                    for half in range(2):
                        row = pl.ds(bag + half, 1)
                        lids = [lid_ref[0, s, row, :] for s in range(8)]
                        low = [
                            jnp.where((x >> 8) == blk, (x & (SUB - 1)).astype(jnp.float32), -1.0)
                            for x in lids
                        ]
                        last = functools.reduce(jnp.maximum, low)
                        first = functools.reduce(
                            jnp.minimum, [jnp.where(x < 0.0, 511.0, x) for x in low]
                        )
                        left = [
                            wide(jnp.where((x == first) | (x == last), -1.0, x)) for x in low
                        ]
                        for c in range(SUB // 16):
                            n = jnp.zeros((16, LANES), jnp.bfloat16)
                            for k in left:
                                n = n + jnp.where(
                                    k == row_ids[c][:, :LANES], jnp.bfloat16(1), jnp.bfloat16(0)
                                )
                            extra[c * 16 : (c + 1) * 16, half * LANES : (half + 1) * LANES] = n
                    for (first, n), tab in zip(layout, tabs):

                        @pl.when((blk >= first) & (blk < first + n))
                        def _(first=first, tab=tab):
                            columns = pl.ds(pl.multiple_of((blk - first) * SUB, SUB), SUB)
                            sums[0, 0, part] += jnp.dot(
                                tab[0, :, columns],
                                extra[...],
                                preferred_element_type=jnp.float32,
                            )

                return carry

            lax.fori_loop(0, n_blocks, fix, 0)

    if is_last:
        for d in range(4):

            @pl.when(step == d)
            def _(d=d):
                for part in range(2):
                    result = sums[0, 0, part].astype(jnp.bfloat16)
                    outs[d][2 * part, 0] = result[:, :LANES]
                    outs[d][2 * part + 1, 0] = result[:, LANES:]


def pool(tables, masks, keys, lids, pieces, base, is_last, name):
    n_tables = len(tables)
    table0 = tables[0]
    emb = pieces[0][0].shape[1]
    sums_block = (1, 1, 2, emb, PAIR)
    sums_spec = pl.BlockSpec(sums_block, lambda j, i: (j, i, 0, 0, 0))
    layout, key_specs, tab_specs = [], [], []
    for array, start_table, shard, start in pieces:
        n = array.shape[2] // SUB
        layout.append(((shard * ROWS_DEV + start) // SUB, n))
        key_specs.append(
            pl.BlockSpec(
                (1, 1, n) + keys.shape[3:],
                lambda j, i, shard=shard, at=start // SUB // n: (table0 + j, shard, at, 0, 0, 0),
            )
        )
        tab_specs.append(
            pl.BlockSpec(
                (1,) + array.shape[1:], lambda j, i, skip=table0 - start_table: (skip + j, 0, 0)
            )
        )
    rows = sum(n for _, n in layout) * SUB
    in_specs = [
        pl.BlockSpec(memory_space=pltpu.SMEM),
        pl.BlockSpec((1,) + lids.shape[1:], lambda j, i: (table0 + j, 0, 0, 0)),
        *key_specs,
        *tab_specs,
    ]
    args = [masks, lids] + [keys] * len(pieces) + [p[0] for p in pieces]
    if base is not None:
        array, start_table = base
        in_specs.append(
            pl.BlockSpec(sums_block, lambda j, i: (table0 - start_table + j, i, 0, 0, 0))
        )
        args.append(array)
    scratch = [
        pltpu.VMEM((2, rows, PAIR), jnp.bfloat16),
        pltpu.VMEM((SUB, PAIR), jnp.bfloat16),
    ]
    if is_last:
        out_specs = [pl.BlockSpec((4, 1, emb, LANES), lambda j, i: (0, j, 0, 0))] * 4
        out_shape = [jax.ShapeDtypeStruct((4, n_tables, emb, LANES), jnp.bfloat16)] * 4
        scratch = [pltpu.VMEM(sums_block, jnp.float32)] + scratch
    else:
        out_specs = sums_spec
        out_shape = jax.ShapeDtypeStruct((n_tables, 4, 2, emb, PAIR), jnp.float32)
    return pl.pallas_call(
        functools.partial(pool_kernel, tuple(layout), base is not None, is_last, table0),
        grid=(n_tables, 4),
        in_specs=in_specs,
        out_specs=out_specs,
        out_shape=out_shape,
        scratch_shapes=scratch,
        compiler_params=pltpu.CompilerParams(vmem_limit_bytes=24 << 20),
        cost_estimate=pl.CostEstimate(
            flops=2 * n_tables * rows * 2048 * 256,
            bytes_accessed=5_000_000,
            transcendentals=0,
        ),
        name=name,
    )(*args)


def tail_kernel(
    host_ref,
    order_ref,
    compress_ref,
    *rest,
):
    parts = rest[:8]
    proj_ref, fm_gain_ref, up_ref, down_ref, gain_ref, out_ref, emb, gram, summed = rest[8:]
    host = host_ref[0]
    for d in range(4):
        source = (host - d) & 3
        for j in range(4):
            at = order_ref[source * 4 + j]
            part = parts[(j // 2) * 4 + d]
            emb[at] = part[j % 2].astype(jnp.float32)
    feats, width, lanes = emb.shape
    rank = proj_ref.shape[0]

    for f in range(feats):
        x = emb[f]
        for g in range(f + 1):
            dot = jnp.sum(x * emb[g], axis=0, keepdims=True)
            gram[f, g : g + 1, :] = dot
            if g != f:
                gram[g, f : f + 1, :] = dot
    proj = [jnp.broadcast_to(proj_ref[:, g : g + 1], (rank, lanes)) for g in range(feats)]
    rows = []
    for f in range(feats):
        row = None
        for g in range(feats):
            term = proj[g] * gram[f, g : g + 1, :]
            row = term if row is None else row + term
        rows.append(row)
    inv = 1.0 / (rank * feats)
    mean = jnp.sum(sum(rows), axis=0, keepdims=True) * inv
    rows = [r - mean for r in rows]
    spread = jnp.sum(sum(r * r for r in rows), axis=0, keepdims=True) * inv
    scale = 1.0 / jnp.sqrt(spread + 1e-05)
    normed = jnp.concatenate(
        [rows[f] * scale * fm_gain_ref[:, f : f + 1] for f in range(feats)], axis=0
    )
    hidden = jnp.maximum(
        jnp.dot(normed.T.astype(jnp.bfloat16), up_ref[...], preferred_element_type=jnp.float32),
        0.0,
    ).astype(jnp.bfloat16)
    fm_block = jnp.dot(hidden, down_ref[...], preferred_element_type=jnp.float32).T
    half = feats // 2
    for m in range(half):
        summed[m] = fm_block[m * width : (m + 1) * width, :] + emb[m]
        acc = emb[half + m]
        for f in range(feats):
            acc = acc + compress_ref[m, f] * emb[f]
        summed[half + m] = acc
    inv = 1.0 / (feats * width)
    total = summed[0]
    for f in range(1, feats):
        total = total + summed[f]
    mean = jnp.sum(total, axis=0, keepdims=True) * inv
    square = None
    for f in range(feats):
        c = summed[f] - mean
        square = c * c if square is None else square + c * c
    spread = jnp.sum(square, axis=0, keepdims=True) * inv
    scale = 1.0 / jnp.sqrt(spread + 1e-05)
    for f in range(feats):
        out_ref[f] = ((summed[f] - mean) * scale * gain_ref[:, f : f + 1]).astype(jnp.bfloat16)


def tail(host, order, proj, compress, parts, fm_gain, up, down, gain):
    feats, width = order.shape[0], parts[0].shape[2]
    smem = pl.BlockSpec(memory_space=pltpu.SMEM)
    vmem = pl.BlockSpec(memory_space=pltpu.VMEM)
    mine = pl.BlockSpec((None,) + parts[0].shape[1:], lambda i: (0, 0, 0, 0))
    there = pl.BlockSpec(parts[1].shape, lambda i: (0, 0, 0))
    return pl.pallas_call(
        tail_kernel,
        grid=(1,),
        in_specs=[smem] * 3 + ([mine] + [there] * 3) * 2 + [vmem] * 5,
        out_specs=vmem,
        out_shape=jax.ShapeDtypeStruct((feats, width, LANES), jnp.bfloat16),
        scratch_shapes=[
            pltpu.VMEM((feats, width, LANES), jnp.float32),
            pltpu.VMEM((feats, feats, LANES), jnp.float32),
            pltpu.VMEM((feats, width, LANES), jnp.float32),
        ],
        compiler_params=pltpu.CompilerParams(vmem_limit_bytes=32 << 20),
        cost_estimate=pl.CostEstimate(
            flops=1_000_000_000, bytes_accessed=8_000_000, transcendentals=0
        ),
        name="tail",
    )(host, order, compress, *parts, proj, fm_gain, up, down, gain)


def row_moves(axis, step):
    pairs = []
    for z in range(4):
        for y in range(4):
            for core in range(2):
                to = {
                    "z": (((z + step) % 4) * 8 + y * 2 + core),
                    "y": (z * 8 + ((y + step) % 4) * 2 + core),
                    "core": (z * 8 + y * 2 + (core + step) % 2),
                }[axis]
                pairs.append((z * 8 + y * 2 + core, to))
    return pairs


def other_core(x):
    return lax.ppermute(x, "row", row_moves("core", 1))


def to_owners(blocks, axis):
    return [blocks[0]] + [
        lax.ppermute(blocks[d], "row", row_moves(axis, d)) for d in range(1, 4)
    ]


def add_up(blocks):
    return sum(b.astype(jnp.float32) for b in blocks).astype(jnp.bfloat16)


def to_hosts(total):
    return [total] + [
        lax.ppermute(total[d], "hst", [(h, (h + d) % 4) for h in range(4)]) for d in range(1, 4)
    ]


def on_device(
    tables,
    indices,
    lengths,
    feature_order,
    proj_weight,
    fm_gain,
    up_weight,
    down_weight,
    compress_weight,
    out_gain,
):
    host = lax.axis_index("hst")
    row = lax.axis_index("row")
    pos = jnp.stack([host, row // 8, (row // 2) % 4, row % 2]).astype(jnp.int32)
    feats = out_gain.shape[0]
    rank = proj_weight.shape[0]

    flipped = jnp.swapaxes(tables, 1, 2)
    keys, lids, masks = prep(pos, jnp.transpose(indices, (1, 2, 0)), lengths.T)
    small = (
        feature_order,
        proj_weight.astype(jnp.float32),
        compress_weight.astype(jnp.float32),
        fm_gain.reshape(feats, rank).T,
        out_gain.T,
    )
    masks, up, down, small = lax.optimization_barrier(
        (masks, up_weight, down_weight, small)
    )
    order, proj, compress, fm_gain, gain = small

    keys = keys.reshape((keys.shape[0], GATHER, ROWS_DEV // SUB) + keys.shape[2:])
    pairs = [(0, 1), (2, 3)]
    axes = ["z", "y"]

    def move(x, axis, step):
        return lax.ppermute(x, "row", row_moves(axis, step))

    mine = [flipped[2 * p : 2 * p + 2] for p in range(2)]
    sides = [[move(mine[p], axes[p], 3), move(mine[p], axes[p], 1)] for p in range(2)]
    own_far = other_core(flipped)
    sides, mine, masks = lax.optimization_barrier((sides, mine, masks))
    beyond = [move(mine[p], axes[p], 2) for p in range(2)]

    def stage(p, arrays, shard):
        return [(x, pairs[p][0], shard + k, 0) for k, x in enumerate(arrays)]

    sums = pool(
        (0, 1, 2, 3),
        masks,
        keys,
        lids,
        [(flipped, 0, 0, 0), (own_far, 0, 1, 0)],
        None,
        False,
        "pool_own",
    )
    early = [other_core(x) for x in (sides[0][0], sides[0][1], sides[1][0])]
    sums, sides, beyond, early, masks = lax.optimization_barrier(
        (sums, sides, beyond, early, masks)
    )
    near = [sides[p] + [beyond[p]] for p in range(2)]
    late = [other_core(x) for x in (beyond[0], sides[1][1], beyond[1])]

    def pool_pair(p, base, masks):
        near_sums = pool(
            pairs[p], masks, keys, lids, stage(p, near[p], 2), base, False, "pool_near"
        )
        masks, _ = lax.optimization_barrier((masks, near_sums))
        return near_sums, masks

    near_sums, masks = pool_pair(0, (sums, 0), masks)
    late, masks = lax.optimization_barrier((late, masks))
    far = [[early[0], early[1], late[0]], [early[2], late[1], late[2]]]
    blocks = pool(
        pairs[0], masks, keys, lids, stage(0, far[0], 5), (near_sums, 0), True, "pool_far"
    )
    masks, _ = lax.optimization_barrier((masks, blocks))
    arrived = to_owners(blocks, axes[1])
    near_sums, masks = pool_pair(1, (sums, 0), masks)
    arrived, masks = lax.optimization_barrier((arrived, masks))
    total = add_up(arrived)
    total, masks = lax.optimization_barrier((total, masks))
    parts = to_hosts(total)
    blocks = pool(
        pairs[1], masks, keys, lids, stage(1, far[1], 5), (near_sums, 2), True, "pool_far"
    )
    blocks, parts = lax.optimization_barrier((blocks, parts))
    parts += to_hosts(add_up(to_owners(blocks, axes[0])))
    result = tail(pos[:1], order, proj, compress, parts, fm_gain, up, down, gain)
    return jnp.transpose(result, (2, 0, 1))


def solution(mesh):
    in_specs = (
        P("hst", "row", None),
        P(None, "hst", None),
        P(None, "hst"),
        P(),
        P(),
        P(),
        P(),
        P(),
        P(),
        P(),
    )
    out_specs = P(("hst", "row"), None, None)
    return jax.shard_map(
        on_device, mesh=mesh, in_specs=in_specs, out_specs=out_specs, check_vma=False
    )
```

```python
import functools

import jax
import jax.numpy as jnp
from jax import lax
from jax.experimental import pallas as pl
from jax.experimental.pallas import tpu as pltpu
from jax.sharding import Mesh
from jax.sharding import PartitionSpec as P

LANES = 128
ROWS_DEV = 1024
SUB = 256
GATHER = 8
BLOCKS = GATHER * ROWS_DEV // SUB
BAG_BLOCKS = 16
PAIR = 2 * LANES


def prep_kernel(pos_ref, idx_ref, len_ref, keys_ref, lid_ref, mask_ref):
    host, z, y, core = pos_ref[0], pos_ref[1], pos_ref[2], pos_ref[3]
    table = pl.program_id(0)
    over_z = table < 2
    slot = lax.broadcasted_iota(jnp.int32, (8, LANES), 0)
    pick = lax.broadcasted_iota(jnp.int32, (len_ref.shape[0], LANES), 0)
    for n in range(BAG_BLOCKS):
        high_part, low_part = n // 4, n % 4
        owner_host = jnp.where(over_z, (host + low_part) & 3, high_part)
        row_dev = jnp.where(
            over_z,
            z * 8 + ((y + high_part) & 3) * 2 + core,
            low_part * 8 + y * 2 + core,
        )
        start = pl.multiple_of((owner_host * 32 + row_dev) * LANES, LANES)
        v = idx_ref[0, :, pl.ds(start, LANES)]
        used = jnp.sum(
            jnp.where(pick == table, len_ref[:, pl.ds(start, LANES)], 0), axis=0, keepdims=True
        )
        at_z, at_y, at_core = v >> 13, (v >> 11) & 3, (v >> 10) & 1
        here = jnp.where(over_z, at_y - y, at_z - z) == 0
        away = jnp.where(over_z, at_z - z, at_y - y) & 3
        shard = jnp.where(away == 2, 4, 2 + (away >> 1))
        other = at_core ^ core
        shard = jnp.where(away == 0, other, shard + 3 * other)
        local = shard * ROWS_DEV + (v & (ROWS_DEV - 1))
        local = jnp.where(here & (slot < used), local, -1)
        for s in range(8):
            lid_ref[0, s, n : n + 1, :] = local[s : s + 1, :]
    for g in range(BAG_BLOCKS // 8):
        rows = pl.ds(g * 8, 8)
        lids = [lid_ref[0, s, rows, :] for s in range(8)]
        high = [x >> 8 for x in lids]
        low = [(x & (SUB - 1)).astype(jnp.float32) for x in lids]

        def one_block(blk, mask):
            at = [h == blk for h in high]
            up = [jnp.where(a, l, 511.0) for a, l in zip(at, low)]
            down = [jnp.where(a, l, -1.0) for a, l in zip(at, low)]
            first = functools.reduce(jnp.minimum, up)
            last = functools.reduce(jnp.maximum, down)
            n_first = sum(jnp.where(u == first, 1.0, 0.0) for u in up)
            n_last = sum(jnp.where(d == last, 1.0, 0.0) for d in down)
            total = sum(jnp.where(a, 1.0, 0.0) for a in at)
            more = (n_first + n_last) < total
            keys_ref[0, blk, 0, rows, :] = first
            keys_ref[0, blk, 1, rows, :] = n_first
            keys_ref[0, blk, 2, rows, :] = jnp.where(last == first, -1.0, last)
            keys_ref[0, blk, 3, rows, :] = n_last
            return mask | jnp.where(more, jnp.int32(1) << blk, 0)

        mask = lax.fori_loop(0, BLOCKS, one_block, jnp.zeros((8, LANES), jnp.int32))
        mask_ref[table, rows, :] = mask

    @pl.when(table == pl.num_programs(0) - 1)
    def _():
        masks = mask_ref[...]
        for shift in (64, 32, 16, 8, 4, 2, 1):
            masks = masks | pltpu.roll(masks, shift, 2)
        mask_ref[...] = masks


def prep(pos, idx, lens):
    tables = idx.shape[0]
    return pl.pallas_call(
        prep_kernel,
        grid=(tables,),
        in_specs=[
            pl.BlockSpec(memory_space=pltpu.SMEM),
            pl.BlockSpec((1,) + idx.shape[1:], lambda j: (j, 0, 0)),
            pl.BlockSpec(lens.shape, lambda j: (0, 0)),
        ],
        out_specs=[
            pl.BlockSpec((1, BLOCKS, 4, BAG_BLOCKS, LANES), lambda j: (j, 0, 0, 0, 0)),
            pl.BlockSpec((1, 8, BAG_BLOCKS, LANES), lambda j: (j, 0, 0, 0)),
            pl.BlockSpec((tables, BAG_BLOCKS, LANES), lambda j: (0, 0, 0)),
        ],
        out_shape=[
            jax.ShapeDtypeStruct((tables, BLOCKS, 4, BAG_BLOCKS, LANES), jnp.float32),
            jax.ShapeDtypeStruct((tables, 8, BAG_BLOCKS, LANES), jnp.int32),
            jax.ShapeDtypeStruct((tables, BAG_BLOCKS, LANES), jnp.int32),
        ],
        compiler_params=pltpu.CompilerParams(vmem_limit_bytes=24 << 20),
        cost_estimate=pl.CostEstimate(
            flops=40_000_000, bytes_accessed=9_000_000, transcendentals=0
        ),
        name="prep",
    )(pos, idx, lens)


def pool_kernel(layout, has_base, n_outs, table0, *refs):
    n_pieces = len(layout)
    mask_ref, lid_ref = refs[:2]
    keys = refs[2 : 2 + n_pieces]
    tabs = refs[2 + n_pieces : 2 + 2 * n_pieces]
    refs = refs[2 + 2 * n_pieces :]
    if has_base:
        base_ref, refs = refs[0], refs[1:]
    if n_outs:
        outs, (sums, counts, extra) = refs[:n_outs], refs[n_outs:]
    else:
        sums, counts, extra = refs
    table, step = pl.program_id(0), pl.program_id(1)
    first_block = layout[0][0]
    n_blocks = sum(n for _, n in layout)
    row_ids = [
        (lax.broadcasted_iota(jnp.int32, (16, PAIR), 0) + c * 16)
        .astype(jnp.float32)
        .astype(jnp.bfloat16)
        for c in range(SUB // 16)
    ]

    def wide(x):
        return jnp.broadcast_to(x, (16, LANES)).astype(jnp.bfloat16)

    for part in range(2):
        bag = 4 * step + 2 * part
        for (first, n), key in zip(layout, keys):
            for b in range(n):
                k1, m1, k2, m2 = (
                    jnp.concatenate(
                        [wide(key[0, 0, b, v, pl.ds(bag + half, 1), :]) for half in range(2)],
                        axis=1,
                    )
                    for v in range(4)
                )
                row = (first - first_block + b) * SUB
                for c in range(SUB // 16):
                    counts[part, row + c * 16 : row + (c + 1) * 16, :] = jnp.where(
                        k1 == row_ids[c], m1, jnp.where(k2 == row_ids[c], m2, jnp.bfloat16(0))
                    )
        total = base_ref[0, 0, part] if has_base else None
        for (first, n), tab in zip(layout, tabs):
            row = (first - first_block) * SUB
            product = jnp.dot(
                tab[0], counts[part, row : row + n * SUB, :], preferred_element_type=jnp.float32
            )
            total = product if total is None else total + product
        sums[0, 0, part] = total

    stage_bits = ((1 << n_blocks) - 1) << first_block
    stage_bits = stage_bits - (1 << 32) if stage_bits >= 1 << 31 else stage_bits
    for part in range(2):
        bag = 4 * step + 2 * part
        mask = mask_ref[table0 + table, bag, 0] | mask_ref[table0 + table, bag + 1, 0]

        @pl.when((mask & jnp.int32(stage_bits)) != 0)
        def _(part=part, bag=bag, mask=mask):
            def fix(at, carry):
                blk = first_block + at

                @pl.when(((mask >> blk) & 1) == 1)
                def _():
                    for half in range(2):
                        row = pl.ds(bag + half, 1)
                        lids = [lid_ref[0, s, row, :] for s in range(8)]
                        low = [
                            jnp.where((x >> 8) == blk, (x & (SUB - 1)).astype(jnp.float32), -1.0)
                            for x in lids
                        ]
                        last = functools.reduce(jnp.maximum, low)
                        first = functools.reduce(
                            jnp.minimum, [jnp.where(x < 0.0, 511.0, x) for x in low]
                        )
                        left = [
                            wide(jnp.where((x == first) | (x == last), -1.0, x)) for x in low
                        ]
                        for c in range(SUB // 16):
                            n = jnp.zeros((16, LANES), jnp.bfloat16)
                            for k in left:
                                n = n + jnp.where(
                                    k == row_ids[c][:, :LANES], jnp.bfloat16(1), jnp.bfloat16(0)
                                )
                            extra[c * 16 : (c + 1) * 16, half * LANES : (half + 1) * LANES] = n
                    for (first, n), tab in zip(layout, tabs):

                        @pl.when((blk >= first) & (blk < first + n))
                        def _(first=first, tab=tab):
                            columns = pl.ds(pl.multiple_of((blk - first) * SUB, SUB), SUB)
                            sums[0, 0, part] += jnp.dot(
                                tab[0, :, columns],
                                extra[...],
                                preferred_element_type=jnp.float32,
                            )

                return carry

            lax.fori_loop(0, n_blocks, fix, 0)

    def finish(out):
        for part in range(2):
            result = sums[0, 0, part].astype(jnp.bfloat16)
            out[2 * part, 0] = result[:, :LANES]
            out[2 * part + 1, 0] = result[:, LANES:]

    if n_outs == 1:
        finish(outs[0])
    for d in range(n_outs if n_outs > 1 else 0):

        @pl.when(step == d)
        def _(d=d):
            finish(outs[d])


def pool(tables, masks, keys, lids, pieces, base, n_outs, name):
    n_tables = len(tables)
    table0 = tables[0]
    emb = pieces[0][0].shape[1]
    sums_block = (1, 1, 2, emb, PAIR)
    sums_spec = pl.BlockSpec(sums_block, lambda j, i: (j, i, 0, 0, 0))
    layout, key_specs, tab_specs = [], [], []
    for array, start_table, shard, start in pieces:
        n = array.shape[2] // SUB
        layout.append(((shard * ROWS_DEV + start) // SUB, n))
        key_specs.append(
            pl.BlockSpec(
                (1, 1, n) + keys.shape[3:],
                lambda j, i, shard=shard, at=start // SUB // n: (table0 + j, shard, at, 0, 0, 0),
            )
        )
        tab_specs.append(
            pl.BlockSpec(
                (1,) + array.shape[1:], lambda j, i, skip=table0 - start_table: (skip + j, 0, 0)
            )
        )
    rows = sum(n for _, n in layout) * SUB
    in_specs = [
        pl.BlockSpec(memory_space=pltpu.SMEM),
        pl.BlockSpec((1,) + lids.shape[1:], lambda j, i: (table0 + j, 0, 0, 0)),
        *key_specs,
        *tab_specs,
    ]
    args = [masks, lids] + [keys] * len(pieces) + [p[0] for p in pieces]
    if base is not None:
        array, start_table = base
        in_specs.append(
            pl.BlockSpec(sums_block, lambda j, i: (table0 - start_table + j, i, 0, 0, 0))
        )
        args.append(array)
    scratch = [
        pltpu.VMEM((2, rows, PAIR), jnp.bfloat16),
        pltpu.VMEM((SUB, PAIR), jnp.bfloat16),
    ]
    if n_outs:
        places = BAG_BLOCKS // n_outs
        out_specs = [
            pl.BlockSpec((4, 1, emb, LANES), lambda j, i: (i if n_outs == 1 else 0, j, 0, 0))
        ] * n_outs
        out_shape = [
            jax.ShapeDtypeStruct((places, n_tables, emb, LANES), jnp.bfloat16)
        ] * n_outs
        scratch = [pltpu.VMEM(sums_block, jnp.float32)] + scratch
    else:
        out_specs = sums_spec
        out_shape = jax.ShapeDtypeStruct((n_tables, 4, 2, emb, PAIR), jnp.float32)
    return pl.pallas_call(
        functools.partial(pool_kernel, tuple(layout), base is not None, n_outs, table0),
        grid=(n_tables, 4),
        in_specs=in_specs,
        out_specs=out_specs,
        out_shape=out_shape,
        scratch_shapes=scratch,
        compiler_params=pltpu.CompilerParams(vmem_limit_bytes=24 << 20),
        cost_estimate=pl.CostEstimate(
            flops=2 * n_tables * rows * 2048 * 256,
            bytes_accessed=5_000_000,
            transcendentals=0,
        ),
        name=name,
    )(*args)


def tail_kernel(host_ref, order_ref, *rest):
    parts, summed_here = rest[:4], rest[4]
    proj_ref, fm_gain_ref, up_ref, down_ref, compress_ref, gain_ref, out_ref = rest[5:12]
    emb, gram, summed = rest[12:]
    host = host_ref[0]
    for d in range(4):
        source = (host - d) & 3
        for j in range(2):
            emb[order_ref[source * 4 + j]] = parts[d][j].astype(jnp.float32)
            total = summed_here[4 * d, j].astype(jnp.float32)
            for k in range(1, 4):
                total = total + summed_here[4 * d + k, j].astype(jnp.float32)
            emb[order_ref[d * 4 + 2 + j]] = total.astype(jnp.bfloat16).astype(jnp.float32)
    feats, width, lanes = emb.shape
    rank = proj_ref.shape[1]
    proj_weight = proj_ref[...].astype(jnp.float32).T
    fm_gain = fm_gain_ref[...].T
    compress = compress_ref[...].astype(jnp.float32)
    gain = gain_ref[...].T

    for f in range(feats):
        x = emb[f]
        for g in range(f + 1):
            dot = jnp.sum(x * emb[g], axis=0, keepdims=True)
            gram[f, g : g + 1, :] = dot
            if g != f:
                gram[g, f : f + 1, :] = dot
    proj = [jnp.broadcast_to(proj_weight[:, g : g + 1], (rank, lanes)) for g in range(feats)]
    rows = []
    for f in range(feats):
        row = None
        for g in range(feats):
            term = proj[g] * gram[f, g : g + 1, :]
            row = term if row is None else row + term
        rows.append(row)
    inv = 1.0 / (rank * feats)
    mean = jnp.sum(sum(rows), axis=0, keepdims=True) * inv
    rows = [r - mean for r in rows]
    spread = jnp.sum(sum(r * r for r in rows), axis=0, keepdims=True) * inv
    scale = 1.0 / jnp.sqrt(spread + 1e-05)
    normed = jnp.concatenate([r * scale for r in rows], axis=0)
    normed = jnp.concatenate(
        [
            normed[c * lanes : (c + 1) * lanes] * fm_gain[:, c : c + 1]
            for c in range(rank * feats // lanes)
        ],
        axis=0,
    )
    hidden = jnp.maximum(
        jnp.dot(normed.T.astype(jnp.bfloat16), up_ref[...], preferred_element_type=jnp.float32),
        0.0,
    ).astype(jnp.bfloat16)
    fm_block = jnp.dot(hidden, down_ref[...], preferred_element_type=jnp.float32).T
    half = feats // 2
    for m in range(half):
        summed[m] = fm_block[m * width : (m + 1) * width, :] + emb[m]
        acc = emb[half + m]
        for f in range(feats):
            acc = acc + compress[m : m + 1, f : f + 1] * emb[f]
        summed[half + m] = acc
    inv = 1.0 / (feats * width)
    total = summed[0]
    for f in range(1, feats):
        total = total + summed[f]
    mean = jnp.sum(total, axis=0, keepdims=True) * inv
    square = None
    for f in range(feats):
        c = summed[f] - mean
        square = c * c if square is None else square + c * c
    spread = jnp.sum(square, axis=0, keepdims=True) * inv
    scale = 1.0 / jnp.sqrt(spread + 1e-05)
    for f in range(feats):
        out_ref[f] = ((summed[f] - mean) * scale * gain[:, f : f + 1]).astype(jnp.bfloat16)


def tail(host, order, parts, *weights):
    feats, width = order.shape[0], parts[0].shape[2]
    smem = pl.BlockSpec(memory_space=pltpu.SMEM)
    vmem = pl.BlockSpec(memory_space=pltpu.VMEM)
    mine = pl.BlockSpec((None,) + parts[0].shape[1:], lambda i: (0, 0, 0, 0))
    there = pl.BlockSpec(parts[1].shape, lambda i: (0, 0, 0))
    return pl.pallas_call(
        tail_kernel,
        grid=(1,),
        in_specs=[smem] * 2 + [mine] + [there] * 3 + [vmem] * 7,
        out_specs=vmem,
        out_shape=jax.ShapeDtypeStruct((feats, width, LANES), jnp.bfloat16),
        scratch_shapes=[
            pltpu.VMEM((feats, width, LANES), jnp.float32),
            pltpu.VMEM((feats, feats, LANES), jnp.float32),
            pltpu.VMEM((feats, width, LANES), jnp.float32),
        ],
        compiler_params=pltpu.CompilerParams(vmem_limit_bytes=32 << 20),
        cost_estimate=pl.CostEstimate(
            flops=1_000_000_000, bytes_accessed=8_000_000, transcendentals=0
        ),
        name="tail",
    )(host, order, *parts, *weights)


def move(x, axis, step):
    size = 2 if axis == "core" else 4
    return lax.ppermute(x, axis, [(i, (i + step) % size) for i in range(size)])


def other_core(x):
    return move(x, "core", 1)


def to_owners(blocks, axis):
    return [blocks[0]] + [move(blocks[d], axis, d) for d in range(1, 4)]


def add_up(blocks):
    return sum(b.astype(jnp.float32) for b in blocks).astype(jnp.bfloat16)


def to_hosts(total):
    return [total] + [move(total[d], "hst", d) for d in range(1, 4)]


def on_device(
    tables,
    indices,
    lengths,
    feature_order,
    proj_weight,
    fm_gain,
    up_weight,
    down_weight,
    compress_weight,
    out_gain,
):
    pos = jnp.stack([lax.axis_index(a) for a in ("hst", "z", "y", "core")]).astype(jnp.int32)

    flipped = jnp.swapaxes(tables, 1, 2)
    keys, lids, masks = prep(pos, jnp.transpose(indices, (1, 2, 0)), lengths.T)
    keys = keys.reshape((keys.shape[0], GATHER, ROWS_DEV // SUB) + keys.shape[2:])
    pairs = [(0, 1), (2, 3)]
    axes = ["z", "y"]

    mine = [flipped[2 * p : 2 * p + 2] for p in range(2)]
    sides = [[move(mine[p], axes[p], 3), move(mine[p], axes[p], 1)] for p in range(2)]
    own_far = other_core(flipped)
    sides, mine, masks = lax.optimization_barrier((sides, mine, masks))
    beyond = [move(mine[p], axes[p], 2) for p in range(2)]

    def stage(p, arrays, shard):
        return [(x, pairs[p][0], shard + k, 0) for k, x in enumerate(arrays)]

    sums = pool(
        (0, 1, 2, 3),
        masks,
        keys,
        lids,
        [(flipped, 0, 0, 0), (own_far, 0, 1, 0)],
        None,
        0,
        "pool_own",
    )
    early = [other_core(x) for x in (sides[0][0], sides[0][1], sides[1][0])]
    sums, sides, beyond, early, masks = lax.optimization_barrier(
        (sums, sides, beyond, early, masks)
    )
    near = [sides[p] + [beyond[p]] for p in range(2)]
    late = [other_core(x) for x in (beyond[0], sides[1][1], beyond[1])]

    def pool_pair(p, base, masks):
        near_sums = pool(
            pairs[p], masks, keys, lids, stage(p, near[p], 2), base, 0, "pool_near"
        )
        masks, _ = lax.optimization_barrier((masks, near_sums))
        return near_sums, masks

    near_sums, masks = pool_pair(0, (sums, 0), masks)
    late, masks = lax.optimization_barrier((late, masks))
    far = [[early[0], early[1], late[0]], [early[2], late[1], late[2]]]
    blocks = pool(
        pairs[0], masks, keys, lids, stage(0, far[0], 5), (near_sums, 0), 4, "pool_far"
    )
    masks, _ = lax.optimization_barrier((masks, blocks))
    arrived = to_owners(blocks, axes[1])
    near_sums, masks = pool_pair(1, (sums, 0), masks)
    (blocks,) = pool(
        pairs[1], masks, keys, lids, stage(1, far[1], 5), (near_sums, 2), 1, "pool_far"
    )
    arrived, blocks = lax.optimization_barrier((arrived, blocks))
    total, blocks = lax.optimization_barrier((add_up(arrived), blocks))
    parts = to_hosts(total)
    parts.append(lax.all_to_all(blocks, ("hst", axes[0]), 0, 0, tiled=True))
    result = tail(
        pos[:1],
        feature_order,
        parts,
        proj_weight.T,
        fm_gain.reshape(-1, LANES),
        up_weight,
        down_weight,
        compress_weight,
        out_gain,
    )
    return jnp.transpose(result, (2, 0, 1))


def solution(mesh):
    fine = Mesh(mesh.devices.reshape(4, 4, 4, 2), ("hst", "z", "y", "core"))
    row = ("z", "y", "core")
    in_specs = (
        P("hst", row, None),
        P(None, "hst", None),
        P(None, "hst"),
        P(),
        P(),
        P(),
        P(),
        P(),
        P(),
        P(),
    )
    out_specs = P(("hst",) + row, None, None)
    return jax.shard_map(
        on_device, mesh=fine, in_specs=in_specs, out_specs=out_specs, check_vma=False
    )
```

```python
import functools

import jax
import jax.numpy as jnp
from jax import lax
from jax.experimental import pallas as pl
from jax.experimental.pallas import tpu as pltpu
from jax.sharding import Mesh
from jax.sharding import PartitionSpec as P

LANES = 128
ROWS_DEV = 1024
SUB = 256
GATHER = 8
BLOCKS = GATHER * ROWS_DEV // SUB
BAG_BLOCKS = 16
PAIR = 2 * LANES


def prep_kernel(pos_ref, idx_ref, len_ref, keys_ref, lid_ref, mask_ref):
    host, z, y, core = pos_ref[0], pos_ref[1], pos_ref[2], pos_ref[3]
    table = pl.program_id(0)
    over_z = table < 2
    slot = lax.broadcasted_iota(jnp.int32, (8, LANES), 0)
    pick = lax.broadcasted_iota(jnp.int32, (len_ref.shape[0], LANES), 0)
    for n in range(BAG_BLOCKS):
        high_part, low_part = n // 4, n % 4
        owner_host = jnp.where(over_z, (host + low_part) & 3, high_part)
        row_dev = jnp.where(
            over_z,
            z * 8 + ((y + high_part) & 3) * 2 + core,
            low_part * 8 + y * 2 + core,
        )
        start = pl.multiple_of((owner_host * 32 + row_dev) * LANES, LANES)
        v = idx_ref[0, :, pl.ds(start, LANES)]
        used = jnp.sum(
            jnp.where(pick == table, len_ref[:, pl.ds(start, LANES)], 0), axis=0, keepdims=True
        )
        at_z, at_y, at_core = v >> 13, (v >> 11) & 3, (v >> 10) & 1
        here = jnp.where(over_z, at_y - y, at_z - z) == 0
        away = jnp.where(over_z, at_z - z, at_y - y) & 3
        other = at_core ^ core
        shard = jnp.where(away == 2, 6 + other, 2 + (away >> 1) + 2 * other)
        shard = jnp.where(away == 0, other, shard)
        local = shard * ROWS_DEV + (v & (ROWS_DEV - 1))
        local = jnp.where(here & (slot < used), local, -1)
        for s in range(8):
            lid_ref[0, s, n : n + 1, :] = local[s : s + 1, :]
    for g in range(BAG_BLOCKS // 8):
        rows = pl.ds(g * 8, 8)
        lids = [lid_ref[0, s, rows, :] for s in range(8)]
        high = [x >> 8 for x in lids]
        low = [(x & (SUB - 1)).astype(jnp.float32) for x in lids]

        def one_block(blk, mask):
            at = [h == blk for h in high]
            up = [jnp.where(a, l, 511.0) for a, l in zip(at, low)]
            down = [jnp.where(a, l, -1.0) for a, l in zip(at, low)]
            first = functools.reduce(jnp.minimum, up)
            last = functools.reduce(jnp.maximum, down)
            n_first = sum(jnp.where(u == first, 1.0, 0.0) for u in up)
            n_last = sum(jnp.where(d == last, 1.0, 0.0) for d in down)
            total = sum(jnp.where(a, 1.0, 0.0) for a in at)
            more = (n_first + n_last) < total
            keys_ref[0, blk, 0, rows, :] = first
            keys_ref[0, blk, 1, rows, :] = n_first
            keys_ref[0, blk, 2, rows, :] = jnp.where(last == first, -1.0, last)
            keys_ref[0, blk, 3, rows, :] = n_last
            return mask | jnp.where(more, jnp.int32(1) << blk, 0)

        mask = lax.fori_loop(0, BLOCKS, one_block, jnp.zeros((8, LANES), jnp.int32))
        mask_ref[table, rows, :] = mask

    @pl.when(table == pl.num_programs(0) - 1)
    def _():
        masks = mask_ref[...]
        for shift in (64, 32, 16, 8, 4, 2, 1):
            masks = masks | pltpu.roll(masks, shift, 2)
        mask_ref[...] = masks


def prep(pos, idx, lens):
    tables = idx.shape[0]
    return pl.pallas_call(
        prep_kernel,
        grid=(tables,),
        in_specs=[
            pl.BlockSpec(memory_space=pltpu.SMEM),
            pl.BlockSpec((1,) + idx.shape[1:], lambda j: (j, 0, 0)),
            pl.BlockSpec(lens.shape, lambda j: (0, 0)),
        ],
        out_specs=[
            pl.BlockSpec((1, BLOCKS, 4, BAG_BLOCKS, LANES), lambda j: (j, 0, 0, 0, 0)),
            pl.BlockSpec((1, 8, BAG_BLOCKS, LANES), lambda j: (j, 0, 0, 0)),
            pl.BlockSpec((tables, BAG_BLOCKS, LANES), lambda j: (0, 0, 0)),
        ],
        out_shape=[
            jax.ShapeDtypeStruct((tables, BLOCKS, 4, BAG_BLOCKS, LANES), jnp.float32),
            jax.ShapeDtypeStruct((tables, 8, BAG_BLOCKS, LANES), jnp.int32),
            jax.ShapeDtypeStruct((tables, BAG_BLOCKS, LANES), jnp.int32),
        ],
        compiler_params=pltpu.CompilerParams(vmem_limit_bytes=24 << 20),
        cost_estimate=pl.CostEstimate(
            flops=40_000_000, bytes_accessed=9_000_000, transcendentals=0
        ),
        name="prep",
    )(pos, idx, lens)


def pool_kernel(layout, has_base, n_outs, table0, *refs):
    n_pieces = len(layout)
    mask_ref, lid_ref = refs[:2]
    keys = refs[2 : 2 + n_pieces]
    tabs = refs[2 + n_pieces : 2 + 2 * n_pieces]
    refs = refs[2 + 2 * n_pieces :]
    if has_base:
        base_ref, refs = refs[0], refs[1:]
    if n_outs:
        outs, (sums, counts, extra) = refs[:n_outs], refs[n_outs:]
    else:
        sums, counts, extra = refs
    table, step = pl.program_id(0), pl.program_id(1)
    first_block = layout[0][0]
    n_blocks = sum(n for _, n in layout)
    row_ids = [
        (lax.broadcasted_iota(jnp.int32, (16, PAIR), 0) + c * 16)
        .astype(jnp.float32)
        .astype(jnp.bfloat16)
        for c in range(SUB // 16)
    ]

    def wide(x):
        return jnp.broadcast_to(x, (16, LANES)).astype(jnp.bfloat16)

    for part in range(2):
        bag = 4 * step + 2 * part
        for (first, n), key in zip(layout, keys):
            for b in range(n):
                k1, m1, k2, m2 = (
                    jnp.concatenate(
                        [wide(key[0, 0, b, v, pl.ds(bag + half, 1), :]) for half in range(2)],
                        axis=1,
                    )
                    for v in range(4)
                )
                row = (first - first_block + b) * SUB
                for c in range(SUB // 16):
                    counts[part, row + c * 16 : row + (c + 1) * 16, :] = jnp.where(
                        k1 == row_ids[c], m1, jnp.where(k2 == row_ids[c], m2, jnp.bfloat16(0))
                    )
        total = base_ref[0, 0, part] if has_base else None
        for (first, n), tab in zip(layout, tabs):
            row = (first - first_block) * SUB
            product = jnp.dot(
                tab[0], counts[part, row : row + n * SUB, :], preferred_element_type=jnp.float32
            )
            total = product if total is None else total + product
        sums[0, 0, part] = total

    stage_bits = ((1 << n_blocks) - 1) << first_block
    stage_bits = stage_bits - (1 << 32) if stage_bits >= 1 << 31 else stage_bits
    for part in range(2):
        bag = 4 * step + 2 * part
        mask = mask_ref[table0 + table, bag, 0] | mask_ref[table0 + table, bag + 1, 0]

        @pl.when((mask & jnp.int32(stage_bits)) != 0)
        def _(part=part, bag=bag, mask=mask):
            def fix(at, carry):
                blk = first_block + at

                @pl.when(((mask >> blk) & 1) == 1)
                def _():
                    for half in range(2):
                        row = pl.ds(bag + half, 1)
                        lids = [lid_ref[0, s, row, :] for s in range(8)]
                        low = [
                            jnp.where((x >> 8) == blk, (x & (SUB - 1)).astype(jnp.float32), -1.0)
                            for x in lids
                        ]
                        last = functools.reduce(jnp.maximum, low)
                        first = functools.reduce(
                            jnp.minimum, [jnp.where(x < 0.0, 511.0, x) for x in low]
                        )
                        left = [
                            wide(jnp.where((x == first) | (x == last), -1.0, x)) for x in low
                        ]
                        for c in range(SUB // 16):
                            n = jnp.zeros((16, LANES), jnp.bfloat16)
                            for k in left:
                                n = n + jnp.where(
                                    k == row_ids[c][:, :LANES], jnp.bfloat16(1), jnp.bfloat16(0)
                                )
                            extra[c * 16 : (c + 1) * 16, half * LANES : (half + 1) * LANES] = n
                    for (first, n), tab in zip(layout, tabs):

                        @pl.when((blk >= first) & (blk < first + n))
                        def _(first=first, tab=tab):
                            columns = pl.ds(pl.multiple_of((blk - first) * SUB, SUB), SUB)
                            sums[0, 0, part] += jnp.dot(
                                tab[0, :, columns],
                                extra[...],
                                preferred_element_type=jnp.float32,
                            )

                return carry

            lax.fori_loop(0, n_blocks, fix, 0)

    def finish(out):
        for part in range(2):
            result = sums[0, 0, part].astype(jnp.bfloat16)
            out[2 * part, 0] = result[:, :LANES]
            out[2 * part + 1, 0] = result[:, LANES:]

    if n_outs == 1:
        finish(outs[0])
    for d in range(n_outs if n_outs > 1 else 0):

        @pl.when(step == d)
        def _(d=d):
            finish(outs[d])


def pool(tables, masks, keys, lids, pieces, base, n_outs, name):
    n_tables = len(tables)
    table0 = tables[0]
    emb = pieces[0][0].shape[1]
    sums_block = (1, 1, 2, emb, PAIR)
    sums_spec = pl.BlockSpec(sums_block, lambda j, i: (j, i, 0, 0, 0))
    layout, key_specs, tab_specs = [], [], []
    for array, start_table, shard, start in pieces:
        n = array.shape[2] // SUB
        layout.append(((shard * ROWS_DEV + start) // SUB, n))
        key_specs.append(
            pl.BlockSpec(
                (1, 1, n) + keys.shape[3:],
                lambda j, i, shard=shard, at=start // SUB // n: (table0 + j, shard, at, 0, 0, 0),
            )
        )
        tab_specs.append(
            pl.BlockSpec(
                (1,) + array.shape[1:], lambda j, i, skip=table0 - start_table: (skip + j, 0, 0)
            )
        )
    rows = sum(n for _, n in layout) * SUB
    in_specs = [
        pl.BlockSpec(memory_space=pltpu.SMEM),
        pl.BlockSpec((1,) + lids.shape[1:], lambda j, i: (table0 + j, 0, 0, 0)),
        *key_specs,
        *tab_specs,
    ]
    args = [masks, lids] + [keys] * len(pieces) + [p[0] for p in pieces]
    if base is not None:
        array, start_table = base
        in_specs.append(
            pl.BlockSpec(sums_block, lambda j, i: (table0 - start_table + j, i, 0, 0, 0))
        )
        args.append(array)
    scratch = [
        pltpu.VMEM((2, rows, PAIR), jnp.bfloat16),
        pltpu.VMEM((SUB, PAIR), jnp.bfloat16),
    ]
    if n_outs:
        places = BAG_BLOCKS // n_outs
        out_specs = [
            pl.BlockSpec((4, 1, emb, LANES), lambda j, i: (i if n_outs == 1 else 0, j, 0, 0))
        ] * n_outs
        out_shape = [
            jax.ShapeDtypeStruct((places, n_tables, emb, LANES), jnp.bfloat16)
        ] * n_outs
        scratch = [pltpu.VMEM(sums_block, jnp.float32)] + scratch
    else:
        out_specs = sums_spec
        out_shape = jax.ShapeDtypeStruct((n_tables, 4, 2, emb, PAIR), jnp.float32)
    return pl.pallas_call(
        functools.partial(pool_kernel, tuple(layout), base is not None, n_outs, table0),
        grid=(n_tables, 4),
        in_specs=in_specs,
        out_specs=out_specs,
        out_shape=out_shape,
        scratch_shapes=scratch,
        compiler_params=pltpu.CompilerParams(vmem_limit_bytes=24 << 20),
        cost_estimate=pl.CostEstimate(
            flops=2 * n_tables * rows * 2048 * 256,
            bytes_accessed=5_000_000,
            transcendentals=0,
        ),
        name=name,
    )(*args)


def tail_kernel(host_ref, order_ref, *rest):
    parts, summed_here = rest[:4], rest[4]
    proj_ref, fm_gain_ref, up_ref, down_ref, compress_ref, gain_ref, out_ref = rest[5:12]
    emb, gram, summed = rest[12:]
    host = host_ref[0]
    for d in range(4):
        source = (host - d) & 3
        for j in range(2):
            emb[order_ref[source * 4 + j]] = parts[d][j].astype(jnp.float32)
            total = summed_here[4 * d, j].astype(jnp.float32)
            for k in range(1, 4):
                total = total + summed_here[4 * d + k, j].astype(jnp.float32)
            emb[order_ref[d * 4 + 2 + j]] = total.astype(jnp.bfloat16).astype(jnp.float32)
    feats, width, lanes = emb.shape
    rank = proj_ref.shape[1]
    proj_weight = proj_ref[...].astype(jnp.float32).T
    fm_gain = fm_gain_ref[...].T
    compress = compress_ref[...].astype(jnp.float32)
    gain = gain_ref[...].T

    for f in range(feats):
        x = emb[f]
        for g in range(f + 1):
            dot = jnp.sum(x * emb[g], axis=0, keepdims=True)
            gram[f, g : g + 1, :] = dot
            if g != f:
                gram[g, f : f + 1, :] = dot
    proj = [jnp.broadcast_to(proj_weight[:, g : g + 1], (rank, lanes)) for g in range(feats)]
    rows = []
    for f in range(feats):
        row = None
        for g in range(feats):
            term = proj[g] * gram[f, g : g + 1, :]
            row = term if row is None else row + term
        rows.append(row)
    inv = 1.0 / (rank * feats)
    mean = jnp.sum(sum(rows), axis=0, keepdims=True) * inv
    rows = [r - mean for r in rows]
    spread = jnp.sum(sum(r * r for r in rows), axis=0, keepdims=True) * inv
    scale = 1.0 / jnp.sqrt(spread + 1e-05)
    normed = jnp.concatenate([r * scale for r in rows], axis=0)
    normed = jnp.concatenate(
        [
            normed[c * lanes : (c + 1) * lanes] * fm_gain[:, c : c + 1]
            for c in range(rank * feats // lanes)
        ],
        axis=0,
    )
    hidden = jnp.maximum(
        jnp.dot(normed.T.astype(jnp.bfloat16), up_ref[...], preferred_element_type=jnp.float32),
        0.0,
    ).astype(jnp.bfloat16)
    fm_block = jnp.dot(hidden, down_ref[...], preferred_element_type=jnp.float32).T
    half = feats // 2
    for m in range(half):
        summed[m] = fm_block[m * width : (m + 1) * width, :] + emb[m]
        acc = emb[half + m]
        for f in range(feats):
            acc = acc + compress[m : m + 1, f : f + 1] * emb[f]
        summed[half + m] = acc
    inv = 1.0 / (feats * width)
    total = summed[0]
    for f in range(1, feats):
        total = total + summed[f]
    mean = jnp.sum(total, axis=0, keepdims=True) * inv
    square = None
    for f in range(feats):
        c = summed[f] - mean
        square = c * c if square is None else square + c * c
    spread = jnp.sum(square, axis=0, keepdims=True) * inv
    scale = 1.0 / jnp.sqrt(spread + 1e-05)
    for f in range(feats):
        out_ref[f] = ((summed[f] - mean) * scale * gain[:, f : f + 1]).astype(jnp.bfloat16)


def tail(host, order, parts, *weights):
    feats, width = order.shape[0], parts[0].shape[2]
    smem = pl.BlockSpec(memory_space=pltpu.SMEM)
    vmem = pl.BlockSpec(memory_space=pltpu.VMEM)
    mine = pl.BlockSpec((None,) + parts[0].shape[1:], lambda i: (0, 0, 0, 0))
    there = pl.BlockSpec(parts[1].shape, lambda i: (0, 0, 0))
    return pl.pallas_call(
        tail_kernel,
        grid=(1,),
        in_specs=[smem] * 2 + [mine] + [there] * 3 + [vmem] * 7,
        out_specs=vmem,
        out_shape=jax.ShapeDtypeStruct((feats, width, LANES), jnp.bfloat16),
        scratch_shapes=[
            pltpu.VMEM((feats, width, LANES), jnp.float32),
            pltpu.VMEM((feats, feats, LANES), jnp.float32),
            pltpu.VMEM((feats, width, LANES), jnp.float32),
        ],
        compiler_params=pltpu.CompilerParams(vmem_limit_bytes=32 << 20),
        cost_estimate=pl.CostEstimate(
            flops=1_000_000_000, bytes_accessed=8_000_000, transcendentals=0
        ),
        name="tail",
    )(host, order, *parts, *weights)


def move(x, axis, step):
    size = 2 if axis == "core" else 4
    return lax.ppermute(x, axis, [(i, (i + step) % size) for i in range(size)])


def other_core(x):
    return move(x, "core", 1)


def to_owners(blocks, axis):
    return [blocks[0]] + [move(blocks[d], axis, d) for d in range(1, 4)]


def add_up(blocks):
    return sum(b.astype(jnp.float32) for b in blocks).astype(jnp.bfloat16)


def to_hosts(total):
    return [total] + [move(total[d], "hst", d) for d in range(1, 4)]


def on_device(
    tables,
    indices,
    lengths,
    feature_order,
    proj_weight,
    fm_gain,
    up_weight,
    down_weight,
    compress_weight,
    out_gain,
):
    pos = jnp.stack([lax.axis_index(a) for a in ("hst", "z", "y", "core")]).astype(jnp.int32)

    flipped = jnp.swapaxes(tables, 1, 2)
    keys, lids, masks = prep(pos, jnp.transpose(indices, (1, 2, 0)), lengths.T)
    keys = keys.reshape((keys.shape[0], GATHER, ROWS_DEV // SUB) + keys.shape[2:])
    pairs = [(0, 1), (2, 3)]
    axes = ["z", "y"]

    mine = [flipped[2 * p : 2 * p + 2] for p in range(2)]
    sides = [[move(mine[p], axes[p], 3), move(mine[p], axes[p], 1)] for p in range(2)]
    own_far = other_core(flipped)

    def stage(tables, arrays, shard, base, n_outs, name):
        pieces = [(x, 0 if x.shape[0] == 4 else tables[0]) for x in arrays]
        pieces = [(x, start, shard + k, 0) for k, (x, start) in enumerate(pieces)]
        return pool(tables, masks, keys, lids, pieces, base, n_outs, name)

    sums = stage((0, 1, 2, 3), [flipped], 0, None, 0, "pool_own")
    sums, sides, mine, masks = lax.optimization_barrier((sums, sides, mine, masks))
    beyond = [move(mine[p], axes[p], 2) for p in range(2)]
    early = [other_core(x) for x in (sides[0][0], sides[0][1], sides[1][0])]
    middle = []
    for p in range(2):
        middle.append(stage(pairs[p], [own_far] + sides[p], 1, (sums, 0), 0, "pool_sides"))
        masks, _ = lax.optimization_barrier((masks, middle[p]))
    sides, beyond, early, masks = lax.optimization_barrier((sides, beyond, early, masks))
    late = [other_core(x) for x in (beyond[0], sides[1][1], beyond[1])]
    first = stage(pairs[0], early[:2], 4, (middle[0], 0), 0, "pool_other")
    masks, _ = lax.optimization_barrier((masks, first))
    blocks = stage(pairs[0], [beyond[0], late[0]], 6, (first, 0), 4, "pool_beyond")
    masks, _ = lax.optimization_barrier((masks, blocks))
    arrived = to_owners(blocks, axes[1])
    (blocks,) = stage(
        pairs[1],
        [early[2], late[1], beyond[1], late[2]],
        4,
        (middle[1], 2),
        1,
        "pool_rest",
    )
    arrived, blocks = lax.optimization_barrier((arrived, blocks))
    parts = to_hosts(add_up(arrived))
    parts.append(lax.all_to_all(blocks, ("hst", axes[0]), 0, 0, tiled=True))
    result = tail(
        pos[:1],
        feature_order,
        parts,
        proj_weight.T,
        fm_gain.reshape(-1, LANES),
        up_weight,
        down_weight,
        compress_weight,
        out_gain,
    )
    return jnp.transpose(result, (2, 0, 1))


def solution(mesh):
    fine = Mesh(mesh.devices.reshape(4, 4, 4, 2), ("hst", "z", "y", "core"))
    row = ("z", "y", "core")
    in_specs = (
        P("hst", row, None),
        P(None, "hst", None),
        P(None, "hst"),
        P(),
        P(),
        P(),
        P(),
        P(),
        P(),
        P(),
    )
    out_specs = P(("hst",) + row, None, None)
    return jax.shard_map(
        on_device, mesh=fine, in_specs=in_specs, out_specs=out_specs, check_vma=False
    )
```

```python
import functools

import jax
import jax.numpy as jnp
from jax import lax
from jax.experimental import pallas as pl
from jax.experimental.pallas import tpu as pltpu
from jax.sharding import Mesh
from jax.sharding import PartitionSpec as P

LANES = 128
ROWS_DEV = 1024
SUB = 256
GATHER = 8
BLOCKS = GATHER * ROWS_DEV // SUB
BAG_BLOCKS = 16
PAIR = 2 * LANES
PARTS = 4
STEPS = BAG_BLOCKS // (2 * PARTS)


def prep_kernel(pos_ref, idx_ref, len_ref, keys_ref, lid_ref, mask_ref):
    host, z, y, core = pos_ref[0], pos_ref[1], pos_ref[2], pos_ref[3]
    table = pl.program_id(0)
    over_z = table < 2
    slot = lax.broadcasted_iota(jnp.int32, (8, LANES), 0)
    pick = lax.broadcasted_iota(jnp.int32, (len_ref.shape[0], LANES), 0)
    for n in range(BAG_BLOCKS):
        high_part, low_part = n // 4, n % 4
        owner_host = jnp.where(over_z, (host + low_part) & 3, high_part)
        row_dev = jnp.where(
            over_z,
            z * 8 + ((y + high_part) & 3) * 2 + core,
            low_part * 8 + y * 2 + core,
        )
        start = pl.multiple_of((owner_host * 32 + row_dev) * LANES, LANES)
        v = idx_ref[0, :, pl.ds(start, LANES)]
        used = jnp.sum(
            jnp.where(pick == table, len_ref[:, pl.ds(start, LANES)], 0), axis=0, keepdims=True
        )
        at_z, at_y, at_core = v >> 13, (v >> 11) & 3, (v >> 10) & 1
        here = jnp.where(over_z, at_y - y, at_z - z) == 0
        away = jnp.where(over_z, at_z - z, at_y - y) & 3
        other = at_core ^ core
        shard = jnp.where(away == 2, 6 + other, 2 + (away >> 1) + 2 * other)
        shard = jnp.where(away == 0, other, shard)
        local = shard * ROWS_DEV + (v & (ROWS_DEV - 1))
        local = jnp.where(here & (slot < used), local, -1)
        for s in range(8):
            lid_ref[0, s, n : n + 1, :] = local[s : s + 1, :]
    for g in range(BAG_BLOCKS // 8):
        rows = pl.ds(g * 8, 8)
        lids = [lid_ref[0, s, rows, :] for s in range(8)]
        high = [x >> 8 for x in lids]
        low = [(x & (SUB - 1)).astype(jnp.float32) for x in lids]

        def one_block(blk, mask):
            at = [h == blk for h in high]
            up = [jnp.where(a, l, 511.0) for a, l in zip(at, low)]
            down = [jnp.where(a, l, -1.0) for a, l in zip(at, low)]
            first = functools.reduce(jnp.minimum, up)
            last = functools.reduce(jnp.maximum, down)
            n_first = sum(jnp.where(u == first, 1.0, 0.0) for u in up)
            n_last = sum(jnp.where(d == last, 1.0, 0.0) for d in down)
            total = sum(jnp.where(a, 1.0, 0.0) for a in at)
            more = (n_first + n_last) < total
            keys_ref[0, blk, 0, rows, :] = first
            keys_ref[0, blk, 1, rows, :] = n_first
            keys_ref[0, blk, 2, rows, :] = jnp.where(last == first, -1.0, last)
            keys_ref[0, blk, 3, rows, :] = n_last
            return mask | jnp.where(more, jnp.int32(1) << blk, 0)

        mask = lax.fori_loop(0, BLOCKS, one_block, jnp.zeros((8, LANES), jnp.int32))
        mask_ref[table, rows, :] = mask

    @pl.when(table == pl.num_programs(0) - 1)
    def _():
        masks = mask_ref[...]
        for shift in (64, 32, 16, 8, 4, 2, 1):
            masks = masks | pltpu.roll(masks, shift, 2)
        mask_ref[...] = masks


def prep(pos, idx, lens):
    tables = idx.shape[0]
    return pl.pallas_call(
        prep_kernel,
        grid=(tables,),
        in_specs=[
            pl.BlockSpec(memory_space=pltpu.SMEM),
            pl.BlockSpec((1,) + idx.shape[1:], lambda j: (j, 0, 0)),
            pl.BlockSpec(lens.shape, lambda j: (0, 0)),
        ],
        out_specs=[
            pl.BlockSpec((1, BLOCKS, 4, BAG_BLOCKS, LANES), lambda j: (j, 0, 0, 0, 0)),
            pl.BlockSpec((1, 8, BAG_BLOCKS, LANES), lambda j: (j, 0, 0, 0)),
            pl.BlockSpec((tables, BAG_BLOCKS, LANES), lambda j: (0, 0, 0)),
        ],
        out_shape=[
            jax.ShapeDtypeStruct((tables, BLOCKS, 4, BAG_BLOCKS, LANES), jnp.float32),
            jax.ShapeDtypeStruct((tables, 8, BAG_BLOCKS, LANES), jnp.int32),
            jax.ShapeDtypeStruct((tables, BAG_BLOCKS, LANES), jnp.int32),
        ],
        compiler_params=pltpu.CompilerParams(vmem_limit_bytes=24 << 20),
        cost_estimate=pl.CostEstimate(
            flops=40_000_000, bytes_accessed=9_000_000, transcendentals=0
        ),
        name="prep",
    )(pos, idx, lens)


def pool_kernel(layout, has_base, n_outs, table0, *refs):
    n_pieces = len(layout)
    mask_ref, lid_ref = refs[:2]
    keys = refs[2 : 2 + n_pieces]
    tabs = refs[2 + n_pieces : 2 + 2 * n_pieces]
    refs = refs[2 + 2 * n_pieces :]
    if has_base:
        base_ref, refs = refs[0], refs[1:]
    if n_outs:
        outs, (sums, counts, extra) = refs[:n_outs], refs[n_outs:]
    else:
        sums, counts, extra = refs
    table, step = pl.program_id(0), pl.program_id(1)
    first_block = layout[0][0]
    n_blocks = sum(n for _, n in layout)
    row_ids = [
        (lax.broadcasted_iota(jnp.int32, (16, PAIR), 0) + c * 16)
        .astype(jnp.float32)
        .astype(jnp.bfloat16)
        for c in range(SUB // 16)
    ]

    def wide(x):
        return jnp.broadcast_to(x, (16, LANES)).astype(jnp.bfloat16)

    for part in range(PARTS):
        bag = 2 * (PARTS * step + part)
        for (first, n), key in zip(layout, keys):
            for b in range(n):
                k1, m1, k2, m2 = (
                    jnp.concatenate(
                        [wide(key[0, 0, b, v, pl.ds(bag + half, 1), :]) for half in range(2)],
                        axis=1,
                    )
                    for v in range(4)
                )
                row = (first - first_block + b) * SUB
                for c in range(SUB // 16):
                    counts[part, row + c * 16 : row + (c + 1) * 16, :] = jnp.where(
                        k1 == row_ids[c], m1, jnp.where(k2 == row_ids[c], m2, jnp.bfloat16(0))
                    )
        total = base_ref[0, 0, part] if has_base else None
        for (first, n), tab in zip(layout, tabs):
            row = (first - first_block) * SUB
            product = jnp.dot(
                tab[0], counts[part, row : row + n * SUB, :], preferred_element_type=jnp.float32
            )
            total = product if total is None else total + product
        sums[0, 0, part] = total

    stage_bits = ((1 << n_blocks) - 1) << first_block
    stage_bits = stage_bits - (1 << 32) if stage_bits >= 1 << 31 else stage_bits
    for part in range(PARTS):
        bag = 2 * (PARTS * step + part)
        mask = mask_ref[table0 + table, bag, 0] | mask_ref[table0 + table, bag + 1, 0]

        @pl.when((mask & jnp.int32(stage_bits)) != 0)
        def _(part=part, bag=bag, mask=mask):
            def fix(at, carry):
                blk = first_block + at

                @pl.when(((mask >> blk) & 1) == 1)
                def _():
                    for half in range(2):
                        row = pl.ds(bag + half, 1)
                        lids = [lid_ref[0, s, row, :] for s in range(8)]
                        low = [
                            jnp.where((x >> 8) == blk, (x & (SUB - 1)).astype(jnp.float32), -1.0)
                            for x in lids
                        ]
                        last = functools.reduce(jnp.maximum, low)
                        first = functools.reduce(
                            jnp.minimum, [jnp.where(x < 0.0, 511.0, x) for x in low]
                        )
                        left = [
                            wide(jnp.where((x == first) | (x == last), -1.0, x)) for x in low
                        ]
                        for c in range(SUB // 16):
                            n = jnp.zeros((16, LANES), jnp.bfloat16)
                            for k in left:
                                n = n + jnp.where(
                                    k == row_ids[c][:, :LANES], jnp.bfloat16(1), jnp.bfloat16(0)
                                )
                            extra[c * 16 : (c + 1) * 16, half * LANES : (half + 1) * LANES] = n
                    for (first, n), tab in zip(layout, tabs):

                        @pl.when((blk >= first) & (blk < first + n))
                        def _(first=first, tab=tab):
                            columns = pl.ds(pl.multiple_of((blk - first) * SUB, SUB), SUB)
                            sums[0, 0, part] += jnp.dot(
                                tab[0, :, columns],
                                extra[...],
                                preferred_element_type=jnp.float32,
                            )

                return carry

            lax.fori_loop(0, n_blocks, fix, 0)

    def finish(out, first_part, n_parts):
        for k in range(n_parts):
            result = sums[0, 0, first_part + k].astype(jnp.bfloat16)
            out[2 * k, 0] = result[:, :LANES]
            out[2 * k + 1, 0] = result[:, LANES:]

    if n_outs == 1:
        finish(outs[0], 0, PARTS)
    for d in range(n_outs if n_outs > 1 else 0):

        @pl.when(step == 2 * d // PARTS)
        def _(d=d):
            finish(outs[d], 2 * d % PARTS, 2)


def pool(tables, masks, keys, lids, pieces, base, n_outs, name):
    n_tables = len(tables)
    table0 = tables[0]
    emb = pieces[0][0].shape[1]
    sums_block = (1, 1, PARTS, emb, PAIR)
    sums_spec = pl.BlockSpec(sums_block, lambda j, i: (j, i, 0, 0, 0))
    layout, key_specs, tab_specs = [], [], []
    for array, start_table, shard, start in pieces:
        n = array.shape[2] // SUB
        layout.append(((shard * ROWS_DEV + start) // SUB, n))
        key_specs.append(
            pl.BlockSpec(
                (1, 1, n) + keys.shape[3:],
                lambda j, i, shard=shard, at=start // SUB // n: (table0 + j, shard, at, 0, 0, 0),
            )
        )
        tab_specs.append(
            pl.BlockSpec(
                (1,) + array.shape[1:], lambda j, i, skip=table0 - start_table: (skip + j, 0, 0)
            )
        )
    rows = sum(n for _, n in layout) * SUB
    in_specs = [
        pl.BlockSpec(memory_space=pltpu.SMEM),
        pl.BlockSpec((1,) + lids.shape[1:], lambda j, i: (table0 + j, 0, 0, 0)),
        *key_specs,
        *tab_specs,
    ]
    args = [masks, lids] + [keys] * len(pieces) + [p[0] for p in pieces]
    if base is not None:
        array, start_table = base
        in_specs.append(
            pl.BlockSpec(sums_block, lambda j, i: (table0 - start_table + j, i, 0, 0, 0))
        )
        args.append(array)
    scratch = [
        pltpu.VMEM((PARTS, rows, PAIR), jnp.bfloat16),
        pltpu.VMEM((SUB, PAIR), jnp.bfloat16),
    ]
    if n_outs:
        places = BAG_BLOCKS // n_outs
        out_specs = [
            pl.BlockSpec(
                (2 * PARTS if n_outs == 1 else places, 1, emb, LANES),
                lambda j, i: (i if n_outs == 1 else 0, j, 0, 0),
            )
        ] * n_outs
        out_shape = [
            jax.ShapeDtypeStruct((places, n_tables, emb, LANES), jnp.bfloat16)
        ] * n_outs
        scratch = [pltpu.VMEM(sums_block, jnp.float32)] + scratch
    else:
        out_specs = sums_spec
        out_shape = jax.ShapeDtypeStruct((n_tables, STEPS, PARTS, emb, PAIR), jnp.float32)
    return pl.pallas_call(
        functools.partial(pool_kernel, tuple(layout), base is not None, n_outs, table0),
        grid=(n_tables, STEPS),
        in_specs=in_specs,
        out_specs=out_specs,
        out_shape=out_shape,
        scratch_shapes=scratch,
        compiler_params=pltpu.CompilerParams(vmem_limit_bytes=24 << 20),
        cost_estimate=pl.CostEstimate(
            flops=2 * n_tables * rows * 2048 * 256,
            bytes_accessed=5_000_000,
            transcendentals=0,
        ),
        name=name,
    )(*args)


def tail_kernel(host_ref, order_ref, *rest):
    parts, summed_here = rest[:4], rest[4]
    proj_ref, fm_gain_ref, up_ref, down_ref, compress_ref, gain_ref, out_ref = rest[5:12]
    emb, gram, summed = rest[12:]
    host = host_ref[0]
    for d in range(4):
        source = (host - d) & 3
        for j in range(2):
            emb[order_ref[source * 4 + j]] = parts[d][j].astype(jnp.float32)
            total = summed_here[4 * d, j].astype(jnp.float32)
            for k in range(1, 4):
                total = total + summed_here[4 * d + k, j].astype(jnp.float32)
            emb[order_ref[d * 4 + 2 + j]] = total.astype(jnp.bfloat16).astype(jnp.float32)
    feats, width, lanes = emb.shape
    rank = proj_ref.shape[1]
    proj_weight = proj_ref[...].astype(jnp.float32).T
    fm_gain = fm_gain_ref[...].T
    compress = compress_ref[...].astype(jnp.float32)
    gain = gain_ref[...].T

    for f in range(feats):
        x = emb[f]
        for g in range(f + 1):
            dot = jnp.sum(x * emb[g], axis=0, keepdims=True)
            gram[f, g : g + 1, :] = dot
            if g != f:
                gram[g, f : f + 1, :] = dot
    proj = [jnp.broadcast_to(proj_weight[:, g : g + 1], (rank, lanes)) for g in range(feats)]
    rows = []
    for f in range(feats):
        row = None
        for g in range(feats):
            term = proj[g] * gram[f, g : g + 1, :]
            row = term if row is None else row + term
        rows.append(row)
    inv = 1.0 / (rank * feats)
    mean = jnp.sum(sum(rows), axis=0, keepdims=True) * inv
    rows = [r - mean for r in rows]
    spread = jnp.sum(sum(r * r for r in rows), axis=0, keepdims=True) * inv
    scale = 1.0 / jnp.sqrt(spread + 1e-05)
    normed = jnp.concatenate([r * scale for r in rows], axis=0)
    normed = jnp.concatenate(
        [
            normed[c * lanes : (c + 1) * lanes] * fm_gain[:, c : c + 1]
            for c in range(rank * feats // lanes)
        ],
        axis=0,
    )
    hidden = jnp.maximum(
        jnp.dot(normed.T.astype(jnp.bfloat16), up_ref[...], preferred_element_type=jnp.float32),
        0.0,
    ).astype(jnp.bfloat16)
    fm_block = jnp.dot(hidden, down_ref[...], preferred_element_type=jnp.float32).T
    half = feats // 2
    for m in range(half):
        summed[m] = fm_block[m * width : (m + 1) * width, :] + emb[m]
        acc = emb[half + m]
        for f in range(feats):
            acc = acc + compress[m : m + 1, f : f + 1] * emb[f]
        summed[half + m] = acc
    inv = 1.0 / (feats * width)
    total = summed[0]
    for f in range(1, feats):
        total = total + summed[f]
    mean = jnp.sum(total, axis=0, keepdims=True) * inv
    square = None
    for f in range(feats):
        c = summed[f] - mean
        square = c * c if square is None else square + c * c
    spread = jnp.sum(square, axis=0, keepdims=True) * inv
    scale = 1.0 / jnp.sqrt(spread + 1e-05)
    for f in range(feats):
        out_ref[f] = ((summed[f] - mean) * scale * gain[:, f : f + 1]).astype(jnp.bfloat16)


def tail(host, order, parts, *weights):
    feats, width = order.shape[0], parts[0].shape[2]
    smem = pl.BlockSpec(memory_space=pltpu.SMEM)
    vmem = pl.BlockSpec(memory_space=pltpu.VMEM)
    mine = pl.BlockSpec((None,) + parts[0].shape[1:], lambda i: (0, 0, 0, 0))
    there = pl.BlockSpec(parts[1].shape, lambda i: (0, 0, 0))
    return pl.pallas_call(
        tail_kernel,
        grid=(1,),
        in_specs=[smem] * 2 + [mine] + [there] * 3 + [vmem] * 7,
        out_specs=vmem,
        out_shape=jax.ShapeDtypeStruct((feats, width, LANES), jnp.bfloat16),
        scratch_shapes=[
            pltpu.VMEM((feats, width, LANES), jnp.float32),
            pltpu.VMEM((feats, feats, LANES), jnp.float32),
            pltpu.VMEM((feats, width, LANES), jnp.float32),
        ],
        compiler_params=pltpu.CompilerParams(vmem_limit_bytes=20 << 20),
        cost_estimate=pl.CostEstimate(
            flops=1_000_000_000, bytes_accessed=8_000_000, transcendentals=0
        ),
        name="tail",
    )(host, order, *parts, *weights)


def move(x, axis, step):
    size = 2 if axis == "core" else 4
    return lax.ppermute(x, axis, [(i, (i + step) % size) for i in range(size)])


def other_core(x):
    return move(x, "core", 1)


def to_owners(blocks, axis):
    return [blocks[0]] + [move(blocks[d], axis, d) for d in range(1, 4)]


def add_up(blocks):
    return sum(b.astype(jnp.float32) for b in blocks).astype(jnp.bfloat16)


def to_hosts(total):
    return [total] + [move(total[d], "hst", d) for d in range(1, 4)]


def on_device(
    tables,
    indices,
    lengths,
    feature_order,
    proj_weight,
    fm_gain,
    up_weight,
    down_weight,
    compress_weight,
    out_gain,
):
    pos = jnp.stack([lax.axis_index(a) for a in ("hst", "z", "y", "core")]).astype(jnp.int32)

    flipped = jnp.swapaxes(tables, 1, 2)
    keys, lids, masks = prep(pos, jnp.transpose(indices, (1, 2, 0)), lengths.T)
    keys = keys.reshape((keys.shape[0], GATHER, ROWS_DEV // SUB) + keys.shape[2:])
    pairs = [(0, 1), (2, 3)]
    axes = ["z", "y"]

    mine = [flipped[2 * p : 2 * p + 2] for p in range(2)]
    sides = [[move(mine[p], axes[p], 3), move(mine[p], axes[p], 1)] for p in range(2)]
    own_far = other_core(flipped)

    def stage(tables, arrays, shard, base, n_outs, name):
        pieces = [(x, 0 if x.shape[0] == 4 else tables[0]) for x in arrays]
        pieces = [(x, start, shard + k, 0) for k, (x, start) in enumerate(pieces)]
        return pool(tables, masks, keys, lids, pieces, base, n_outs, name)

    sums = stage((0, 1, 2, 3), [flipped], 0, None, 0, "pool_own")
    sums, sides, mine, masks = lax.optimization_barrier((sums, sides, mine, masks))
    beyond = [move(mine[p], axes[p], 2) for p in range(2)]
    early = [other_core(x) for x in (sides[0][0], sides[0][1], sides[1][0])]
    middle = []
    for p in range(2):
        middle.append(stage(pairs[p], [own_far] + sides[p], 1, (sums, 0), 0, "pool_sides"))
        masks, _ = lax.optimization_barrier((masks, middle[p]))
    sides, beyond, early, masks = lax.optimization_barrier((sides, beyond, early, masks))
    late = [other_core(x) for x in (beyond[0], sides[1][1], beyond[1])]
    first = stage(pairs[0], early[:2], 4, (middle[0], 0), 0, "pool_other")
    masks, _ = lax.optimization_barrier((masks, first))
    blocks = stage(pairs[0], [beyond[0], late[0]], 6, (first, 0), 4, "pool_beyond")
    masks, _ = lax.optimization_barrier((masks, blocks))
    arrived = to_owners(blocks, axes[1])
    (blocks,) = stage(
        pairs[1],
        [early[2], late[1], beyond[1], late[2]],
        4,
        (middle[1], 2),
        1,
        "pool_rest",
    )
    arrived, blocks = lax.optimization_barrier((arrived, blocks))
    parts = to_hosts(add_up(arrived))
    parts.append(lax.all_to_all(blocks, ("hst", axes[0]), 0, 0, tiled=True))
    result = tail(
        pos[:1],
        feature_order,
        parts,
        proj_weight.T,
        fm_gain.reshape(-1, LANES),
        up_weight,
        down_weight,
        compress_weight,
        out_gain,
    )
    return jnp.transpose(result, (2, 0, 1))


def solution(mesh):
    fine = Mesh(mesh.devices.reshape(4, 4, 4, 2), ("hst", "z", "y", "core"))
    row = ("z", "y", "core")
    in_specs = (
        P("hst", row, None),
        P(None, "hst", None),
        P(None, "hst"),
        P(),
        P(),
        P(),
        P(),
        P(),
        P(),
        P(),
    )
    out_specs = P(("hst",) + row, None, None)
    return jax.shard_map(
        on_device, mesh=fine, in_specs=in_specs, out_specs=out_specs, check_vma=False
    )
```

```python
import functools

import jax
import jax.numpy as jnp
from jax import lax
from jax.experimental import pallas as pl
from jax.experimental.pallas import tpu as pltpu
from jax.sharding import Mesh
from jax.sharding import PartitionSpec as P

LANES = 128
ROWS_DEV = 1024
SUB = 256
GATHER = 8
BLOCKS = GATHER * ROWS_DEV // SUB
BAG_BLOCKS = 16
PAIR = 2 * LANES
PARTS = 4
STEPS = BAG_BLOCKS // (2 * PARTS)


def prep_kernel(pos_ref, idx_ref, len_ref, keys_ref, lid_ref, mask_ref):
    host, z, y, core = pos_ref[0], pos_ref[1], pos_ref[2], pos_ref[3]
    table = pl.program_id(0)
    over_z = table < 2
    slot = lax.broadcasted_iota(jnp.int32, (8, LANES), 0)
    pick = lax.broadcasted_iota(jnp.int32, (len_ref.shape[0], LANES), 0)
    for n in range(BAG_BLOCKS):
        high_part, low_part = n // 4, n % 4
        owner_host = jnp.where(over_z, (host + low_part) & 3, high_part)
        row_dev = jnp.where(
            over_z,
            z * 8 + ((y + high_part) & 3) * 2 + core,
            low_part * 8 + y * 2 + core,
        )
        start = pl.multiple_of((owner_host * 32 + row_dev) * LANES, LANES)
        v = idx_ref[0, :, pl.ds(start, LANES)]
        used = jnp.sum(
            jnp.where(pick == table, len_ref[:, pl.ds(start, LANES)], 0), axis=0, keepdims=True
        )
        at_z, at_y, at_core = v >> 13, (v >> 11) & 3, (v >> 10) & 1
        here = jnp.where(over_z, at_y - y, at_z - z) == 0
        away = jnp.where(over_z, at_z - z, at_y - y) & 3
        other = at_core ^ core
        shard = jnp.where(away == 2, 6 + other, 2 + (away >> 1) + 2 * other)
        shard = jnp.where(away == 0, other, shard)
        local = shard * ROWS_DEV + (v & (ROWS_DEV - 1))
        local = jnp.where(here & (slot < used), local, -1)
        for s in range(8):
            lid_ref[0, s, n : n + 1, :] = local[s : s + 1, :]
    for g in range(BAG_BLOCKS // 8):
        rows = pl.ds(g * 8, 8)
        lids = [lid_ref[0, s, rows, :] for s in range(8)]
        high = [x >> 8 for x in lids]
        low = [(x & (SUB - 1)).astype(jnp.float32) for x in lids]

        def one_block(blk, mask):
            at = [h == blk for h in high]
            up = [jnp.where(a, l, 511.0) for a, l in zip(at, low)]
            down = [jnp.where(a, l, -1.0) for a, l in zip(at, low)]
            first = functools.reduce(jnp.minimum, up)
            last = functools.reduce(jnp.maximum, down)
            n_first = sum(jnp.where(u == first, 1.0, 0.0) for u in up)
            n_last = sum(jnp.where(d == last, 1.0, 0.0) for d in down)
            total = sum(jnp.where(a, 1.0, 0.0) for a in at)
            more = (n_first + n_last) < total
            keys_ref[0, blk, 0, rows, :] = first
            keys_ref[0, blk, 1, rows, :] = n_first
            keys_ref[0, blk, 2, rows, :] = jnp.where(last == first, -1.0, last)
            keys_ref[0, blk, 3, rows, :] = n_last
            return mask | jnp.where(more, jnp.int32(1) << blk, 0)

        mask = lax.fori_loop(0, BLOCKS, one_block, jnp.zeros((8, LANES), jnp.int32))
        mask_ref[table, rows, :] = mask

    @pl.when(table == pl.num_programs(0) - 1)
    def _():
        masks = mask_ref[...]
        for shift in (64, 32, 16, 8, 4, 2, 1):
            masks = masks | pltpu.roll(masks, shift, 2)
        mask_ref[...] = masks


def prep(pos, idx, lens):
    tables = idx.shape[0]
    return pl.pallas_call(
        prep_kernel,
        grid=(tables,),
        in_specs=[
            pl.BlockSpec(memory_space=pltpu.SMEM),
            pl.BlockSpec((1,) + idx.shape[1:], lambda j: (j, 0, 0)),
            pl.BlockSpec(lens.shape, lambda j: (0, 0)),
        ],
        out_specs=[
            pl.BlockSpec((1, BLOCKS, 4, BAG_BLOCKS, LANES), lambda j: (j, 0, 0, 0, 0)),
            pl.BlockSpec((1, 8, BAG_BLOCKS, LANES), lambda j: (j, 0, 0, 0)),
            pl.BlockSpec((tables, BAG_BLOCKS, LANES), lambda j: (0, 0, 0)),
        ],
        out_shape=[
            jax.ShapeDtypeStruct((tables, BLOCKS, 4, BAG_BLOCKS, LANES), jnp.float32),
            jax.ShapeDtypeStruct((tables, 8, BAG_BLOCKS, LANES), jnp.int32),
            jax.ShapeDtypeStruct((tables, BAG_BLOCKS, LANES), jnp.int32),
        ],
        compiler_params=pltpu.CompilerParams(vmem_limit_bytes=24 << 20),
        cost_estimate=pl.CostEstimate(
            flops=40_000_000, bytes_accessed=9_000_000, transcendentals=0
        ),
        name="prep",
    )(pos, idx, lens)


def pool_kernel(layout, has_base, n_outs, table0, *refs):
    n_pieces = len(layout)
    mask_ref, lid_ref = refs[:2]
    keys = refs[2 : 2 + n_pieces]
    tabs = refs[2 + n_pieces : 2 + 2 * n_pieces]
    refs = refs[2 + 2 * n_pieces :]
    if has_base:
        base_ref, refs = refs[0], refs[1:]
    if n_outs:
        outs, (sums, counts, extra) = refs[:n_outs], refs[n_outs:]
    else:
        sums, counts, extra = refs
    table, step = pl.program_id(0), pl.program_id(1)
    first_block = layout[0][0]
    n_blocks = sum(n for _, n in layout)
    row_ids = [
        (lax.broadcasted_iota(jnp.int32, (16, PAIR), 0) + c * 16)
        .astype(jnp.float32)
        .astype(jnp.bfloat16)
        for c in range(SUB // 16)
    ]

    def wide(x):
        return jnp.broadcast_to(x, (16, LANES)).astype(jnp.bfloat16)

    for part in range(PARTS):
        bag = 2 * (PARTS * step + part)
        for (first, n), key in zip(layout, keys):
            for b in range(n):
                k1, m1, k2, m2 = (
                    jnp.concatenate(
                        [wide(key[0, 0, b, v, pl.ds(bag + half, 1), :]) for half in range(2)],
                        axis=1,
                    )
                    for v in range(4)
                )
                row = (first - first_block + b) * SUB
                for c in range(SUB // 16):
                    counts[part, row + c * 16 : row + (c + 1) * 16, :] = jnp.where(
                        k1 == row_ids[c], m1, jnp.where(k2 == row_ids[c], m2, jnp.bfloat16(0))
                    )
        total = base_ref[0, 0, part] if has_base else None
        for (first, n), tab in zip(layout, tabs):
            row = (first - first_block) * SUB
            product = jnp.dot(
                tab[0], counts[part, row : row + n * SUB, :], preferred_element_type=jnp.float32
            )
            total = product if total is None else total + product
        sums[0, 0, part] = total

    stage_bits = ((1 << n_blocks) - 1) << first_block
    stage_bits = stage_bits - (1 << 32) if stage_bits >= 1 << 31 else stage_bits
    for part in range(PARTS):
        bag = 2 * (PARTS * step + part)
        mask = mask_ref[table0 + table, bag, 0] | mask_ref[table0 + table, bag + 1, 0]

        @pl.when((mask & jnp.int32(stage_bits)) != 0)
        def _(part=part, bag=bag, mask=mask):
            def fix(at, carry):
                blk = first_block + at

                @pl.when(((mask >> blk) & 1) == 1)
                def _():
                    for half in range(2):
                        row = pl.ds(bag + half, 1)
                        lids = [lid_ref[0, s, row, :] for s in range(8)]
                        low = [
                            jnp.where((x >> 8) == blk, (x & (SUB - 1)).astype(jnp.float32), -1.0)
                            for x in lids
                        ]
                        last = functools.reduce(jnp.maximum, low)
                        first = functools.reduce(
                            jnp.minimum, [jnp.where(x < 0.0, 511.0, x) for x in low]
                        )
                        left = [
                            wide(jnp.where((x == first) | (x == last), -1.0, x)) for x in low
                        ]
                        for c in range(SUB // 16):
                            n = jnp.zeros((16, LANES), jnp.bfloat16)
                            for k in left:
                                n = n + jnp.where(
                                    k == row_ids[c][:, :LANES], jnp.bfloat16(1), jnp.bfloat16(0)
                                )
                            extra[c * 16 : (c + 1) * 16, half * LANES : (half + 1) * LANES] = n
                    for (first, n), tab in zip(layout, tabs):

                        @pl.when((blk >= first) & (blk < first + n))
                        def _(first=first, tab=tab):
                            columns = pl.ds(pl.multiple_of((blk - first) * SUB, SUB), SUB)
                            sums[0, 0, part] += jnp.dot(
                                tab[0, :, columns],
                                extra[...],
                                preferred_element_type=jnp.float32,
                            )

                return carry

            lax.fori_loop(0, n_blocks, fix, 0)

    def finish(out, first_part, n_parts):
        for k in range(n_parts):
            result = sums[0, 0, first_part + k].astype(jnp.bfloat16)
            out[2 * k, 0] = result[:, :LANES]
            out[2 * k + 1, 0] = result[:, LANES:]

    if n_outs == 1:
        finish(outs[0], 0, PARTS)
    for d in range(n_outs if n_outs > 1 else 0):

        @pl.when(step == 2 * d // PARTS)
        def _(d=d):
            finish(outs[d], 2 * d % PARTS, 2)


def pool(tables, masks, keys, lids, pieces, base, n_outs, name):
    n_tables = len(tables)
    table0 = tables[0]
    emb = pieces[0][0].shape[1]
    sums_block = (1, 1, PARTS, emb, PAIR)
    sums_spec = pl.BlockSpec(sums_block, lambda j, i: (j, i, 0, 0, 0))
    layout, key_specs, tab_specs = [], [], []
    for array, start_table, shard, start in pieces:
        n = array.shape[2] // SUB
        layout.append(((shard * ROWS_DEV + start) // SUB, n))
        key_specs.append(
            pl.BlockSpec(
                (1, 1, n) + keys.shape[3:],
                lambda j, i, shard=shard, at=start // SUB // n: (table0 + j, shard, at, 0, 0, 0),
            )
        )
        tab_specs.append(
            pl.BlockSpec(
                (1,) + array.shape[1:], lambda j, i, skip=table0 - start_table: (skip + j, 0, 0)
            )
        )
    rows = sum(n for _, n in layout) * SUB
    in_specs = [
        pl.BlockSpec(memory_space=pltpu.SMEM),
        pl.BlockSpec((1,) + lids.shape[1:], lambda j, i: (table0 + j, 0, 0, 0)),
        *key_specs,
        *tab_specs,
    ]
    args = [masks, lids] + [keys] * len(pieces) + [p[0] for p in pieces]
    if base is not None:
        array, start_table = base
        in_specs.append(
            pl.BlockSpec(sums_block, lambda j, i: (table0 - start_table + j, i, 0, 0, 0))
        )
        args.append(array)
    scratch = [
        pltpu.VMEM((PARTS, rows, PAIR), jnp.bfloat16),
        pltpu.VMEM((SUB, PAIR), jnp.bfloat16),
    ]
    if n_outs:
        places = BAG_BLOCKS // n_outs
        out_specs = [
            pl.BlockSpec(
                (2 * PARTS if n_outs == 1 else places, 1, emb, LANES),
                lambda j, i: (i if n_outs == 1 else 0, j, 0, 0),
            )
        ] * n_outs
        out_shape = [
            jax.ShapeDtypeStruct((places, n_tables, emb, LANES), jnp.bfloat16)
        ] * n_outs
        scratch = [pltpu.VMEM(sums_block, jnp.float32)] + scratch
    else:
        out_specs = sums_spec
        out_shape = jax.ShapeDtypeStruct((n_tables, STEPS, PARTS, emb, PAIR), jnp.float32)
    return pl.pallas_call(
        functools.partial(pool_kernel, tuple(layout), base is not None, n_outs, table0),
        grid=(n_tables, STEPS),
        in_specs=in_specs,
        out_specs=out_specs,
        out_shape=out_shape,
        scratch_shapes=scratch,
        compiler_params=pltpu.CompilerParams(vmem_limit_bytes=24 << 20),
        cost_estimate=pl.CostEstimate(
            flops=2 * n_tables * rows * 2048 * 256,
            bytes_accessed=5_000_000,
            transcendentals=0,
        ),
        name=name,
    )(*args)


def tail_kernel(host_ref, order_ref, *rest):
    parts, summed_here = rest[:4], rest[4]
    proj_ref, fm_gain_ref, up_ref, down_ref, compress_ref, gain_ref, out_ref = rest[5:12]
    emb, gram, summed = rest[12:]
    host = host_ref[0]
    for d in range(4):
        source = (host - d) & 3
        for j in range(2):
            emb[order_ref[source * 4 + j]] = parts[d][j].astype(jnp.float32)
            total = summed_here[4 * d, j].astype(jnp.float32)
            for k in range(1, 4):
                total = total + summed_here[4 * d + k, j].astype(jnp.float32)
            emb[order_ref[d * 4 + 2 + j]] = total.astype(jnp.bfloat16).astype(jnp.float32)
    feats, width, lanes = emb.shape
    rank = proj_ref.shape[1]
    proj_weight = proj_ref[...].astype(jnp.float32).T
    fm_gain = fm_gain_ref[...].T
    compress = compress_ref[...].astype(jnp.float32)
    gain = gain_ref[...].T

    for f in range(feats):
        x = emb[f]
        for g in range(f + 1):
            dot = jnp.sum(x * emb[g], axis=0, keepdims=True)
            gram[f, g : g + 1, :] = dot
            if g != f:
                gram[g, f : f + 1, :] = dot
    proj = [jnp.broadcast_to(proj_weight[:, g : g + 1], (rank, lanes)) for g in range(feats)]
    rows = []
    for f in range(feats):
        row = None
        for g in range(feats):
            term = proj[g] * gram[f, g : g + 1, :]
            row = term if row is None else row + term
        rows.append(row)
    inv = 1.0 / (rank * feats)
    mean = jnp.sum(sum(rows), axis=0, keepdims=True) * inv
    rows = [r - mean for r in rows]
    spread = jnp.sum(sum(r * r for r in rows), axis=0, keepdims=True) * inv
    scale = 1.0 / jnp.sqrt(spread + 1e-05)
    normed = jnp.concatenate([r * scale for r in rows], axis=0)
    normed = jnp.concatenate(
        [
            normed[c * lanes : (c + 1) * lanes] * fm_gain[:, c : c + 1]
            for c in range(rank * feats // lanes)
        ],
        axis=0,
    )
    hidden = jnp.maximum(
        jnp.dot(normed.T.astype(jnp.bfloat16), up_ref[...], preferred_element_type=jnp.float32),
        0.0,
    ).astype(jnp.bfloat16)
    fm_block = jnp.dot(hidden, down_ref[...], preferred_element_type=jnp.float32).T
    half = feats // 2
    for m in range(half):
        summed[m] = fm_block[m * width : (m + 1) * width, :] + emb[m]
        acc = emb[half + m]
        for f in range(feats):
            acc = acc + compress[m : m + 1, f : f + 1] * emb[f]
        summed[half + m] = acc
    inv = 1.0 / (feats * width)
    total = summed[0]
    for f in range(1, feats):
        total = total + summed[f]
    mean = jnp.sum(total, axis=0, keepdims=True) * inv
    square = None
    for f in range(feats):
        c = summed[f] - mean
        square = c * c if square is None else square + c * c
    spread = jnp.sum(square, axis=0, keepdims=True) * inv
    scale = 1.0 / jnp.sqrt(spread + 1e-05)
    for f in range(feats):
        out_ref[f] = ((summed[f] - mean) * scale * gain[:, f : f + 1]).astype(jnp.bfloat16)


def tail(host, order, parts, *weights):
    feats, width = order.shape[0], parts[0].shape[2]
    smem = pl.BlockSpec(memory_space=pltpu.SMEM)
    vmem = pl.BlockSpec(memory_space=pltpu.VMEM)
    mine = pl.BlockSpec((None,) + parts[0].shape[1:], lambda i: (0, 0, 0, 0))
    there = pl.BlockSpec(parts[1].shape, lambda i: (0, 0, 0))
    return pl.pallas_call(
        tail_kernel,
        grid=(1,),
        in_specs=[smem] * 2 + [mine] + [there] * 3 + [vmem] * 7,
        out_specs=vmem,
        out_shape=jax.ShapeDtypeStruct((feats, width, LANES), jnp.bfloat16),
        scratch_shapes=[
            pltpu.VMEM((feats, width, LANES), jnp.float32),
            pltpu.VMEM((feats, feats, LANES), jnp.float32),
            pltpu.VMEM((feats, width, LANES), jnp.float32),
        ],
        compiler_params=pltpu.CompilerParams(vmem_limit_bytes=20 << 20),
        cost_estimate=pl.CostEstimate(
            flops=1_000_000_000, bytes_accessed=8_000_000, transcendentals=0
        ),
        name="tail",
    )(host, order, *parts, *weights)


def move(x, axis, step):
    size = 2 if axis == "core" else 4
    return lax.ppermute(x, axis, [(i, (i + step) % size) for i in range(size)])


def other_core(x):
    return move(x, "core", 1)


def to_owners(blocks, axis):
    return [blocks[0]] + [move(blocks[d], axis, d) for d in range(1, 4)]


def add_up(blocks):
    return sum(b.astype(jnp.float32) for b in blocks).astype(jnp.bfloat16)


def to_hosts(total):
    return [total] + [move(total[d], "hst", d) for d in range(1, 4)]


def on_device(
    tables,
    indices,
    lengths,
    feature_order,
    proj_weight,
    fm_gain,
    up_weight,
    down_weight,
    compress_weight,
    out_gain,
):
    pos = jnp.stack([lax.axis_index(a) for a in ("hst", "z", "y", "core")]).astype(jnp.int32)

    flipped = jnp.swapaxes(tables, 1, 2)
    keys, lids, masks = prep(pos, jnp.transpose(indices, (1, 2, 0)), lengths.T)
    keys = keys.reshape((keys.shape[0], GATHER, ROWS_DEV // SUB) + keys.shape[2:])
    pairs = [(0, 1), (2, 3)]
    axes = ["z", "y"]

    mine = [flipped[2 * p : 2 * p + 2] for p in range(2)]
    sides = [[move(mine[p], axes[p], 3), move(mine[p], axes[p], 1)] for p in range(2)]
    own_far = other_core(flipped)

    def stage(tables, arrays, shard, base, n_outs, name):
        pieces = [(x, 0 if x.shape[0] == 4 else tables[0]) for x in arrays]
        pieces = [(x, start, shard + k, 0) for k, (x, start) in enumerate(pieces)]
        return pool(tables, masks, keys, lids, pieces, base, n_outs, name)

    sums = stage((0, 1, 2, 3), [flipped], 0, None, 0, "pool_own")
    sums, sides, mine, masks = lax.optimization_barrier((sums, sides, mine, masks))
    beyond = [move(mine[p], axes[p], 2) for p in range(2)]
    sides, own_far = lax.optimization_barrier((sides, own_far))
    early = [other_core(x) for x in (sides[0][0], sides[0][1], sides[1][0])]
    middle = []
    for p in range(2):
        middle.append(stage(pairs[p], [own_far] + sides[p], 1, (sums, 0), 0, "pool_sides"))
        masks, _ = lax.optimization_barrier((masks, middle[p]))
    sides, beyond, early, masks = lax.optimization_barrier((sides, beyond, early, masks))
    late = [other_core(x) for x in (beyond[0], sides[1][1], beyond[1])]
    first = stage(pairs[0], early[:2], 4, (middle[0], 0), 0, "pool_other")
    masks, _ = lax.optimization_barrier((masks, first))
    blocks = stage(pairs[0], [beyond[0], late[0]], 6, (first, 0), 4, "pool_beyond")
    masks, _ = lax.optimization_barrier((masks, blocks))
    arrived = to_owners(blocks, axes[1])
    (blocks,) = stage(
        pairs[1],
        [early[2], late[1], beyond[1], late[2]],
        4,
        (middle[1], 2),
        1,
        "pool_rest",
    )
    arrived, blocks = lax.optimization_barrier((arrived, blocks))
    parts = to_hosts(add_up(arrived))
    parts.append(lax.all_to_all(blocks, ("hst", axes[0]), 0, 0, tiled=True))
    result = tail(
        pos[:1],
        feature_order,
        parts,
        proj_weight.T,
        fm_gain.reshape(-1, LANES),
        up_weight,
        down_weight,
        compress_weight,
        out_gain,
    )
    return jnp.transpose(result, (2, 0, 1))


def solution(mesh):
    fine = Mesh(mesh.devices.reshape(4, 4, 4, 2), ("hst", "z", "y", "core"))
    row = ("z", "y", "core")
    in_specs = (
        P("hst", row, None),
        P(None, "hst", None),
        P(None, "hst"),
        P(),
        P(),
        P(),
        P(),
        P(),
        P(),
        P(),
    )
    out_specs = P(("hst",) + row, None, None)
    return jax.shard_map(
        on_device, mesh=fine, in_specs=in_specs, out_specs=out_specs, check_vma=False
    )
```
